32 devices in a mesh: groups: 2 (over x), dev: 16 (over z, y, core).
Axes of the slice: x: 2, y: 2, z: 4, core: 2. Of those that a mesh axis runs over, the one named last changes fastest.
Arguments:
- basis_rows: bfloat16 [2097152, 128], P(('groups', 'dev')), parts along dimension 0, may hold values from -4 to 4
- vector: bfloat16 [2097152], P(('groups', 'dev')), parts along dimension 0, may hold values from -6 to 6
- scores: float32 [2097152], P(('groups', 'dev')), parts along dimension 0, may hold values from -8 to 8
- assign: int32 [2097152], P(('groups', 'dev')), parts along dimension 0, may hold values from 0 to 63, as said below
- slot_of: int32 [128], P('groups'), parts along dimension 0, may hold values from 0 to 63, as said below
- partners: int32 [128, 64], P(('groups', 'dev')), parts along dimension 0, may hold values from 0 to 63
- link_blocks: bfloat16 [128, 64, 128, 128], P(('groups', 'dev')), parts along dimension 0, may hold values from -0.0625 to 0.0625
Outputs:
- product: float32 [2097152], P(('groups', 'dev')), parts along dimension 0
The draws below stay inside these ranges and needn't reach their ends.
There are 2 independent parts, one for each index of `groups`. The reference program is written for one: setup_inputs(seed, part) draws one part's arguments, and reference() takes and returns one part's arrays. A program takes and returns all parts, laid end to end along the dimension named above; each array names one. Nothing has to cross between parts.
Inputs may be any that keep to these rules, and one draw needn't show every extreme that they name: A sample in the block of 65536 samples number d has its slot slot_of[assign[s]] on a device (d + o) mod the number of devices with -2 <= o <= 2; cluster sizes are uneven. slot_of is a permutation of the slots.
All inputs are finite; a program needn't handle non-finite values.
Results may differ from the reference program's by a relative error of at most 0.0075.
Values may be sent and summed in bfloat16 or wider, within the bound.
No kernel may reach another device: no remote copies, remote signals or barrier semaphores. Data moves between devices by JAX's collectives and lax.ppermute only.
A program may use at most 128 MiB of HBM per device.

```python
import math
import jax
import jax.numpy as jnp
from jax import lax

R = 128
P_SIZE = 64
REACH = 2
CL_DEV = 4
S_DEV = 65536
C = 64
S = 1048576
N_DEV = 16


def cluster_order(key):
    return jax.random.permutation(key, C).astype(jnp.int32)


def draw_slot_of(key, part):
    order = cluster_order(key)
    return jnp.argsort(order, stable=True).astype(jnp.int32)


def draw_assign(key, part):
    order = cluster_order(key)
    key = jax.random.fold_in(key, 7)
    key_off, key_one, key_two = jax.random.split(key, 3)
    device_of = (jnp.arange(S, dtype=jnp.int32) // S_DEV).astype(jnp.int32)
    offset = jax.random.randint(key_off, (S,), -REACH, REACH + 1, dtype=jnp.int32)
    first_pick = jax.random.randint(key_one, (S,), 0, CL_DEV, dtype=jnp.int32)
    second_pick = jax.random.randint(key_two, (S,), 0, CL_DEV, dtype=jnp.int32)
    local = jnp.minimum(first_pick, second_pick)
    owner = (device_of + offset + N_DEV) % N_DEV
    slot = owner * CL_DEV + local
    return order[slot].astype(jnp.int32)


def place_ends(values, stream_key, least, top_value):
    place = [jax.random.randint(jax.random.fold_in(stream_key, axis), (), 0, length) for axis, length in enumerate(values.shape)]
    widest = values.shape.index(max(values.shape))
    next_to = place[:widest] + [(place[widest] + 1) % values.shape[widest]] + place[widest + 1:]
    return values.at[tuple(place)].set(least).at[tuple(next_to)].set(top_value)


def shard_levels(own_key, extent, pieces, smallest, high):
    def one(position, parts):
        heights = jax.random.uniform(jax.random.fold_in(jax.random.fold_in(own_key, 6), position), (parts,), jnp.float32, smallest / len(pieces), high / len(pieces))
        return jnp.repeat(jnp.exp(heights), extent[position] // parts).reshape((-1,) + (1,) * (len(extent) - position - 1))

    gain = one(*pieces[0])
    for cut in pieces[1:]:
        gain = gain * one(*cut)
    return gain


def noise(own_key, dims, deviation, most, cuts=(), kind=jnp.bfloat16):
    factor_of = shard_levels(own_key, dims, cuts, -0.22, 0.18) if cuts else 1.0
    entries = jax.random.normal(own_key, dims, jnp.float32) * deviation * factor_of
    return jnp.minimum(jnp.maximum(entries, -most), most).astype(kind)


def setup_inputs(seed: int = 0, part: int = 0) -> dict:
    splits = jax.random.split(jax.random.key(seed), 8)
    part_splits = jax.random.split(jax.random.fold_in(splits[7], part), 8)
    return {
        "basis_rows": noise(part_splits[0], (S, R), 0.3, 4.0, ((0, 16),)),
        "vector": noise(part_splits[1], (S,), 1.0, 6.0, ((0, 16),)),
        "scores": noise(part_splits[2], (S,), 2.0, 8.0, ((0, 16),), jnp.float32),
        "assign": draw_assign(jax.random.fold_in(jax.random.fold_in(splits[7], part), 71), part),
        "slot_of": draw_slot_of(jax.random.fold_in(jax.random.fold_in(splits[7], part), 71), part),
        "partners": place_ends(jax.random.randint(part_splits[5], (C, P_SIZE), 0, C), jax.random.fold_in(part_splits[5], 1), 0, C - 1).astype(jnp.int32),
        "link_blocks": noise(part_splits[6], (C, P_SIZE, R, R), (P_SIZE * R) ** -0.5, 0.0625, ((0, 16),)),
    }


ridge = 0.5

def kernel_apply(basis_rows, weights, slot, slot_of, partners, link_blocks):
    coef = jax.ops.segment_sum(basis_rows.astype(jnp.float32) * weights.astype(jnp.float32)[:, None], slot, num_segments=C)
    scaled = (coef / math.sqrt(S_DEV // CL_DEV)).astype(jnp.bfloat16)
    gathered = scaled[slot_of[partners]]
    mixed = jnp.einsum('kpij,kpj->ki', link_blocks.astype(jnp.float32), gathered.astype(jnp.float32)).astype(jnp.bfloat16)
    rows = mixed[slot]
    return lax.optimization_barrier(jnp.sum(basis_rows.astype(jnp.float32) * rows.astype(jnp.float32), axis=-1))

def reference(basis_rows, vector, scores, assign, slot_of, partners, link_blocks):
    slot = slot_of[assign]
    first = kernel_apply(basis_rows, vector, slot, slot_of, partners, link_blocks)
    sig = jax.nn.sigmoid(scores)
    weighted = (sig * (1.0 - sig) * first).astype(jnp.bfloat16)
    second = kernel_apply(basis_rows, weighted, slot, slot_of, partners, link_blocks)
    return second + ridge * first
```

```python
import functools
import math

import jax
import jax.numpy as jnp
from jax import lax
from jax.experimental import pallas as pl
from jax.experimental.pallas import tpu as pltpu
from jax.sharding import PartitionSpec as P

REACH = 2
NEAR = 2 * REACH + 1
CL_DEV = 4
S_DEV = 65536
LANES = 128
ROWS = 32

TILE = 4096
PIECE = 1024
LINKS = 32

ridge = 0.5


def near_clusters(devices, per_dev, slot_of_ref, cl_ref):
    clusters = devices * per_dev
    me = lax.axis_index("dev")
    near = lax.broadcasted_iota(jnp.int32, (ROWS, clusters), 0)
    slots = (me + devices - REACH) * per_dev + near
    slots = lax.rem(slots, clusters)
    number = lax.broadcasted_iota(jnp.int32, (ROWS, clusters), 1)
    hit = (slot_of_ref[...] == slots) & (near < NEAR * per_dev)
    found = jnp.sum(jnp.where(hit, number + 1, 0), axis=1, keepdims=True) - 1
    cl_ref[...] = jnp.broadcast_to(found, cl_ref.shape)


def spread_near(devices, per_dev, sums, out_ref):
    me = lax.axis_index("dev")
    out_ref[...] = jnp.zeros_like(out_ref)
    for g in range(NEAR):
        owner = lax.rem(me + devices + g - REACH, devices)
        out_ref[owner] = sums[g * per_dev : (g + 1) * per_dev]


def near_rows(devices, per_dev, mixed_ref, rows_ref):
    me = lax.axis_index("dev")
    rows_ref[...] = jnp.zeros_like(rows_ref)
    for g in range(NEAR):
        owner = lax.rem(me + devices + g - REACH, devices)
        rows_ref[g * per_dev : (g + 1) * per_dev, :] = mixed_ref[owner].astype(jnp.float32)


def coef_kernel(devices, per_dev, slot_of_ref, assign_ref, x_ref, basis_ref, out_ref, cl_ref, sum_ref, xf_ref):
    step = pl.program_id(0)

    @pl.when(step == 0)
    def _():
        near_clusters(devices, per_dev, slot_of_ref, cl_ref)
        sum_ref[...] = jnp.zeros_like(sum_ref)

    xf_ref[...] = x_ref[...].astype(jnp.float32)
    cl = cl_ref[...]
    total = sum_ref[...]
    for p in range(TILE // PIECE):
        parts = []
        for r in range(p * PIECE // LANES, (p + 1) * PIECE // LANES):
            hit = assign_ref[r : r + 1, :] == cl
            parts.append(jnp.where(hit, xf_ref[r : r + 1, :], 0.0).astype(jnp.bfloat16))
        left = jnp.concatenate(parts, axis=1)
        total += jnp.dot(left, basis_ref[p * PIECE : (p + 1) * PIECE, :], preferred_element_type=jnp.float32)
    sum_ref[...] = total

    @pl.when(step == pl.num_programs(0) - 1)
    def _():
        spread_near(devices, per_dev, sum_ref[...], out_ref)


def link_kernel(norm, slot_of_ref, partners_ref, coef_ref, links_ref, out_ref, scaled_ref, acc_ref, mixed_ref):
    j = pl.program_id(0)
    part = pl.program_id(1)

    @pl.when((j == 0) & (part == 0))
    def _():
        scaled_ref[...] = (coef_ref[...] * norm).astype(jnp.bfloat16).astype(jnp.float32)
        mixed_ref[...] = jnp.zeros_like(mixed_ref)

    @pl.when(part == 0)
    def _():
        acc_ref[...] = jnp.zeros_like(acc_ref)

    def body(k, acc):
        s = slot_of_ref[partners_ref[j, part * LINKS + k]]
        return acc + links_ref[0, k].astype(jnp.float32) * scaled_ref[pl.ds(s, 1), :]

    acc_ref[...] = lax.fori_loop(0, LINKS, body, acc_ref[...], unroll=8)

    @pl.when(part == pl.num_programs(1) - 1)
    def _():
        mixed_ref[pl.ds(j, 1), :] = jnp.sum(acc_ref[...].T, axis=0, keepdims=True)

    @pl.when((part == pl.num_programs(1) - 1) & (j == pl.num_programs(0) - 1))
    def _():
        out_ref[...] = mixed_ref[: out_ref.shape[0], :].astype(jnp.bfloat16)


def rows_times(rows, piece):
    return lax.dot_general(rows, piece, (((1,), (1,)), ((), ())), preferred_element_type=jnp.float32)


def both_kernel(
    devices, per_dev, slot_of_ref, mixed_ref, assign_ref, scores_ref, basis_ref,
    first_ref, out_ref, cl_ref, rows_ref, sum_ref, slope_ref,
):
    step = pl.program_id(0)

    @pl.when(step == 0)
    def _():
        near_clusters(devices, per_dev, slot_of_ref, cl_ref)
        near_rows(devices, per_dev, mixed_ref, rows_ref)
        sum_ref[...] = jnp.zeros_like(sum_ref)

    sig = jax.nn.sigmoid(scores_ref[...])
    slope_ref[...] = sig * (1.0 - sig)
    cl = cl_ref[...]
    rows = rows_ref[...].astype(jnp.bfloat16)
    total = sum_ref[...]
    for p in range(TILE // PIECE):
        piece = basis_ref[p * PIECE : (p + 1) * PIECE, :]
        products = rows_times(rows, piece)
        parts = []
        for i in range(PIECE // LANES):
            r = p * PIECE // LANES + i
            hit = assign_ref[r : r + 1, :] == cl
            first = jnp.sum(jnp.where(hit, products[:, i * LANES : (i + 1) * LANES], 0.0), axis=0, keepdims=True)
            first_ref[r : r + 1, :] = first
            weighted = slope_ref[r : r + 1, :] * first
            parts.append(jnp.where(hit, weighted, 0.0).astype(jnp.bfloat16))
        left = jnp.concatenate(parts, axis=1)
        total += jnp.dot(left, piece, preferred_element_type=jnp.float32)
    sum_ref[...] = total

    @pl.when(step == pl.num_programs(0) - 1)
    def _():
        spread_near(devices, per_dev, sum_ref[...], out_ref)


def last_kernel(
    devices, per_dev, slot_of_ref, mixed_ref, assign_ref, first_ref, basis_ref, out_ref, cl_ref, rows_ref
):
    step = pl.program_id(0)

    @pl.when(step == 0)
    def _():
        near_clusters(devices, per_dev, slot_of_ref, cl_ref)
        near_rows(devices, per_dev, mixed_ref, rows_ref)

    cl = cl_ref[...]
    rows = rows_ref[...].astype(jnp.bfloat16)
    for p in range(TILE // PIECE):
        products = rows_times(rows, basis_ref[p * PIECE : (p + 1) * PIECE, :])
        for i in range(PIECE // LANES):
            r = p * PIECE // LANES + i
            hit = assign_ref[r : r + 1, :] == cl
            second = jnp.sum(jnp.where(hit, products[:, i * LANES : (i + 1) * LANES], 0.0), axis=0, keepdims=True)
            out_ref[r : r + 1, :] = second + ridge * first_ref[r : r + 1, :]


def shards(basis_rows, vector, scores, assign, slot_of, partners, link_blocks):
    devices = lax.axis_size("dev")
    clusters = slot_of.shape[0]
    per_dev, n_links, rank, _ = link_blocks.shape
    samples = assign.shape[0]
    norm = 1.0 / math.sqrt(S_DEV // CL_DEV)
    steps = samples // TILE
    high = TILE // LANES
    f32 = jnp.float32

    vector = vector.reshape(samples // LANES, LANES)
    scores = scores.reshape(samples // LANES, LANES)
    assign = assign.reshape(samples // LANES, LANES)
    slot_row = slot_of.reshape(1, clusters)

    whole = lambda *shape: pl.BlockSpec(shape, lambda i: (0,) * len(shape))
    tile = pl.BlockSpec((high, LANES), lambda i: (i, 0))
    basis_tile = pl.BlockSpec((TILE, rank), lambda i: (i, 0))
    coef_shape = jax.ShapeDtypeStruct((devices, per_dev, rank), f32)
    coef_spec = whole(devices, per_dev, rank)
    row_shape = jax.ShapeDtypeStruct((samples // LANES, LANES), f32)
    params = pltpu.CompilerParams(vmem_limit_bytes=32 * 1024 * 1024)

    coef1 = pl.pallas_call(
        functools.partial(coef_kernel, devices, per_dev),
        grid=(steps,),
        in_specs=[whole(1, clusters), tile, tile, basis_tile],
        out_specs=coef_spec,
        out_shape=coef_shape,
        scratch_shapes=[
            pltpu.VMEM((ROWS, LANES), jnp.int32),
            pltpu.VMEM((ROWS, rank), f32),
            pltpu.VMEM((high, LANES), f32),
        ],
        compiler_params=params,
        name="coef_pass",
    )(slot_row, assign, vector, basis_rows)

    def mix(coef):
        coef = lax.psum(coef, "dev").reshape(clusters, rank)
        mixed = pl.pallas_call(
            functools.partial(link_kernel, norm),
            grid_spec=pltpu.PrefetchScalarGridSpec(
                num_scalar_prefetch=2,
                grid=(per_dev, n_links // LINKS),
                in_specs=[
                    pl.BlockSpec((clusters, rank), lambda j, p, *_: (0, 0)),
                    pl.BlockSpec((1, LINKS, rank, rank), lambda j, p, *_: (j, p, 0, 0)),
                ],
                out_specs=pl.BlockSpec((per_dev, rank), lambda j, p, *_: (0, 0)),
                scratch_shapes=[
                    pltpu.VMEM((clusters, rank), f32),
                    pltpu.VMEM((rank, rank), f32),
                    pltpu.VMEM((8, rank), f32),
                ],
            ),
            out_shape=jax.ShapeDtypeStruct((per_dev, rank), jnp.bfloat16),
            compiler_params=params,
            name="link_product",
        )(slot_of, partners, coef, link_blocks)
        copies = jnp.broadcast_to(mixed[None], (devices, per_dev, rank))
        return lax.all_to_all(copies, "dev", 0, 0, tiled=True)

    first, coef2 = pl.pallas_call(
        functools.partial(both_kernel, devices, per_dev),
        grid=(steps,),
        in_specs=[whole(1, clusters), coef_spec, tile, tile, basis_tile],
        out_specs=[tile, coef_spec],
        out_shape=[row_shape, coef_shape],
        scratch_shapes=[
            pltpu.VMEM((ROWS, LANES), jnp.int32),
            pltpu.VMEM((ROWS, rank), f32),
            pltpu.VMEM((ROWS, rank), f32),
            pltpu.VMEM((high, LANES), f32),
        ],
        compiler_params=params,
        name="first_and_coef_pass",
    )(slot_row, mix(coef1), assign, scores, basis_rows)

    out = pl.pallas_call(
        functools.partial(last_kernel, devices, per_dev),
        grid=(steps,),
        in_specs=[whole(1, clusters), coef_spec, tile, tile, basis_tile],
        out_specs=tile,
        out_shape=row_shape,
        scratch_shapes=[
            pltpu.VMEM((ROWS, LANES), jnp.int32),
            pltpu.VMEM((ROWS, rank), f32),
        ],
        compiler_params=params,
        name="last_pass",
    )(slot_row, mix(coef2), assign, first, basis_rows)
    return out.reshape(samples)


def solution(mesh):
    in_specs = (
        P(("groups", "dev"), None),
        P(("groups", "dev")),
        P(("groups", "dev")),
        P(("groups", "dev")),
        P("groups"),
        P(("groups", "dev"), None),
        P(("groups", "dev"), None, None, None),
    )
    out_specs = P(("groups", "dev"))
    return jax.shard_map(shards, mesh=mesh, in_specs=in_specs, out_specs=out_specs, check_vma=False)
```

```python
import functools
import math

import jax
import jax.numpy as jnp
from jax import lax
from jax.experimental import pallas as pl
from jax.experimental.pallas import tpu as pltpu
from jax.sharding import PartitionSpec as P

REACH = 2
NEAR = 2 * REACH + 1
CL_DEV = 4
S_DEV = 65536
LANES = 128
ROWS = 32

TILE = 4096
PIECE = 1024
SLOTS = 4

ridge = 0.5


def near_clusters(devices, per_dev, slot_of_ref, cl_ref):
    clusters = devices * per_dev
    me = lax.axis_index("dev")
    near = lax.broadcasted_iota(jnp.int32, (ROWS, clusters), 0)
    slots = (me + devices - REACH) * per_dev + near
    slots = lax.rem(slots, clusters)
    number = lax.broadcasted_iota(jnp.int32, (ROWS, clusters), 1)
    hit = (slot_of_ref[...] == slots) & (near < NEAR * per_dev)
    found = jnp.sum(jnp.where(hit, number + 1, 0), axis=1, keepdims=True) - 1
    cl_ref[...] = jnp.broadcast_to(found, cl_ref.shape)


def near_rows(devices, per_dev, mixed_ref, rows_ref):
    me = lax.axis_index("dev")
    rows_ref[...] = jnp.zeros_like(rows_ref)
    for g in range(NEAR):
        owner = lax.rem(me + devices + g - REACH, devices)
        rows_ref[g * per_dev : (g + 1) * per_dev, :] = mixed_ref[owner].astype(jnp.float32)


def tile_copy(basis_hbm, slots_ref, sem, t):
    slot = lax.rem(t, SLOTS)
    rows = pl.ds(pl.multiple_of(t * TILE, TILE), TILE)
    return pltpu.make_async_copy(basis_hbm.at[rows, :], slots_ref.at[slot], sem.at[slot])


def coef_kernel(
    devices, per_dev, slot_of_ref, assign_hbm, vector_hbm, basis_hbm, links_hbm,
    out_ref, turned_ref, assign_ref, links_ref,
    cl_ref, sum_ref, vector_ref, x_ref, slots_ref, small_sem, basis_sem, links_sem,
):
    tiles = basis_hbm.shape[0] // TILE
    high = TILE // LANES

    def basis_copy(t):
        return tile_copy(basis_hbm, slots_ref, basis_sem, t)

    assign_copy = pltpu.make_async_copy(assign_hbm, assign_ref, small_sem.at[0])
    vector_copy = pltpu.make_async_copy(vector_hbm, vector_ref, small_sem.at[1])
    links_copy = pltpu.make_async_copy(links_hbm, links_ref, links_sem)
    assign_copy.start()
    vector_copy.start()
    for t in range(SLOTS):
        basis_copy(t).start()
    near_clusters(devices, per_dev, slot_of_ref, cl_ref)
    sum_ref[...] = jnp.zeros_like(sum_ref)
    assign_copy.wait()
    vector_copy.wait()
    x_ref[...] = vector_ref[...].astype(jnp.float32)
    cl = cl_ref[...]

    @pl.loop(0, tiles)
    def _(t):
        basis_copy(t).wait()
        total = sum_ref[...]
        for p in range(TILE // PIECE):
            parts = []
            for i in range(PIECE // LANES):
                r = pl.ds(t * high + p * (PIECE // LANES) + i, 1)
                hit = assign_ref[r, :] == cl
                parts.append(jnp.where(hit, x_ref[r, :], 0.0).astype(jnp.bfloat16))
            left = jnp.concatenate(parts, axis=1)
            at = pl.ds(pl.multiple_of(t * TILE + p * PIECE, PIECE), PIECE)
            piece = slots_ref[lax.rem(t, SLOTS), p * PIECE : (p + 1) * PIECE, :]
            turned_ref[:, at] = piece.T
            total += jnp.dot(left, piece, preferred_element_type=jnp.float32)
        sum_ref[...] = total

        @pl.when(t + SLOTS < tiles)
        def _():
            basis_copy(t + SLOTS).start()

        @pl.when(t + SLOTS == tiles)
        def _():
            links_copy.start()

    out_ref[...] = sum_ref[: NEAR * per_dev, :]
    links_copy.wait()


def link_kernel(norm, devices, per_dev, slot_of_ref, partners_ref, parts_ref, links_ref, out_ref, scaled_ref, mixed_ref):
    for owner in range(devices):
        coef = parts_ref[(owner + REACH) % devices, :per_dev, :]
        for g in range(1, NEAR):
            coef += parts_ref[(owner + REACH - g) % devices, g * per_dev : (g + 1) * per_dev, :]
        scaled_ref[owner * per_dev : (owner + 1) * per_dev, :] = (coef * norm).astype(jnp.bfloat16).astype(jnp.float32)
    mixed_ref[...] = jnp.zeros_like(mixed_ref)
    n_links = links_ref.shape[1]
    for j in range(per_dev):
        def body(k, acc):
            s = slot_of_ref[partners_ref[j, k]]
            return acc + links_ref[j, k].astype(jnp.float32) * scaled_ref[pl.ds(s, 1), :]

        acc = lax.fori_loop(0, n_links, body, jnp.zeros(links_ref.shape[2:], jnp.float32), unroll=8)
        mixed_ref[j : j + 1, :] = jnp.sum(acc.T, axis=0, keepdims=True)
    out_ref[...] = mixed_ref[:per_dev, :].astype(jnp.bfloat16)


def both_kernel(
    devices, per_dev, slot_of_ref, mixed_ref, assign_ref, scores_ref, turned_ref, basis_hbm,
    first_ref, out_ref, cl_ref, rows_ref, sum_ref, slope_ref, slots_ref, basis_sem,
):
    tiles = basis_hbm.shape[0] // TILE

    def basis_copy(t):
        return tile_copy(basis_hbm, slots_ref, basis_sem, t)

    for t in range(SLOTS):
        basis_copy(t).start()
    near_clusters(devices, per_dev, slot_of_ref, cl_ref)
    near_rows(devices, per_dev, mixed_ref, rows_ref)
    sum_ref[...] = jnp.zeros_like(sum_ref)
    sig = jax.nn.sigmoid(scores_ref[...])
    slope_ref[...] = sig * (1.0 - sig)
    cl = cl_ref[...]
    rows = rows_ref[...].astype(jnp.bfloat16)

    @pl.loop(0, tiles)
    def _(t):
        basis_copy(t).wait()
        total = sum_ref[...]
        for p in range(TILE // PIECE):
            at = pl.ds(pl.multiple_of(t * TILE + p * PIECE, PIECE), PIECE)
            products = jnp.dot(rows, turned_ref[:, at], preferred_element_type=jnp.float32)
            parts = []
            for i in range(PIECE // LANES):
                r = pl.ds((t * TILE + p * PIECE) // LANES + i, 1)
                hit = assign_ref[r, :] == cl
                first = jnp.sum(jnp.where(hit, products[:, i * LANES : (i + 1) * LANES], 0.0), axis=0, keepdims=True)
                first_ref[r, :] = first
                weighted = slope_ref[r, :] * first
                parts.append(jnp.where(hit, weighted, 0.0).astype(jnp.bfloat16))
            left = jnp.concatenate(parts, axis=1)
            piece = slots_ref[lax.rem(t, SLOTS), p * PIECE : (p + 1) * PIECE, :]
            total += jnp.dot(left, piece, preferred_element_type=jnp.float32)
        sum_ref[...] = total

        @pl.when(t + SLOTS < tiles)
        def _():
            basis_copy(t + SLOTS).start()

    out_ref[...] = sum_ref[: NEAR * per_dev, :]


def last_kernel(devices, per_dev, slot_of_ref, mixed_ref, assign_ref, first_ref, turned_ref, out_ref, cl_ref, rows_ref):
    near_clusters(devices, per_dev, slot_of_ref, cl_ref)
    near_rows(devices, per_dev, mixed_ref, rows_ref)
    cl = cl_ref[...]
    rows = rows_ref[...].astype(jnp.bfloat16)

    @pl.loop(0, turned_ref.shape[1] // TILE)
    def _(t):
        for p in range(TILE // PIECE):
            at = pl.ds(pl.multiple_of(t * TILE + p * PIECE, PIECE), PIECE)
            products = jnp.dot(rows, turned_ref[:, at], preferred_element_type=jnp.float32)
            for i in range(PIECE // LANES):
                r = pl.ds((t * TILE + p * PIECE) // LANES + i, 1)
                hit = assign_ref[r, :] == cl
                second = jnp.sum(jnp.where(hit, products[:, i * LANES : (i + 1) * LANES], 0.0), axis=0, keepdims=True)
                out_ref[r, :] = second + ridge * first_ref[r, :]


def shards(basis_rows, vector, scores, assign, slot_of, partners, link_blocks):
    devices = lax.axis_size("dev")
    clusters = slot_of.shape[0]
    per_dev, n_links, rank, _ = link_blocks.shape
    samples = assign.shape[0]
    norm = 1.0 / math.sqrt(S_DEV // CL_DEV)
    high = samples // LANES
    near = NEAR * per_dev
    f32, bf16 = jnp.float32, jnp.bfloat16

    vector = vector.reshape(high, LANES)
    scores = scores.reshape(high, LANES)
    assign = assign.reshape(high, LANES)
    slot_row = slot_of.reshape(1, clusters)

    far = lambda x: pltpu.with_memory_space_constraint(x, pltpu.HBM)
    close = lambda x: pltpu.with_memory_space_constraint(x, pltpu.VMEM)
    vmem = pl.BlockSpec(memory_space=pltpu.VMEM)
    smem = pl.BlockSpec(memory_space=pltpu.SMEM)
    hbm = pl.BlockSpec(memory_space=pltpu.HBM)
    coef_shape = jax.ShapeDtypeStruct((near, rank), f32)
    params = pltpu.CompilerParams(vmem_limit_bytes=8 * 1024 * 1024)

    coef1, turned_v, assign_v, links_v = pl.pallas_call(
        functools.partial(coef_kernel, devices, per_dev),
        in_specs=[vmem, hbm, hbm, hbm, hbm],
        out_specs=[vmem] * 4,
        out_shape=[
            coef_shape,
            pltpu.VMEM((rank, samples), bf16),
            pltpu.VMEM((high, LANES), jnp.int32),
            pltpu.VMEM(link_blocks.shape, bf16),
        ],
        scratch_shapes=[
            pltpu.VMEM((ROWS, LANES), jnp.int32),
            pltpu.VMEM((ROWS, rank), f32),
            pltpu.VMEM((high, LANES), bf16),
            pltpu.VMEM((high, LANES), f32),
            pltpu.VMEM((SLOTS, TILE, rank), bf16),
            pltpu.SemaphoreType.DMA((2,)),
            pltpu.SemaphoreType.DMA((SLOTS,)),
            pltpu.SemaphoreType.DMA,
        ],
        compiler_params=params,
        name="coef_pass",
    )(slot_row, far(assign), far(vector), far(basis_rows), far(link_blocks))

    def to_all(block):
        copies = jnp.broadcast_to(block[None], (devices,) + block.shape)
        return lax.all_to_all(copies, "dev", 0, 0, tiled=True)

    def mix(coef):
        mixed = pl.pallas_call(
            functools.partial(link_kernel, norm, devices, per_dev),
            in_specs=[smem, smem, vmem, vmem],
            out_specs=vmem,
            scratch_shapes=[
                pltpu.VMEM((clusters, rank), f32),
                pltpu.VMEM((8, rank), f32),
            ],
            out_shape=jax.ShapeDtypeStruct((per_dev, rank), bf16),
            compiler_params=params,
            name="link_product",
        )(slot_of, partners, to_all(coef), close(links_v))
        return to_all(mixed)

    first, coef2 = pl.pallas_call(
        functools.partial(both_kernel, devices, per_dev),
        in_specs=[vmem] * 5 + [hbm],
        out_specs=[vmem, vmem],
        out_shape=[pltpu.VMEM((high, LANES), f32), coef_shape],
        scratch_shapes=[
            pltpu.VMEM((ROWS, LANES), jnp.int32),
            pltpu.VMEM((ROWS, rank), f32),
            pltpu.VMEM((ROWS, rank), f32),
            pltpu.VMEM((high, LANES), f32),
            pltpu.VMEM((SLOTS, TILE, rank), bf16),
            pltpu.SemaphoreType.DMA((SLOTS,)),
        ],
        compiler_params=params,
        name="first_and_coef_pass",
    )(slot_row, mix(coef1), close(assign_v), scores, close(turned_v), far(basis_rows))

    out = pl.pallas_call(
        functools.partial(last_kernel, devices, per_dev),
        in_specs=[vmem] * 5,
        out_specs=vmem,
        out_shape=jax.ShapeDtypeStruct((high, LANES), f32),
        scratch_shapes=[
            pltpu.VMEM((ROWS, LANES), jnp.int32),
            pltpu.VMEM((ROWS, rank), f32),
        ],
        compiler_params=params,
        name="last_pass",
    )(slot_row, mix(coef2), close(assign_v), close(first), close(turned_v))
    return out.reshape(samples)


def solution(mesh):
    in_specs = (
        P(("groups", "dev"), None),
        P(("groups", "dev")),
        P(("groups", "dev")),
        P(("groups", "dev")),
        P("groups"),
        P(("groups", "dev"), None),
        P(("groups", "dev"), None, None, None),
    )
    out_specs = P(("groups", "dev"))
    return jax.shard_map(shards, mesh=mesh, in_specs=in_specs, out_specs=out_specs, check_vma=False)
```

```python
import functools
import math

import jax
import jax.numpy as jnp
from jax import lax
from jax.experimental import pallas as pl
from jax.experimental.pallas import tpu as pltpu
from jax.sharding import PartitionSpec as P

REACH = 2
NEAR = 2 * REACH + 1
CL_DEV = 4
S_DEV = 65536
LANES = 128
ROWS = 24

COPY = 4096
TILE = 2048
GROUP = 8

ridge = 0.5


def near_clusters(devices, per_dev, slot_of_ref, cl_ref):
    clusters = devices * per_dev
    me = lax.axis_index("dev")
    near = lax.broadcasted_iota(jnp.int32, (ROWS, clusters), 0)
    slots = (me + devices - REACH) * per_dev + near
    slots = lax.rem(slots, clusters)
    number = lax.broadcasted_iota(jnp.int32, (ROWS, clusters), 1)
    hit = (slot_of_ref[...] == slots) & (near < NEAR * per_dev)
    found = jnp.sum(jnp.where(hit, number + 1, 0), axis=1, keepdims=True) - 1
    cl_ref[...] = jnp.broadcast_to(found, cl_ref.shape)


def near_rows(devices, per_dev, mixed_ref, rows_ref):
    me = lax.axis_index("dev")
    rows_ref[...] = jnp.zeros_like(rows_ref)
    for g in range(NEAR):
        owner = lax.rem(me + devices + g - REACH, devices)
        rows_ref[g * per_dev : (g + 1) * per_dev, :] = mixed_ref[owner].astype(jnp.float32)


def put_sums(per_dev, sum_ref, out_ref):
    for g in range(NEAR):
        out_ref[:, g * LANES : (g + 1) * LANES] = sum_ref[g * per_dev : (g + 1) * per_dev, :]


def times_turned(rows, block):
    return lax.dot_general(rows, block, (((1,), (1,)), ((), ())), preferred_element_type=jnp.float32)


def tile_at(t):
    return pl.ds(pl.multiple_of(t * TILE, TILE), TILE)


def row_at(t, i):
    return pl.ds(t * (TILE // LANES) + i, 1)


def coef_kernel(
    devices, per_dev, slot_of_ref, assign_hbm, vector_hbm, basis_hbm,
    out_ref, basis_ref, assign_ref,
    cl_ref, sum_ref, vector_ref, x_ref, small_sem, basis_sem,
):
    copies = basis_ref.shape[0] // COPY

    def basis_copy(t):
        rows = pl.ds(pl.multiple_of(t * COPY, COPY), COPY)
        return pltpu.make_async_copy(basis_hbm.at[rows, :], basis_ref.at[rows, :], basis_sem.at[t])

    assign_copy = pltpu.make_async_copy(assign_hbm, assign_ref, small_sem.at[0])
    vector_copy = pltpu.make_async_copy(vector_hbm, vector_ref, small_sem.at[1])
    assign_copy.start()
    vector_copy.start()
    for t in range(copies):
        basis_copy(t).start()
    near_clusters(devices, per_dev, slot_of_ref, cl_ref)
    sum_ref[...] = jnp.zeros_like(sum_ref)
    assign_copy.wait()
    vector_copy.wait()
    x_ref[...] = vector_ref[...].astype(jnp.float32)
    cl = cl_ref[...]

    @pl.loop(0, copies)
    def _(c):
        basis_copy(c).wait()
        total = sum_ref[...]
        for p in range(COPY // TILE):
            t = c * (COPY // TILE) + p
            parts = []
            for i in range(TILE // LANES):
                hit = assign_ref[row_at(t, i), :] == cl
                parts.append(jnp.where(hit, x_ref[row_at(t, i), :], 0.0).astype(jnp.bfloat16))
            left = jnp.concatenate(parts, axis=1)
            total += jnp.dot(left, basis_ref[tile_at(t), :], preferred_element_type=jnp.float32)
        sum_ref[...] = total

    put_sums(per_dev, sum_ref, out_ref)


def link_kernel(norm, devices, per_dev, slot_of_ref, partners_ref, parts_ref, links_ref, out_ref, scaled_ref, picked_ref, mixed_ref):
    for owner in range(devices):
        coef = parts_ref[(owner + REACH) % devices, :, :LANES]
        for g in range(1, NEAR):
            coef += parts_ref[(owner + REACH - g) % devices, :, g * LANES : (g + 1) * LANES]
        scaled_ref[owner * per_dev : (owner + 1) * per_dev, :] = (coef * norm).astype(jnp.bfloat16).astype(jnp.float32)
    n_links, rank = links_ref.shape[1:3]
    for j in range(per_dev):
        @pl.loop(0, n_links, unroll=8)
        def _(k):
            s = slot_of_ref[partners_ref[j, k]]
            picked_ref[pl.ds(j * n_links + k, 1), :] = scaled_ref[pl.ds(s, 1), :]

    mixed_ref[...] = jnp.zeros_like(mixed_ref)
    row = lax.broadcasted_iota(jnp.int32, (GROUP, rank), 0)
    for j in range(per_dev):
        acc = jnp.zeros((GROUP, rank), jnp.float32)
        for k in range(0, n_links, GROUP):
            at = j * n_links + k
            picked = picked_ref[at : at + GROUP, :].astype(jnp.bfloat16)
            block = links_ref[j, k : k + GROUP].reshape(GROUP * rank, rank)
            products = times_turned(picked, block)
            for i in range(GROUP):
                acc += jnp.where(row == i, products[:, i * rank : (i + 1) * rank], 0.0)
        mixed_ref[j : j + 1, :] = jnp.sum(acc, axis=0, keepdims=True)
    out_ref[...] = mixed_ref[:per_dev, :].astype(jnp.bfloat16)


def own_product(hit, products):
    return jnp.sum(jnp.where(hit, products, 0.0), axis=0, keepdims=True)


def both_kernel(
    devices, per_dev, slot_of_ref, mixed_ref, assign_ref, scores_ref, basis_ref,
    first_ref, out_ref, cl_ref, rows_ref, sum_ref, slope_ref, even_ref, odd_ref, even_left, odd_left,
):
    tiles = basis_ref.shape[0] // TILE
    near_clusters(devices, per_dev, slot_of_ref, cl_ref)
    near_rows(devices, per_dev, mixed_ref, rows_ref)
    sum_ref[...] = jnp.zeros_like(sum_ref)
    sig = jax.nn.sigmoid(scores_ref[...])
    slope_ref[...] = sig * (1.0 - sig)
    cl = cl_ref[...]
    rows = rows_ref[...].astype(jnp.bfloat16)
    products_of = (even_ref, odd_ref)
    left_of = (even_left, odd_left)

    def multiply(t, side):
        products_of[side][...] = times_turned(rows, basis_ref[tile_at(t), :])

    def select(t, side):
        for i in range(TILE // LANES):
            at = slice(i * LANES, (i + 1) * LANES)
            hit = assign_ref[row_at(t, i), :] == cl
            first = own_product(hit, products_of[side][:, at])
            first_ref[row_at(t, i), :] = first
            weighted = slope_ref[row_at(t, i), :] * first
            left_of[side][:, at] = jnp.where(hit, weighted, 0.0).astype(jnp.bfloat16)

    def add_up(t, side):
        sum_ref[...] += jnp.dot(left_of[side][...], basis_ref[tile_at(t), :], preferred_element_type=jnp.float32)

    multiply(0, 0)
    select(0, 0)
    multiply(1, 1)

    @pl.loop(0, tiles // 2 - 1)
    def _(i):
        t = 2 * i + 2
        add_up(t - 2, 0)
        multiply(t, 0)
        select(t - 1, 1)
        add_up(t - 1, 1)
        multiply(t + 1, 1)
        select(t, 0)

    add_up(tiles - 2, 0)
    select(tiles - 1, 1)
    add_up(tiles - 1, 1)
    put_sums(per_dev, sum_ref, out_ref)


def last_kernel(
    devices, per_dev, slot_of_ref, mixed_ref, assign_ref, first_ref, basis_ref, out_ref, cl_ref, rows_ref, even_ref, odd_ref
):
    tiles = basis_ref.shape[0] // TILE
    near_clusters(devices, per_dev, slot_of_ref, cl_ref)
    near_rows(devices, per_dev, mixed_ref, rows_ref)
    cl = cl_ref[...]
    rows = rows_ref[...].astype(jnp.bfloat16)
    products_of = (even_ref, odd_ref)

    def multiply(t, side):
        products_of[side][...] = times_turned(rows, basis_ref[tile_at(t), :])

    def select(t, side):
        for i in range(TILE // LANES):
            hit = assign_ref[row_at(t, i), :] == cl
            second = own_product(hit, products_of[side][:, i * LANES : (i + 1) * LANES])
            out_ref[row_at(t, i), :] = second + ridge * first_ref[row_at(t, i), :]

    multiply(0, 0)

    @pl.loop(0, tiles // 2 - 1)
    def _(i):
        t = 2 * i + 1
        multiply(t, 1)
        select(t - 1, 0)
        multiply(t + 1, 0)
        select(t, 1)

    multiply(tiles - 1, 1)
    select(tiles - 2, 0)
    select(tiles - 1, 1)


def shards(basis_rows, vector, scores, assign, slot_of, partners, link_blocks):
    devices = lax.axis_size("dev")
    clusters = slot_of.shape[0]
    per_dev, n_links, rank, _ = link_blocks.shape
    samples = assign.shape[0]
    norm = 1.0 / math.sqrt(S_DEV // CL_DEV)
    high = samples // LANES
    f32, bf16 = jnp.float32, jnp.bfloat16

    vector = vector.reshape(high, LANES)
    scores = scores.reshape(high, LANES)
    assign = assign.reshape(high, LANES)
    slot_row = slot_of.reshape(1, clusters)

    far = lambda x: pltpu.with_memory_space_constraint(x, pltpu.HBM)
    close = lambda x: pltpu.with_memory_space_constraint(x, pltpu.VMEM)
    vmem = pl.BlockSpec(memory_space=pltpu.VMEM)
    smem = pl.BlockSpec(memory_space=pltpu.SMEM)
    hbm = pl.BlockSpec(memory_space=pltpu.HBM)
    coef_shape = jax.ShapeDtypeStruct((per_dev, NEAR * rank), f32)
    params = pltpu.CompilerParams(vmem_limit_bytes=8 * 1024 * 1024)

    coef1, basis_v, assign_v = pl.pallas_call(
        functools.partial(coef_kernel, devices, per_dev),
        in_specs=[vmem, hbm, hbm, hbm],
        out_specs=[vmem] * 3,
        out_shape=[
            coef_shape,
            pltpu.VMEM((samples, rank), bf16),
            pltpu.VMEM((high, LANES), jnp.int32),
        ],
        scratch_shapes=[
            pltpu.VMEM((ROWS, LANES), jnp.int32),
            pltpu.VMEM((ROWS, rank), f32),
            pltpu.VMEM((high, LANES), bf16),
            pltpu.VMEM((high, LANES), f32),
            pltpu.SemaphoreType.DMA((2,)),
            pltpu.SemaphoreType.DMA((samples // COPY,)),
        ],
        compiler_params=params,
        name="coef_pass",
    )(slot_row, far(assign), far(vector), far(basis_rows))

    def to_all(block):
        copies = jnp.broadcast_to(block[None], (devices,) + block.shape)
        return lax.all_to_all(copies, "dev", 0, 0, tiled=True)

    def mix(coef):
        mixed = pl.pallas_call(
            functools.partial(link_kernel, norm, devices, per_dev),
            in_specs=[smem, smem, vmem, vmem],
            out_specs=vmem,
            scratch_shapes=[
                pltpu.VMEM((clusters, rank), f32),
                pltpu.VMEM((per_dev * n_links, rank), f32),
                pltpu.VMEM((8, rank), f32),
            ],
            out_shape=jax.ShapeDtypeStruct((per_dev, rank), bf16),
            compiler_params=params,
            name="link_product",
        )(slot_of, partners, to_all(coef), close(link_blocks))
        return to_all(mixed)

    first, coef2 = pl.pallas_call(
        functools.partial(both_kernel, devices, per_dev),
        in_specs=[vmem] * 5,
        out_specs=[vmem, vmem],
        out_shape=[pltpu.VMEM((high, LANES), f32), coef_shape],
        scratch_shapes=[
            pltpu.VMEM((ROWS, LANES), jnp.int32),
            pltpu.VMEM((ROWS, rank), f32),
            pltpu.VMEM((ROWS, rank), f32),
            pltpu.VMEM((high, LANES), f32),
            pltpu.VMEM((ROWS, TILE), f32),
            pltpu.VMEM((ROWS, TILE), f32),
            pltpu.VMEM((ROWS, TILE), bf16),
            pltpu.VMEM((ROWS, TILE), bf16),
        ],
        compiler_params=params,
        name="first_and_coef_pass",
    )(slot_row, mix(coef1), close(assign_v), scores, close(basis_v))

    out = pl.pallas_call(
        functools.partial(last_kernel, devices, per_dev),
        in_specs=[vmem] * 5,
        out_specs=vmem,
        out_shape=jax.ShapeDtypeStruct((high, LANES), f32),
        scratch_shapes=[
            pltpu.VMEM((ROWS, LANES), jnp.int32),
            pltpu.VMEM((ROWS, rank), f32),
            pltpu.VMEM((ROWS, TILE), f32),
            pltpu.VMEM((ROWS, TILE), f32),
        ],
        compiler_params=params,
        name="last_pass",
    )(slot_row, mix(coef2), close(assign_v), close(first), close(basis_v))
    return out.reshape(samples)


def solution(mesh):
    in_specs = (
        P(("groups", "dev"), None),
        P(("groups", "dev")),
        P(("groups", "dev")),
        P(("groups", "dev")),
        P("groups"),
        P(("groups", "dev"), None),
        P(("groups", "dev"), None, None, None),
    )
    out_specs = P(("groups", "dev"))
    return jax.shard_map(shards, mesh=mesh, in_specs=in_specs, out_specs=out_specs, check_vma=False)
```

```python
import functools
import math

import jax
import jax.numpy as jnp
from jax import lax
from jax.experimental import pallas as pl
from jax.experimental.pallas import tpu as pltpu
from jax.sharding import PartitionSpec as P

REACH = 2
NEAR = 2 * REACH + 1
CL_DEV = 4
S_DEV = 65536
LANES = 128
ROWS = 24

COPY = 4096
TILE = 2048
SLOTS = 4

ridge = 0.5


def near_clusters(devices, per_dev, slot_of_ref, cl_ref):
    clusters = devices * per_dev
    me = lax.axis_index("dev")
    near = lax.broadcasted_iota(jnp.int32, (ROWS, clusters), 0)
    slots = (me + devices - REACH) * per_dev + near
    slots = lax.rem(slots, clusters)
    number = lax.broadcasted_iota(jnp.int32, (ROWS, clusters), 1)
    hit = (slot_of_ref[...] == slots) & (near < NEAR * per_dev)
    found = jnp.sum(jnp.where(hit, number + 1, 0), axis=1, keepdims=True) - 1
    cl_ref[...] = jnp.broadcast_to(found, cl_ref.shape)


def near_rows(devices, per_dev, mixed_ref, rows_ref):
    me = lax.axis_index("dev")
    rows_ref[...] = jnp.zeros_like(rows_ref)
    for g in range(NEAR):
        owner = lax.rem(me + devices + g - REACH, devices)
        rows_ref[g * per_dev : (g + 1) * per_dev, :] = mixed_ref[owner].astype(jnp.float32)


def put_sums(per_dev, sum_ref, out_ref):
    for g in range(NEAR):
        out_ref[:, g * LANES : (g + 1) * LANES] = sum_ref[g * per_dev : (g + 1) * per_dev, :]


def slot_copy(basis_hbm, slots_ref, sem, c):
    slot = lax.rem(c, SLOTS)
    rows = pl.ds(pl.multiple_of(c * COPY, COPY), COPY)
    return pltpu.make_async_copy(basis_hbm.at[rows, :], slots_ref.at[slot], sem.at[slot])


def tile_at(t):
    return pl.ds(pl.multiple_of(t * TILE, TILE), TILE)


def row_at(t, i):
    return pl.ds(t * (TILE // LANES) + i, 1)


def coef_kernel(
    devices, per_dev, slot_of_ref, assign_hbm, vector_hbm, basis_hbm,
    out_ref, turned_ref, assign_ref,
    cl_ref, sum_ref, vector_ref, x_ref, slots_ref, small_sem, basis_sem,
):
    copies = basis_hbm.shape[0] // COPY

    def basis_copy(c):
        return slot_copy(basis_hbm, slots_ref, basis_sem, c)

    assign_copy = pltpu.make_async_copy(assign_hbm, assign_ref, small_sem.at[0])
    vector_copy = pltpu.make_async_copy(vector_hbm, vector_ref, small_sem.at[1])
    assign_copy.start()
    vector_copy.start()
    for c in range(SLOTS):
        basis_copy(c).start()
    near_clusters(devices, per_dev, slot_of_ref, cl_ref)
    sum_ref[...] = jnp.zeros_like(sum_ref)
    assign_copy.wait()
    vector_copy.wait()
    x_ref[...] = vector_ref[...].astype(jnp.float32)
    cl = cl_ref[...]

    @pl.loop(0, copies)
    def _(c):
        basis_copy(c).wait()
        total = sum_ref[...]
        for p in range(COPY // TILE):
            t = c * (COPY // TILE) + p
            parts = []
            for i in range(TILE // LANES):
                hit = assign_ref[row_at(t, i), :] == cl
                parts.append(jnp.where(hit, x_ref[row_at(t, i), :], 0.0).astype(jnp.bfloat16))
            left = jnp.concatenate(parts, axis=1)
            block = slots_ref[lax.rem(c, SLOTS), p * TILE : (p + 1) * TILE, :]
            turned_ref[:, tile_at(t)] = block.T
            total += jnp.dot(left, block, preferred_element_type=jnp.float32)
        sum_ref[...] = total

        @pl.when(c + SLOTS < copies)
        def _():
            basis_copy(c + SLOTS).start()

    put_sums(per_dev, sum_ref, out_ref)


def link_kernel(norm, devices, per_dev, first_time, slot_of_ref, partners_ref, parts_ref, *refs):
    if first_time:
        links_hbm, out_ref, links_ref, scaled_ref, mixed_ref, links_sem = refs
    else:
        links_ref, out_ref, scaled_ref, mixed_ref = refs
    n_links = links_ref.shape[1]
    halves = (0, 1)

    def half_copy(j, h):
        ks = pl.ds(h * (n_links // 2), n_links // 2)
        return pltpu.make_async_copy(links_hbm.at[j, ks], links_ref.at[j, ks], links_sem.at[2 * j + h])

    if first_time:
        for j in range(per_dev):
            for h in halves:
                half_copy(j, h).start()
    for owner in range(devices):
        coef = parts_ref[(owner + REACH) % devices, :, :LANES]
        for g in range(1, NEAR):
            coef += parts_ref[(owner + REACH - g) % devices, :, g * LANES : (g + 1) * LANES]
        scaled_ref[owner * per_dev : (owner + 1) * per_dev, :] = (coef * norm).astype(jnp.bfloat16).astype(jnp.float32)
    mixed_ref[...] = jnp.zeros_like(mixed_ref)
    for j in range(per_dev):
        def body(k, acc):
            s = slot_of_ref[partners_ref[j, k]]
            return acc + links_ref[j, k].astype(jnp.float32) * scaled_ref[pl.ds(s, 1), :]

        acc = jnp.zeros(links_ref.shape[2:], jnp.float32)
        for h in halves:
            if first_time:
                half_copy(j, h).wait()
            acc = lax.fori_loop(h * (n_links // 2), (h + 1) * (n_links // 2), body, acc, unroll=8)
        mixed_ref[j : j + 1, :] = jnp.sum(acc.T, axis=0, keepdims=True)
    out_ref[...] = mixed_ref[:per_dev, :].astype(jnp.bfloat16)


def own_product(hit, products):
    return jnp.sum(jnp.where(hit, products, 0.0), axis=0, keepdims=True)


def both_kernel(
    devices, per_dev, slot_of_ref, mixed_ref, assign_ref, scores_ref, turned_ref, basis_hbm,
    first_ref, out_ref, cl_ref, rows_ref, sum_ref, slope_ref, even_ref, odd_ref, even_left, odd_left, slots_ref, basis_sem,
):
    tiles = turned_ref.shape[1] // TILE
    copies = tiles // 2

    def basis_copy(c):
        return slot_copy(basis_hbm, slots_ref, basis_sem, c)

    for c in range(SLOTS):
        basis_copy(c).start()
    near_clusters(devices, per_dev, slot_of_ref, cl_ref)
    near_rows(devices, per_dev, mixed_ref, rows_ref)
    sum_ref[...] = jnp.zeros_like(sum_ref)
    sig = jax.nn.sigmoid(scores_ref[...])
    slope_ref[...] = sig * (1.0 - sig)
    cl = cl_ref[...]
    rows = rows_ref[...].astype(jnp.bfloat16)
    products_of = (even_ref, odd_ref)
    left_of = (even_left, odd_left)

    def multiply(t, side):
        products_of[side][...] = jnp.dot(rows, turned_ref[:, tile_at(t)], preferred_element_type=jnp.float32)

    def select(t, side):
        for i in range(TILE // LANES):
            at = slice(i * LANES, (i + 1) * LANES)
            hit = assign_ref[row_at(t, i), :] == cl
            first = own_product(hit, products_of[side][:, at])
            first_ref[row_at(t, i), :] = first
            weighted = slope_ref[row_at(t, i), :] * first
            left_of[side][:, at] = jnp.where(hit, weighted, 0.0).astype(jnp.bfloat16)

    def add_up(c, side):
        block = slots_ref[lax.rem(c, SLOTS), side * TILE : (side + 1) * TILE, :]
        sum_ref[...] += jnp.dot(left_of[side][...], block, preferred_element_type=jnp.float32)

    multiply(0, 0)
    select(0, 0)
    multiply(1, 1)

    @pl.loop(0, tiles // 2 - 1)
    def _(i):
        t = 2 * i + 2
        basis_copy(i).wait()
        add_up(i, 0)
        multiply(t, 0)
        select(t - 1, 1)
        add_up(i, 1)
        multiply(t + 1, 1)
        select(t, 0)

        @pl.when(i + SLOTS < copies)
        def _():
            basis_copy(i + SLOTS).start()

    basis_copy(copies - 1).wait()
    add_up(copies - 1, 0)
    select(tiles - 1, 1)
    add_up(copies - 1, 1)
    put_sums(per_dev, sum_ref, out_ref)


def last_kernel(
    devices, per_dev, slot_of_ref, mixed_ref, assign_ref, first_ref, turned_ref, out_ref, cl_ref, rows_ref, even_ref, odd_ref
):
    tiles = turned_ref.shape[1] // TILE
    near_clusters(devices, per_dev, slot_of_ref, cl_ref)
    near_rows(devices, per_dev, mixed_ref, rows_ref)
    cl = cl_ref[...]
    rows = rows_ref[...].astype(jnp.bfloat16)
    products_of = (even_ref, odd_ref)

    def multiply(t, side):
        products_of[side][...] = jnp.dot(rows, turned_ref[:, tile_at(t)], preferred_element_type=jnp.float32)

    def select(t, side):
        for i in range(TILE // LANES):
            hit = assign_ref[row_at(t, i), :] == cl
            second = own_product(hit, products_of[side][:, i * LANES : (i + 1) * LANES])
            out_ref[row_at(t, i), :] = second + ridge * first_ref[row_at(t, i), :]

    multiply(0, 0)

    @pl.loop(0, tiles // 2 - 1)
    def _(i):
        t = 2 * i + 1
        multiply(t, 1)
        select(t - 1, 0)
        multiply(t + 1, 0)
        select(t, 1)

    multiply(tiles - 1, 1)
    select(tiles - 2, 0)
    select(tiles - 1, 1)


def shards(basis_rows, vector, scores, assign, slot_of, partners, link_blocks):
    devices = lax.axis_size("dev")
    clusters = slot_of.shape[0]
    per_dev, n_links, rank, _ = link_blocks.shape
    samples = assign.shape[0]
    norm = 1.0 / math.sqrt(S_DEV // CL_DEV)
    high = samples // LANES
    f32, bf16 = jnp.float32, jnp.bfloat16

    vector = vector.reshape(high, LANES)
    scores = scores.reshape(high, LANES)
    assign = assign.reshape(high, LANES)
    slot_row = slot_of.reshape(1, clusters)

    far = lambda x: pltpu.with_memory_space_constraint(x, pltpu.HBM)
    close = lambda x: pltpu.with_memory_space_constraint(x, pltpu.VMEM)
    vmem = pl.BlockSpec(memory_space=pltpu.VMEM)
    smem = pl.BlockSpec(memory_space=pltpu.SMEM)
    hbm = pl.BlockSpec(memory_space=pltpu.HBM)
    coef_shape = jax.ShapeDtypeStruct((per_dev, NEAR * rank), f32)
    params = pltpu.CompilerParams(vmem_limit_bytes=8 * 1024 * 1024)

    coef1, turned_v, assign_v = pl.pallas_call(
        functools.partial(coef_kernel, devices, per_dev),
        in_specs=[vmem, hbm, hbm, hbm],
        out_specs=[vmem] * 3,
        out_shape=[
            coef_shape,
            pltpu.VMEM((rank, samples), bf16),
            pltpu.VMEM((high, LANES), jnp.int32),
        ],
        scratch_shapes=[
            pltpu.VMEM((ROWS, LANES), jnp.int32),
            pltpu.VMEM((ROWS, rank), f32),
            pltpu.VMEM((high, LANES), bf16),
            pltpu.VMEM((high, LANES), f32),
            pltpu.VMEM((SLOTS, COPY, rank), bf16),
            pltpu.SemaphoreType.DMA((2,)),
            pltpu.SemaphoreType.DMA((SLOTS,)),
        ],
        compiler_params=params,
        name="coef_pass",
    )(slot_row, far(assign), far(vector), far(basis_rows))

    def to_all(block):
        copies = jnp.broadcast_to(block[None], (devices,) + block.shape)
        return lax.all_to_all(copies, "dev", 0, 0, tiled=True)

    def mix(coef, links, first_time):
        out = pl.pallas_call(
            functools.partial(link_kernel, norm, devices, per_dev, first_time),
            in_specs=[smem, smem, vmem, hbm if first_time else vmem],
            out_specs=[vmem, vmem] if first_time else [vmem],
            out_shape=[jax.ShapeDtypeStruct((per_dev, rank), bf16)] + [pltpu.VMEM(links.shape, bf16)] * first_time,
            scratch_shapes=[
                pltpu.VMEM((clusters, rank), f32),
                pltpu.VMEM((8, rank), f32),
            ]
            + [pltpu.SemaphoreType.DMA((2 * per_dev,))] * first_time,
            compiler_params=params,
            name="link_product",
        )(slot_of, partners, to_all(coef), links)
        return (to_all(out[0]), *out[1:])

    mixed1, links_v = mix(coef1, far(link_blocks), True)
    first, coef2 = pl.pallas_call(
        functools.partial(both_kernel, devices, per_dev),
        in_specs=[vmem] * 5 + [hbm],
        out_specs=[vmem, vmem],
        out_shape=[pltpu.VMEM((high, LANES), f32), coef_shape],
        scratch_shapes=[
            pltpu.VMEM((ROWS, LANES), jnp.int32),
            pltpu.VMEM((ROWS, rank), f32),
            pltpu.VMEM((ROWS, rank), f32),
            pltpu.VMEM((high, LANES), f32),
            pltpu.VMEM((ROWS, TILE), f32),
            pltpu.VMEM((ROWS, TILE), f32),
            pltpu.VMEM((ROWS, TILE), bf16),
            pltpu.VMEM((ROWS, TILE), bf16),
            pltpu.VMEM((SLOTS, COPY, rank), bf16),
            pltpu.SemaphoreType.DMA((SLOTS,)),
        ],
        compiler_params=params,
        name="first_and_coef_pass",
    )(slot_row, mixed1, close(assign_v), scores, close(turned_v), far(basis_rows))
    (mixed2,) = mix(coef2, close(links_v), False)

    out = pl.pallas_call(
        functools.partial(last_kernel, devices, per_dev),
        in_specs=[vmem] * 5,
        out_specs=vmem,
        out_shape=jax.ShapeDtypeStruct((high, LANES), f32),
        scratch_shapes=[
            pltpu.VMEM((ROWS, LANES), jnp.int32),
            pltpu.VMEM((ROWS, rank), f32),
            pltpu.VMEM((ROWS, TILE), f32),
            pltpu.VMEM((ROWS, TILE), f32),
        ],
        compiler_params=params,
        name="last_pass",
    )(slot_row, mixed2, close(assign_v), close(first), close(turned_v))
    return out.reshape(samples)


def solution(mesh):
    in_specs = (
        P(("groups", "dev"), None),
        P(("groups", "dev")),
        P(("groups", "dev")),
        P(("groups", "dev")),
        P("groups"),
        P(("groups", "dev"), None),
        P(("groups", "dev"), None, None, None),
    )
    out_specs = P(("groups", "dev"))
    return jax.shard_map(shards, mesh=mesh, in_specs=in_specs, out_specs=out_specs, check_vma=False)
```

```python
import functools
import math

import jax
import jax.numpy as jnp
from jax import lax
from jax.experimental import pallas as pl
from jax.experimental.pallas import tpu as pltpu
from jax.sharding import PartitionSpec as P

REACH = 2
NEAR = 2 * REACH + 1
CL_DEV = 4
S_DEV = 65536
LANES = 128
ROWS = 24

COPY = 2048
TILE = 2048
SLOTS = 8
PIECES = 4

ridge = 0.5


def near_clusters(devices, per_dev, slot_of_ref, cl_ref):
    clusters = devices * per_dev
    me = lax.axis_index("dev")
    near = lax.broadcasted_iota(jnp.int32, (ROWS, clusters), 0)
    slots = (me + devices - REACH) * per_dev + near
    slots = lax.rem(slots, clusters)
    number = lax.broadcasted_iota(jnp.int32, (ROWS, clusters), 1)
    hit = (slot_of_ref[...] == slots) & (near < NEAR * per_dev)
    found = jnp.sum(jnp.where(hit, number + 1, 0), axis=1, keepdims=True) - 1
    cl_ref[...] = jnp.broadcast_to(found, cl_ref.shape)


def near_rows(devices, per_dev, mixed_ref, rows_ref):
    me = lax.axis_index("dev")
    rows_ref[...] = jnp.zeros_like(rows_ref)
    for g in range(NEAR):
        owner = lax.rem(me + devices + g - REACH, devices)
        rows_ref[g * per_dev : (g + 1) * per_dev, :] = mixed_ref[owner].astype(jnp.float32)


def put_sums(per_dev, sum_ref, out_ref):
    for g in range(NEAR):
        out_ref[:, g * LANES : (g + 1) * LANES] = sum_ref[g * per_dev : (g + 1) * per_dev, :].astype(jnp.bfloat16)


def slot_copy(basis_hbm, slots_ref, sem, c):
    slot = lax.rem(c, SLOTS)
    rows = pl.ds(pl.multiple_of(c * COPY, COPY), COPY)
    return pltpu.make_async_copy(basis_hbm.at[rows, :], slots_ref.at[slot], sem.at[slot])


def tile_at(t):
    return pl.ds(pl.multiple_of(t * TILE, TILE), TILE)


def row_at(t, i):
    return pl.ds(t * (TILE // LANES) + i, 1)


def coef_kernel(
    devices, per_dev, slot_of_hbm, assign_hbm, vector_hbm, basis_hbm,
    out_ref, turned_ref, assign_ref,
    slot_of_ref, cl_ref, sum_ref, vector_ref, x_ref, slots_ref, small_sem, basis_sem,
):
    copies = basis_hbm.shape[0] // COPY

    def basis_copy(c):
        return slot_copy(basis_hbm, slots_ref, basis_sem, c)

    slot_of_copy = pltpu.make_async_copy(slot_of_hbm, slot_of_ref, small_sem.at[2])
    assign_copy = pltpu.make_async_copy(assign_hbm, assign_ref, small_sem.at[0])
    vector_copy = pltpu.make_async_copy(vector_hbm, vector_ref, small_sem.at[1])
    slot_of_copy.start()
    assign_copy.start()
    vector_copy.start()
    for c in range(SLOTS):
        basis_copy(c).start()
    slot_of_copy.wait()
    near_clusters(devices, per_dev, slot_of_ref, cl_ref)
    sum_ref[...] = jnp.zeros_like(sum_ref)
    assign_copy.wait()
    vector_copy.wait()
    x_ref[...] = vector_ref[...].astype(jnp.float32)
    cl = cl_ref[...]

    @pl.loop(0, copies)
    def _(c):
        basis_copy(c).wait()
        total = sum_ref[...]
        for p in range(COPY // TILE):
            t = c * (COPY // TILE) + p
            parts = []
            for i in range(TILE // LANES):
                hit = assign_ref[row_at(t, i), :] == cl
                parts.append(jnp.where(hit, x_ref[row_at(t, i), :], 0.0).astype(jnp.bfloat16))
            left = jnp.concatenate(parts, axis=1)
            block = slots_ref[lax.rem(c, SLOTS), p * TILE : (p + 1) * TILE, :]
            turned_ref[:, tile_at(t)] = block.T
            total += jnp.dot(left, block, preferred_element_type=jnp.float32)
        sum_ref[...] = total

        @pl.when(c + SLOTS < copies)
        def _():
            basis_copy(c + SLOTS).start()

    put_sums(per_dev, sum_ref, out_ref)


def link_kernel(norm, devices, per_dev, first_time, slot_of_ref, partners_ref, parts_ref, *refs):
    if first_time:
        links_hbm, out_ref, links_ref, scaled_ref, mixed_ref, links_sem = refs
    else:
        links_ref, out_ref, scaled_ref, mixed_ref = refs
    n_links = links_ref.shape[1]
    piece = n_links // PIECES

    def piece_copy(j, h):
        ks = pl.ds(h * piece, piece)
        return pltpu.make_async_copy(links_hbm.at[j, ks], links_ref.at[j, ks], links_sem.at[PIECES * j + h])

    if first_time:
        for j in range(per_dev):
            for h in range(PIECES):
                piece_copy(j, h).start()
    for owner in range(devices):
        coef = parts_ref[(owner + REACH) % devices, :, :LANES].astype(jnp.float32)
        for g in range(1, NEAR):
            coef += parts_ref[(owner + REACH - g) % devices, :, g * LANES : (g + 1) * LANES].astype(jnp.float32)
        scaled_ref[owner * per_dev : (owner + 1) * per_dev, :] = (coef * norm).astype(jnp.bfloat16).astype(jnp.float32)
    mixed_ref[...] = jnp.zeros_like(mixed_ref)
    for j in range(per_dev):
        def body(k, acc):
            s = slot_of_ref[partners_ref[j, k]]
            return acc + links_ref[j, k].astype(jnp.float32) * scaled_ref[pl.ds(s, 1), :]

        acc = jnp.zeros(links_ref.shape[2:], jnp.float32)
        for h in range(PIECES):
            if first_time:
                piece_copy(j, h).wait()
            acc = lax.fori_loop(h * piece, (h + 1) * piece, body, acc, unroll=8)
        mixed_ref[j : j + 1, :] = jnp.sum(acc.T, axis=0, keepdims=True)
    out_ref[...] = mixed_ref[:per_dev, :].astype(jnp.bfloat16)


def own_product(hit, products):
    return jnp.sum(jnp.where(hit, products, 0.0), axis=0, keepdims=True)


def both_kernel(
    devices, per_dev, slot_of_ref, mixed_ref, assign_ref, scores_ref, turned_ref, basis_hbm,
    first_ref, out_ref, cl_ref, rows_ref, sum_ref, slope_ref, even_ref, odd_ref, even_left, odd_left, slots_ref, basis_sem,
):
    tiles = turned_ref.shape[1] // TILE
    copies = tiles

    def basis_copy(c):
        return slot_copy(basis_hbm, slots_ref, basis_sem, c)

    for c in range(SLOTS):
        basis_copy(c).start()
    near_clusters(devices, per_dev, slot_of_ref, cl_ref)
    near_rows(devices, per_dev, mixed_ref, rows_ref)
    sum_ref[...] = jnp.zeros_like(sum_ref)
    sig = jax.nn.sigmoid(scores_ref[...])
    slope_ref[...] = sig * (1.0 - sig)
    cl = cl_ref[...]
    rows = rows_ref[...].astype(jnp.bfloat16)
    products_of = (even_ref, odd_ref)
    left_of = (even_left, odd_left)

    def multiply(t, side):
        products_of[side][...] = jnp.dot(rows, turned_ref[:, tile_at(t)], preferred_element_type=jnp.float32)

    def select(t, side):
        for i in range(TILE // LANES):
            at = slice(i * LANES, (i + 1) * LANES)
            hit = assign_ref[row_at(t, i), :] == cl
            first = own_product(hit, products_of[side][:, at])
            first_ref[row_at(t, i), :] = first
            weighted = slope_ref[row_at(t, i), :] * first
            left_of[side][:, at] = jnp.where(hit, weighted, 0.0).astype(jnp.bfloat16)

    def add_up(c, side):
        basis_copy(c).wait()
        block = slots_ref[lax.rem(c, SLOTS)]
        sum_ref[...] += jnp.dot(left_of[side][...], block, preferred_element_type=jnp.float32)

    multiply(0, 0)
    select(0, 0)
    multiply(1, 1)

    @pl.loop(0, tiles // 2 - 1)
    def _(i):
        t = 2 * i + 2
        add_up(t - 2, 0)
        multiply(t, 0)
        select(t - 1, 1)
        add_up(t - 1, 1)
        multiply(t + 1, 1)
        select(t, 0)

        @pl.when(t - 2 + SLOTS < copies)
        def _():
            basis_copy(t - 2 + SLOTS).start()
            basis_copy(t - 1 + SLOTS).start()

    add_up(copies - 2, 0)
    select(tiles - 1, 1)
    add_up(copies - 1, 1)
    put_sums(per_dev, sum_ref, out_ref)


def last_kernel(
    devices, per_dev, slot_of_ref, mixed_ref, assign_ref, first_ref, turned_ref, out_ref, cl_ref, rows_ref, even_ref, odd_ref
):
    tiles = turned_ref.shape[1] // TILE
    near_clusters(devices, per_dev, slot_of_ref, cl_ref)
    near_rows(devices, per_dev, mixed_ref, rows_ref)
    cl = cl_ref[...]
    rows = rows_ref[...].astype(jnp.bfloat16)
    products_of = (even_ref, odd_ref)

    def multiply(t, side):
        products_of[side][...] = jnp.dot(rows, turned_ref[:, tile_at(t)], preferred_element_type=jnp.float32)

    def select(t, side):
        for i in range(TILE // LANES):
            hit = assign_ref[row_at(t, i), :] == cl
            second = own_product(hit, products_of[side][:, i * LANES : (i + 1) * LANES])
            out_ref[row_at(t, i), :] = second + ridge * first_ref[row_at(t, i), :]

    multiply(0, 0)

    @pl.loop(0, tiles // 2 - 1)
    def _(i):
        t = 2 * i + 1
        multiply(t, 1)
        select(t - 1, 0)
        multiply(t + 1, 0)
        select(t, 1)

    multiply(tiles - 1, 1)
    select(tiles - 2, 0)
    select(tiles - 1, 1)


def shards(basis_rows, vector, scores, assign, slot_of, partners, link_blocks):
    devices = lax.axis_size("dev")
    clusters = slot_of.shape[0]
    per_dev, n_links, rank, _ = link_blocks.shape
    samples = assign.shape[0]
    norm = 1.0 / math.sqrt(S_DEV // CL_DEV)
    high = samples // LANES
    f32, bf16 = jnp.float32, jnp.bfloat16

    vector = vector.reshape(high, LANES)
    scores = scores.reshape(high, LANES)
    assign = assign.reshape(high, LANES)
    slot_row = slot_of.reshape(1, clusters)

    far = lambda x: pltpu.with_memory_space_constraint(x, pltpu.HBM)
    close = lambda x: pltpu.with_memory_space_constraint(x, pltpu.VMEM)
    vmem = pl.BlockSpec(memory_space=pltpu.VMEM)
    smem = pl.BlockSpec(memory_space=pltpu.SMEM)
    hbm = pl.BlockSpec(memory_space=pltpu.HBM)
    coef_shape = jax.ShapeDtypeStruct((per_dev, NEAR * rank), bf16)
    params = pltpu.CompilerParams(vmem_limit_bytes=8 * 1024 * 1024)

    coef1, turned_v, assign_v = pl.pallas_call(
        functools.partial(coef_kernel, devices, per_dev),
        in_specs=[hbm] * 4,
        out_specs=[vmem] * 3,
        out_shape=[
            coef_shape,
            pltpu.VMEM((rank, samples), bf16),
            pltpu.VMEM((high, LANES), jnp.int32),
        ],
        scratch_shapes=[
            pltpu.VMEM((1, clusters), jnp.int32),
            pltpu.VMEM((ROWS, LANES), jnp.int32),
            pltpu.VMEM((ROWS, rank), f32),
            pltpu.VMEM((high, LANES), bf16),
            pltpu.VMEM((high, LANES), f32),
            pltpu.VMEM((SLOTS, COPY, rank), bf16),
            pltpu.SemaphoreType.DMA((3,)),
            pltpu.SemaphoreType.DMA((SLOTS,)),
        ],
        compiler_params=params,
        name="coef_pass",
    )(far(slot_row), far(assign), far(vector), far(basis_rows))

    def to_all(block):
        copies = jnp.broadcast_to(block[None], (devices,) + block.shape)
        return lax.all_to_all(copies, "dev", 0, 0, tiled=True)

    def mix(coef, links, first_time):
        out = pl.pallas_call(
            functools.partial(link_kernel, norm, devices, per_dev, first_time),
            in_specs=[smem, smem, vmem, hbm if first_time else vmem],
            out_specs=[vmem, vmem] if first_time else [vmem],
            out_shape=[jax.ShapeDtypeStruct((per_dev, rank), bf16)] + [pltpu.VMEM(links.shape, bf16)] * first_time,
            scratch_shapes=[
                pltpu.VMEM((clusters, rank), f32),
                pltpu.VMEM((8, rank), f32),
            ]
            + [pltpu.SemaphoreType.DMA((PIECES * per_dev,))] * first_time,
            compiler_params=params,
            name="link_product",
        )(slot_of, partners, to_all(coef), links)
        return (to_all(out[0]), *out[1:])

    mixed1, links_v = mix(coef1, far(link_blocks), True)
    first, coef2 = pl.pallas_call(
        functools.partial(both_kernel, devices, per_dev),
        in_specs=[vmem] * 5 + [hbm],
        out_specs=[vmem, vmem],
        out_shape=[pltpu.VMEM((high, LANES), f32), coef_shape],
        scratch_shapes=[
            pltpu.VMEM((ROWS, LANES), jnp.int32),
            pltpu.VMEM((ROWS, rank), f32),
            pltpu.VMEM((ROWS, rank), f32),
            pltpu.VMEM((high, LANES), f32),
            pltpu.VMEM((ROWS, TILE), f32),
            pltpu.VMEM((ROWS, TILE), f32),
            pltpu.VMEM((ROWS, TILE), bf16),
            pltpu.VMEM((ROWS, TILE), bf16),
            pltpu.VMEM((SLOTS, COPY, rank), bf16),
            pltpu.SemaphoreType.DMA((SLOTS,)),
        ],
        compiler_params=params,
        name="first_and_coef_pass",
    )(slot_row, mixed1, close(assign_v), scores, close(turned_v), far(basis_rows))
    (mixed2,) = mix(coef2, close(links_v), False)

    out = pl.pallas_call(
        functools.partial(last_kernel, devices, per_dev),
        in_specs=[vmem] * 5,
        out_specs=vmem,
        out_shape=jax.ShapeDtypeStruct((high, LANES), f32),
        scratch_shapes=[
            pltpu.VMEM((ROWS, LANES), jnp.int32),
            pltpu.VMEM((ROWS, rank), f32),
            pltpu.VMEM((ROWS, TILE), f32),
            pltpu.VMEM((ROWS, TILE), f32),
        ],
        compiler_params=params,
        name="last_pass",
    )(slot_row, mixed2, close(assign_v), close(first), close(turned_v))
    return out.reshape(samples)


def solution(mesh):
    in_specs = (
        P(("groups", "dev"), None),
        P(("groups", "dev")),
        P(("groups", "dev")),
        P(("groups", "dev")),
        P("groups"),
        P(("groups", "dev"), None),
        P(("groups", "dev"), None, None, None),
    )
    out_specs = P(("groups", "dev"))
    return jax.shard_map(shards, mesh=mesh, in_specs=in_specs, out_specs=out_specs, check_vma=False)
```

```python
import functools
import math

import jax
import jax.numpy as jnp
from jax import lax
from jax.experimental import pallas as pl
from jax.experimental.pallas import tpu as pltpu
from jax.sharding import PartitionSpec as P

REACH = 2
NEAR = 2 * REACH + 1
CL_DEV = 4
S_DEV = 65536
LANES = 128
ROWS = 24

COPY = 8192
TILE = 2048
PER_COPY = COPY // TILE
SLOTS = 3
INNER = 4
BODY = 8
PIECES = 4

ridge = 0.5


def near_clusters(devices, per_dev, slot_of_ref, cl_ref):
    clusters = devices * per_dev
    me = lax.axis_index("dev")
    near = lax.broadcasted_iota(jnp.int32, (ROWS, clusters), 0)
    slots = (me + devices - REACH) * per_dev + near
    slots = lax.rem(slots, clusters)
    number = lax.broadcasted_iota(jnp.int32, (ROWS, clusters), 1)
    hit = (slot_of_ref[...] == slots) & (near < NEAR * per_dev)
    found = jnp.sum(jnp.where(hit, number + 1, 0), axis=1, keepdims=True) - 1
    cl_ref[...] = jnp.broadcast_to(found, cl_ref.shape)


def near_rows(devices, per_dev, mixed_ref, rows_ref):
    me = lax.axis_index("dev")
    rows_ref[...] = jnp.zeros_like(rows_ref)
    for g in range(NEAR):
        owner = lax.rem(me + devices + g - REACH, devices)
        rows_ref[g * per_dev : (g + 1) * per_dev, :] = mixed_ref[owner].astype(jnp.float32)


def put_sums(per_dev, sum_ref, out_ref):
    for g in range(NEAR):
        out_ref[:, g * LANES : (g + 1) * LANES] = sum_ref[g * per_dev : (g + 1) * per_dev, :].astype(jnp.bfloat16)


def slot_copy(basis_hbm, slots_ref, sem, c):
    slot = lax.rem(c, SLOTS)
    rows = pl.ds(pl.multiple_of(c * COPY, COPY), COPY)
    return pltpu.make_async_copy(basis_hbm.at[rows, :], slots_ref.at[slot], sem.at[slot])


def tile_at(t):
    return pl.ds(pl.multiple_of(t * TILE, TILE), TILE)


def row_at(t, i):
    return pl.ds(t * (TILE // LANES) + i, 1)


def coef_kernel(
    devices, per_dev, slot_of_hbm, assign_hbm, vector_hbm, basis_hbm,
    out_ref, turned_ref, assign_ref,
    slot_of_ref, cl_ref, sum_ref, vector_ref, x_ref, slots_ref, small_sem, basis_sem,
):
    copies = basis_hbm.shape[0] // COPY

    def basis_copy(c):
        return slot_copy(basis_hbm, slots_ref, basis_sem, c)

    slot_of_copy = pltpu.make_async_copy(slot_of_hbm, slot_of_ref, small_sem.at[2])
    assign_copy = pltpu.make_async_copy(assign_hbm, assign_ref, small_sem.at[0])
    vector_copy = pltpu.make_async_copy(vector_hbm, vector_ref, small_sem.at[1])
    slot_of_copy.start()
    assign_copy.start()
    vector_copy.start()
    for c in range(SLOTS):
        basis_copy(c).start()
    slot_of_copy.wait()
    near_clusters(devices, per_dev, slot_of_ref, cl_ref)
    sum_ref[...] = jnp.zeros_like(sum_ref)
    assign_copy.wait()
    vector_copy.wait()
    x_ref[...] = vector_ref[...].astype(jnp.float32)
    cl = cl_ref[...]

    @pl.loop(0, copies)
    def _(c):
        basis_copy(c).wait()
        total = sum_ref[...]
        for p in range(PER_COPY):
            t = c * PER_COPY + p
            parts = []
            for i in range(TILE // LANES):
                hit = assign_ref[row_at(t, i), :] == cl
                parts.append(jnp.where(hit, x_ref[row_at(t, i), :], 0.0).astype(jnp.bfloat16))
            left = jnp.concatenate(parts, axis=1)
            block = slots_ref[lax.rem(c, SLOTS), p * TILE : (p + 1) * TILE, :]
            turned_ref[:, tile_at(t)] = block.T
            total += jnp.dot(left, block, preferred_element_type=jnp.float32)
        sum_ref[...] = total

        @pl.when(c + SLOTS < copies)
        def _():
            basis_copy(c + SLOTS).start()

    put_sums(per_dev, sum_ref, out_ref)


def link_kernel(norm, devices, per_dev, first_time, slot_of_ref, partners_ref, parts_ref, *refs):
    if first_time:
        links_hbm, out_ref, links_ref, scaled_ref, mixed_ref, links_sem = refs
    else:
        links_ref, out_ref, scaled_ref, mixed_ref = refs
    n_links = links_ref.shape[1]
    piece = n_links // PIECES

    def piece_copy(j, h):
        ks = pl.ds(h * piece, piece)
        return pltpu.make_async_copy(links_hbm.at[j, ks], links_ref.at[j, ks], links_sem.at[PIECES * j + h])

    if first_time:
        for j in range(per_dev):
            for h in range(PIECES):
                piece_copy(j, h).start()
    for owner in range(devices):
        coef = parts_ref[(owner + REACH) % devices, :, :LANES].astype(jnp.float32)
        for g in range(1, NEAR):
            coef += parts_ref[(owner + REACH - g) % devices, :, g * LANES : (g + 1) * LANES].astype(jnp.float32)
        scaled_ref[owner * per_dev : (owner + 1) * per_dev, :] = (coef * norm).astype(jnp.bfloat16).astype(jnp.float32)
    mixed_ref[...] = jnp.zeros_like(mixed_ref)
    for j in range(per_dev):
        def body(k, acc):
            s = slot_of_ref[partners_ref[j, k]]
            return acc + links_ref[j, k].astype(jnp.float32) * scaled_ref[pl.ds(s, 1), :]

        acc = jnp.zeros(links_ref.shape[2:], jnp.float32)
        for h in range(PIECES):
            if first_time:
                piece_copy(j, h).wait()
            acc = lax.fori_loop(h * piece, (h + 1) * piece, body, acc, unroll=8)
        mixed_ref[j : j + 1, :] = jnp.sum(acc.T, axis=0, keepdims=True)
    out_ref[...] = mixed_ref[:per_dev, :].astype(jnp.bfloat16)


def own_product(hit, products):
    return jnp.sum(jnp.where(hit, products, 0.0), axis=0, keepdims=True)


def both_kernel(
    devices, per_dev, slot_of_ref, mixed_ref, assign_ref, scores_ref, turned_ref, basis_hbm,
    first_ref, out_ref, cl_ref, rows_ref, sum_ref, slope_ref, even_ref, odd_ref, even_left, odd_left, slots_ref, basis_sem,
):
    tiles = turned_ref.shape[1] // TILE
    copies = tiles // PER_COPY

    def basis_copy(c):
        return slot_copy(basis_hbm, slots_ref, basis_sem, c)

    for c in range(SLOTS):
        basis_copy(c).start()
    near_clusters(devices, per_dev, slot_of_ref, cl_ref)
    near_rows(devices, per_dev, mixed_ref, rows_ref)
    sum_ref[...] = jnp.zeros_like(sum_ref)
    sig = jax.nn.sigmoid(scores_ref[...])
    slope_ref[...] = sig * (1.0 - sig)
    cl = cl_ref[...]
    rows = rows_ref[...].astype(jnp.bfloat16)
    products_of = (even_ref, odd_ref)
    left_of = (even_left, odd_left)

    def multiply(t, side):
        products_of[side][...] = jnp.dot(rows, turned_ref[:, tile_at(t)], preferred_element_type=jnp.float32)

    def select(t, side):
        for i in range(TILE // LANES):
            at = slice(i * LANES, (i + 1) * LANES)
            hit = assign_ref[row_at(t, i), :] == cl
            first = own_product(hit, products_of[side][:, at])
            first_ref[row_at(t, i), :] = first
            weighted = slope_ref[row_at(t, i), :] * first
            left_of[side][:, at] = jnp.where(hit, weighted, 0.0).astype(jnp.bfloat16)

    def add_up(c, p):
        block = slots_ref[lax.rem(c, SLOTS), p * TILE : (p + 1) * TILE, :]
        sum_ref[...] += jnp.dot(left_of[p % 2][...], block, preferred_element_type=jnp.float32)

    multiply(0, 0)
    select(0, 0)
    multiply(1, 1)

    @pl.loop(0, copies - 1)
    def _(c):
        basis_copy(c).wait()
        for p in range(PER_COPY):
            t = c * PER_COPY + p
            add_up(c, p)
            multiply(t + 2, p % 2)
            select(t + 1, (p + 1) % 2)

        @pl.when(c + SLOTS < copies)
        def _():
            basis_copy(c + SLOTS).start()

    basis_copy(copies - 1).wait()
    for p in range(PER_COPY):
        t = (copies - 1) * PER_COPY + p
        add_up(copies - 1, p)
        if p + 2 < PER_COPY:
            multiply(t + 2, p % 2)
        if p + 1 < PER_COPY:
            select(t + 1, (p + 1) % 2)
    put_sums(per_dev, sum_ref, out_ref)


def last_kernel(
    devices, per_dev, slot_of_ref, mixed_ref, assign_ref, first_ref, turned_ref, out_ref, cl_ref, rows_ref, even_ref, odd_ref
):
    tiles = turned_ref.shape[1] // TILE
    near_clusters(devices, per_dev, slot_of_ref, cl_ref)
    near_rows(devices, per_dev, mixed_ref, rows_ref)
    cl = cl_ref[...]
    rows = rows_ref[...].astype(jnp.bfloat16)
    products_of = (even_ref, odd_ref)

    def multiply(t, side):
        products_of[side][...] = jnp.dot(rows, turned_ref[:, tile_at(t)], preferred_element_type=jnp.float32)

    def select(t, side):
        for i in range(TILE // LANES):
            hit = assign_ref[row_at(t, i), :] == cl
            second = own_product(hit, products_of[side][:, i * LANES : (i + 1) * LANES])
            out_ref[row_at(t, i), :] = second + ridge * first_ref[row_at(t, i), :]

    multiply(0, 0)

    @pl.loop(0, tiles // BODY)
    def _(c):
        for p in range(BODY):
            t = c * BODY + p
            multiply(lax.rem(t + 1, tiles), (p + 1) % 2)
            select(t, p % 2)


def shards(basis_rows, vector, scores, assign, slot_of, partners, link_blocks):
    devices = lax.axis_size("dev")
    clusters = slot_of.shape[0]
    per_dev, n_links, rank, _ = link_blocks.shape
    samples = assign.shape[0]
    norm = 1.0 / math.sqrt(S_DEV // CL_DEV)
    high = samples // LANES
    f32, bf16 = jnp.float32, jnp.bfloat16

    vector = vector.reshape(high, LANES)
    scores = scores.reshape(high, LANES)
    assign = assign.reshape(high, LANES)
    slot_row = slot_of.reshape(1, clusters)

    far = lambda x: pltpu.with_memory_space_constraint(x, pltpu.HBM)
    close = lambda x: pltpu.with_memory_space_constraint(x, pltpu.VMEM)
    vmem = pl.BlockSpec(memory_space=pltpu.VMEM)
    smem = pl.BlockSpec(memory_space=pltpu.SMEM)
    hbm = pl.BlockSpec(memory_space=pltpu.HBM)
    coef_shape = jax.ShapeDtypeStruct((per_dev, NEAR * rank), bf16)
    params = pltpu.CompilerParams(vmem_limit_bytes=10 * 1024 * 1024)

    coef1, turned_v, assign_v = pl.pallas_call(
        functools.partial(coef_kernel, devices, per_dev),
        in_specs=[hbm] * 4,
        out_specs=[vmem] * 3,
        out_shape=[
            coef_shape,
            pltpu.VMEM((rank, samples), bf16),
            pltpu.VMEM((high, LANES), jnp.int32),
        ],
        scratch_shapes=[
            pltpu.VMEM((1, clusters), jnp.int32),
            pltpu.VMEM((ROWS, LANES), jnp.int32),
            pltpu.VMEM((ROWS, rank), f32),
            pltpu.VMEM((high, LANES), bf16),
            pltpu.VMEM((high, LANES), f32),
            pltpu.VMEM((SLOTS, COPY, rank), bf16),
            pltpu.SemaphoreType.DMA((3,)),
            pltpu.SemaphoreType.DMA((SLOTS,)),
        ],
        compiler_params=params,
        name="coef_pass",
    )(far(slot_row), far(assign), far(vector), far(basis_rows))

    def to_all(block):
        copies = jnp.broadcast_to(block[None], (devices,) + block.shape)
        return lax.all_to_all(copies, "dev", 0, 0, tiled=True)

    def to_all_by_phases(block):
        outer = devices // INNER
        near_by = [[o * INNER + i for i in range(INNER)] for o in range(outer)]
        across = [[o * INNER + i for o in range(outer)] for i in range(INNER)]
        copies = jnp.broadcast_to(block[None], (INNER,) + block.shape)
        block = lax.all_to_all(copies, "dev", 0, 0, axis_index_groups=near_by, tiled=True)
        copies = jnp.broadcast_to(block[None], (outer,) + block.shape)
        copies = lax.all_to_all(copies, "dev", 0, 0, axis_index_groups=across, tiled=True)
        return copies.reshape((devices,) + block.shape[1:])

    def mix(coef, links, first_time):
        send = to_all if first_time else to_all_by_phases
        out = pl.pallas_call(
            functools.partial(link_kernel, norm, devices, per_dev, first_time),
            in_specs=[smem, smem, vmem, hbm if first_time else vmem],
            out_specs=[vmem, vmem] if first_time else [vmem],
            out_shape=[jax.ShapeDtypeStruct((per_dev, rank), bf16)] + [pltpu.VMEM(links.shape, bf16)] * first_time,
            scratch_shapes=[
                pltpu.VMEM((clusters, rank), f32),
                pltpu.VMEM((8, rank), f32),
            ]
            + [pltpu.SemaphoreType.DMA((PIECES * per_dev,))] * first_time,
            compiler_params=params,
            name="link_product",
        )(slot_of, partners, send(coef), links)
        return (send(out[0]), *out[1:])

    mixed1, links_v = mix(coef1, far(link_blocks), True)
    first, coef2 = pl.pallas_call(
        functools.partial(both_kernel, devices, per_dev),
        in_specs=[vmem] * 5 + [hbm],
        out_specs=[vmem, vmem],
        out_shape=[pltpu.VMEM((high, LANES), f32), coef_shape],
        scratch_shapes=[
            pltpu.VMEM((ROWS, LANES), jnp.int32),
            pltpu.VMEM((ROWS, rank), f32),
            pltpu.VMEM((ROWS, rank), f32),
            pltpu.VMEM((high, LANES), f32),
            pltpu.VMEM((ROWS, TILE), f32),
            pltpu.VMEM((ROWS, TILE), f32),
            pltpu.VMEM((ROWS, TILE), bf16),
            pltpu.VMEM((ROWS, TILE), bf16),
            pltpu.VMEM((SLOTS, COPY, rank), bf16),
            pltpu.SemaphoreType.DMA((SLOTS,)),
        ],
        compiler_params=params,
        name="first_and_coef_pass",
    )(slot_row, mixed1, close(assign_v), scores, close(turned_v), far(basis_rows))
    (mixed2,) = mix(coef2, close(links_v), False)

    out = pl.pallas_call(
        functools.partial(last_kernel, devices, per_dev),
        in_specs=[vmem] * 5,
        out_specs=vmem,
        out_shape=jax.ShapeDtypeStruct((high, LANES), f32),
        scratch_shapes=[
            pltpu.VMEM((ROWS, LANES), jnp.int32),
            pltpu.VMEM((ROWS, rank), f32),
            pltpu.VMEM((ROWS, TILE), f32),
            pltpu.VMEM((ROWS, TILE), f32),
        ],
        compiler_params=params,
        name="last_pass",
    )(slot_row, mixed2, close(assign_v), close(first), close(turned_v))
    return out.reshape(samples)


def solution(mesh):
    in_specs = (
        P(("groups", "dev"), None),
        P(("groups", "dev")),
        P(("groups", "dev")),
        P(("groups", "dev")),
        P("groups"),
        P(("groups", "dev"), None),
        P(("groups", "dev"), None, None, None),
    )
    out_specs = P(("groups", "dev"))
    return jax.shard_map(shards, mesh=mesh, in_specs=in_specs, out_specs=out_specs, check_vma=False)
```

```python
import functools
import math

import jax
import jax.numpy as jnp
from jax import lax
from jax.experimental import pallas as pl
from jax.experimental.pallas import tpu as pltpu
from jax.sharding import PartitionSpec as P

REACH = 2
NEAR = 2 * REACH + 1
CL_DEV = 4
S_DEV = 65536
LANES = 128
ROWS = 24

COPY = 8192
TILE = 2048
PER_COPY = COPY // TILE
SLOTS = 3
BODY = 16
PIECES = 4

ridge = 0.5


def near_clusters(devices, per_dev, slot_of_ref, cl_ref):
    clusters = devices * per_dev
    me = lax.axis_index("dev")
    near = lax.broadcasted_iota(jnp.int32, (ROWS, clusters), 0)
    slots = (me + devices - REACH) * per_dev + near
    slots = lax.rem(slots, clusters)
    number = lax.broadcasted_iota(jnp.int32, (ROWS, clusters), 1)
    hit = (slot_of_ref[...] == slots) & (near < NEAR * per_dev)
    found = jnp.sum(jnp.where(hit, number + 1, 0), axis=1, keepdims=True) - 1
    cl_ref[...] = jnp.broadcast_to(found, cl_ref.shape)


def near_rows(devices, per_dev, mixed_ref, rows_ref):
    me = lax.axis_index("dev")
    rows_ref[...] = jnp.zeros_like(rows_ref)
    for g in range(NEAR):
        owner = lax.rem(me + devices + g - REACH, devices)
        rows_ref[g * per_dev : (g + 1) * per_dev, :] = mixed_ref[owner].astype(jnp.float32)


def put_sums(per_dev, sum_ref, out_ref):
    for g in range(NEAR):
        out_ref[:, g * LANES : (g + 1) * LANES] = sum_ref[g * per_dev : (g + 1) * per_dev, :].astype(jnp.bfloat16)


def slot_copy(basis_hbm, slots_ref, sem, c):
    slot = lax.rem(c, SLOTS)
    rows = pl.ds(pl.multiple_of(c * COPY, COPY), COPY)
    return pltpu.make_async_copy(basis_hbm.at[rows, :], slots_ref.at[slot], sem.at[slot])


def tile_at(t):
    return pl.ds(pl.multiple_of(t * TILE, TILE), TILE)


def row_at(t, i):
    return pl.ds(t * (TILE // LANES) + i, 1)


def coef_kernel(
    devices, per_dev, slot_of_hbm, assign_hbm, vector_hbm, basis_hbm,
    out_ref, turned_ref, assign_ref,
    slot_of_ref, cl_ref, sum_ref, vector_ref, x_ref, slots_ref, small_sem, basis_sem,
):
    copies = basis_hbm.shape[0] // COPY

    def basis_copy(c):
        return slot_copy(basis_hbm, slots_ref, basis_sem, c)

    slot_of_copy = pltpu.make_async_copy(slot_of_hbm, slot_of_ref, small_sem.at[2])
    assign_copy = pltpu.make_async_copy(assign_hbm, assign_ref, small_sem.at[0])
    vector_copy = pltpu.make_async_copy(vector_hbm, vector_ref, small_sem.at[1])
    slot_of_copy.start()
    assign_copy.start()
    vector_copy.start()
    for c in range(SLOTS):
        basis_copy(c).start()
    slot_of_copy.wait()
    near_clusters(devices, per_dev, slot_of_ref, cl_ref)
    sum_ref[...] = jnp.zeros_like(sum_ref)
    assign_copy.wait()
    vector_copy.wait()
    x_ref[...] = vector_ref[...].astype(jnp.float32)
    cl = cl_ref[...]

    @pl.loop(0, copies)
    def _(c):
        basis_copy(c).wait()
        total = sum_ref[...]
        for p in range(PER_COPY):
            t = c * PER_COPY + p
            parts = []
            for i in range(TILE // LANES):
                hit = assign_ref[row_at(t, i), :] == cl
                parts.append(jnp.where(hit, x_ref[row_at(t, i), :], 0.0).astype(jnp.bfloat16))
            left = jnp.concatenate(parts, axis=1)
            block = slots_ref[lax.rem(c, SLOTS), p * TILE : (p + 1) * TILE, :]
            turned_ref[:, tile_at(t)] = block.T
            total += jnp.dot(left, block, preferred_element_type=jnp.float32)
        sum_ref[...] = total

        @pl.when(c + SLOTS < copies)
        def _():
            basis_copy(c + SLOTS).start()

    put_sums(per_dev, sum_ref, out_ref)


def link_kernel(norm, devices, per_dev, first_time, slot_of_ref, partners_ref, parts_ref, *refs):
    if first_time:
        links_hbm, out_ref, links_ref, scaled_ref, mixed_ref, links_sem = refs
    else:
        links_ref, out_ref, scaled_ref, mixed_ref = refs
    n_links = links_ref.shape[1]
    piece = n_links // PIECES

    def piece_copy(j, h):
        ks = pl.ds(h * piece, piece)
        return pltpu.make_async_copy(links_hbm.at[j, ks], links_ref.at[j, ks], links_sem.at[PIECES * j + h])

    if first_time:
        for j in range(per_dev):
            for h in range(PIECES):
                piece_copy(j, h).start()
    for owner in range(devices):
        coef = parts_ref[(owner + REACH) % devices, :, :LANES].astype(jnp.float32)
        for g in range(1, NEAR):
            coef += parts_ref[(owner + REACH - g) % devices, :, g * LANES : (g + 1) * LANES].astype(jnp.float32)
        scaled_ref[owner * per_dev : (owner + 1) * per_dev, :] = (coef * norm).astype(jnp.bfloat16).astype(jnp.float32)
    mixed_ref[...] = jnp.zeros_like(mixed_ref)
    for j in range(per_dev):
        def body(k, acc):
            s = slot_of_ref[partners_ref[j, k]]
            return acc + links_ref[j, k].astype(jnp.float32) * scaled_ref[pl.ds(s, 1), :]

        acc = jnp.zeros(links_ref.shape[2:], jnp.float32)
        for h in range(PIECES):
            if first_time:
                piece_copy(j, h).wait()
            acc = lax.fori_loop(h * piece, (h + 1) * piece, body, acc, unroll=16)
        mixed_ref[j : j + 1, :] = jnp.sum(acc.T, axis=0, keepdims=True)
    out_ref[...] = mixed_ref[:per_dev, :].astype(jnp.bfloat16)


def own_product(hit, products):
    return jnp.sum(jnp.where(hit, products, 0.0), axis=0, keepdims=True)


def both_kernel(
    devices, per_dev, slot_of_ref, mixed_ref, assign_ref, scores_ref, turned_ref, basis_hbm,
    first_ref, out_ref, cl_ref, rows_ref, sum_ref, slope_ref, even_ref, odd_ref, even_left, odd_left, slots_ref, basis_sem,
):
    tiles = turned_ref.shape[1] // TILE
    copies = tiles // PER_COPY

    def basis_copy(c):
        return slot_copy(basis_hbm, slots_ref, basis_sem, c)

    for c in range(SLOTS):
        basis_copy(c).start()
    near_clusters(devices, per_dev, slot_of_ref, cl_ref)
    near_rows(devices, per_dev, mixed_ref, rows_ref)
    sum_ref[...] = jnp.zeros_like(sum_ref)
    sig = jax.nn.sigmoid(scores_ref[...])
    slope_ref[...] = sig * (1.0 - sig)
    cl = cl_ref[...]
    rows = rows_ref[...].astype(jnp.bfloat16)
    products_of = (even_ref, odd_ref)
    left_of = (even_left, odd_left)

    def multiply(t, side):
        products_of[side][...] = jnp.dot(rows, turned_ref[:, tile_at(t)], preferred_element_type=jnp.float32)

    def select(t, side):
        for i in range(TILE // LANES):
            at = slice(i * LANES, (i + 1) * LANES)
            hit = assign_ref[row_at(t, i), :] == cl
            first = own_product(hit, products_of[side][:, at])
            first_ref[row_at(t, i), :] = first
            weighted = slope_ref[row_at(t, i), :] * first
            left_of[side][:, at] = jnp.where(hit, weighted, 0.0).astype(jnp.bfloat16)

    def add_up(c, p):
        block = slots_ref[lax.rem(c, SLOTS), p * TILE : (p + 1) * TILE, :]
        sum_ref[...] += jnp.dot(left_of[p % 2][...], block, preferred_element_type=jnp.float32)

    multiply(0, 0)
    select(0, 0)
    multiply(1, 1)

    @pl.loop(0, copies - 1)
    def _(c):
        basis_copy(c).wait()
        for p in range(PER_COPY):
            t = c * PER_COPY + p
            add_up(c, p)
            multiply(t + 2, p % 2)
            select(t + 1, (p + 1) % 2)

        @pl.when(c + SLOTS < copies)
        def _():
            basis_copy(c + SLOTS).start()

    basis_copy(copies - 1).wait()
    for p in range(PER_COPY):
        t = (copies - 1) * PER_COPY + p
        add_up(copies - 1, p)
        if p + 2 < PER_COPY:
            multiply(t + 2, p % 2)
        if p + 1 < PER_COPY:
            select(t + 1, (p + 1) % 2)
    put_sums(per_dev, sum_ref, out_ref)


def last_kernel(
    devices, per_dev, slot_of_ref, mixed_ref, assign_ref, first_ref, turned_ref, out_ref, cl_ref, rows_ref, even_ref, odd_ref
):
    tiles = turned_ref.shape[1] // TILE
    near_clusters(devices, per_dev, slot_of_ref, cl_ref)
    near_rows(devices, per_dev, mixed_ref, rows_ref)
    cl = cl_ref[...]
    rows = rows_ref[...].astype(jnp.bfloat16)
    products_of = (even_ref, odd_ref)

    def multiply(t, side):
        products_of[side][...] = jnp.dot(rows, turned_ref[:, tile_at(t)], preferred_element_type=jnp.float32)

    def select(t, side):
        for i in range(TILE // LANES):
            hit = assign_ref[row_at(t, i), :] == cl
            second = own_product(hit, products_of[side][:, i * LANES : (i + 1) * LANES])
            out_ref[row_at(t, i), :] = second + ridge * first_ref[row_at(t, i), :]

    multiply(0, 0)

    @pl.loop(0, tiles // BODY)
    def _(c):
        for p in range(BODY):
            t = c * BODY + p
            multiply(lax.rem(t + 1, tiles), (p + 1) % 2)
            select(t, p % 2)


def shards(basis_rows, vector, scores, assign, slot_of, partners, link_blocks):
    devices = lax.axis_size("dev")
    clusters = slot_of.shape[0]
    per_dev, n_links, rank, _ = link_blocks.shape
    samples = assign.shape[0]
    norm = 1.0 / math.sqrt(S_DEV // CL_DEV)
    high = samples // LANES
    f32, bf16 = jnp.float32, jnp.bfloat16

    vector = vector.reshape(high, LANES)
    scores = scores.reshape(high, LANES)
    assign = assign.reshape(high, LANES)
    slot_row = slot_of.reshape(1, clusters)

    far = lambda x: pltpu.with_memory_space_constraint(x, pltpu.HBM)
    close = lambda x: pltpu.with_memory_space_constraint(x, pltpu.VMEM)
    vmem = pl.BlockSpec(memory_space=pltpu.VMEM)
    smem = pl.BlockSpec(memory_space=pltpu.SMEM)
    hbm = pl.BlockSpec(memory_space=pltpu.HBM)
    coef_shape = jax.ShapeDtypeStruct((per_dev, NEAR * rank), bf16)
    params = pltpu.CompilerParams(vmem_limit_bytes=10 * 1024 * 1024)

    coef1, turned_v, assign_v = pl.pallas_call(
        functools.partial(coef_kernel, devices, per_dev),
        in_specs=[hbm] * 4,
        out_specs=[vmem] * 3,
        out_shape=[
            coef_shape,
            pltpu.VMEM((rank, samples), bf16),
            pltpu.VMEM((high, LANES), jnp.int32),
        ],
        scratch_shapes=[
            pltpu.VMEM((1, clusters), jnp.int32),
            pltpu.VMEM((ROWS, LANES), jnp.int32),
            pltpu.VMEM((ROWS, rank), f32),
            pltpu.VMEM((high, LANES), bf16),
            pltpu.VMEM((high, LANES), f32),
            pltpu.VMEM((SLOTS, COPY, rank), bf16),
            pltpu.SemaphoreType.DMA((3,)),
            pltpu.SemaphoreType.DMA((SLOTS,)),
        ],
        compiler_params=params,
        name="coef_pass",
    )(far(slot_row), far(assign), far(vector), far(basis_rows))

    def to_all(block):
        copies = jnp.broadcast_to(block[None], (devices,) + block.shape)
        return lax.all_to_all(copies, "dev", 0, 0, tiled=True)

    def mix(coef, links, first_time):
        out = pl.pallas_call(
            functools.partial(link_kernel, norm, devices, per_dev, first_time),
            in_specs=[smem, smem, vmem, hbm if first_time else vmem],
            out_specs=[vmem, vmem] if first_time else [vmem],
            out_shape=[jax.ShapeDtypeStruct((per_dev, rank), bf16)] + [pltpu.VMEM(links.shape, bf16)] * first_time,
            scratch_shapes=[
                pltpu.VMEM((clusters, rank), f32),
                pltpu.VMEM((8, rank), f32),
            ]
            + [pltpu.SemaphoreType.DMA((PIECES * per_dev,))] * first_time,
            compiler_params=params,
            name="link_product",
        )(slot_of, partners, to_all(coef), links)
        return (to_all(out[0]), *out[1:])

    mixed1, links_v = mix(coef1, far(link_blocks), True)
    first, coef2 = pl.pallas_call(
        functools.partial(both_kernel, devices, per_dev),
        in_specs=[vmem] * 5 + [hbm],
        out_specs=[vmem, vmem],
        out_shape=[pltpu.VMEM((high, LANES), f32), coef_shape],
        scratch_shapes=[
            pltpu.VMEM((ROWS, LANES), jnp.int32),
            pltpu.VMEM((ROWS, rank), f32),
            pltpu.VMEM((ROWS, rank), f32),
            pltpu.VMEM((high, LANES), f32),
            pltpu.VMEM((ROWS, TILE), f32),
            pltpu.VMEM((ROWS, TILE), f32),
            pltpu.VMEM((ROWS, TILE), bf16),
            pltpu.VMEM((ROWS, TILE), bf16),
            pltpu.VMEM((SLOTS, COPY, rank), bf16),
            pltpu.SemaphoreType.DMA((SLOTS,)),
        ],
        compiler_params=params,
        name="first_and_coef_pass",
    )(slot_row, mixed1, close(assign_v), scores, close(turned_v), far(basis_rows))
    (mixed2,) = mix(coef2, close(links_v), False)

    out = pl.pallas_call(
        functools.partial(last_kernel, devices, per_dev),
        in_specs=[vmem] * 5,
        out_specs=vmem,
        out_shape=jax.ShapeDtypeStruct((high, LANES), f32),
        scratch_shapes=[
            pltpu.VMEM((ROWS, LANES), jnp.int32),
            pltpu.VMEM((ROWS, rank), f32),
            pltpu.VMEM((ROWS, TILE), f32),
            pltpu.VMEM((ROWS, TILE), f32),
        ],
        compiler_params=params,
        name="last_pass",
    )(slot_row, mixed2, close(assign_v), close(first), close(turned_v))
    return out.reshape(samples)


def solution(mesh):
    in_specs = (
        P(("groups", "dev"), None),
        P(("groups", "dev")),
        P(("groups", "dev")),
        P(("groups", "dev")),
        P("groups"),
        P(("groups", "dev"), None),
        P(("groups", "dev"), None, None, None),
    )
    out_specs = P(("groups", "dev"))
    return jax.shard_map(shards, mesh=mesh, in_specs=in_specs, out_specs=out_specs, check_vma=False)
```

```python
import functools
import math

import jax
import jax.numpy as jnp
from jax import lax
from jax.experimental import pallas as pl
from jax.experimental.pallas import tpu as pltpu
from jax.sharding import PartitionSpec as P

REACH = 2
NEAR = 2 * REACH + 1
CL_DEV = 4
S_DEV = 65536
LANES = 128
ROWS = 24

COPY = 8192
TILE = 2048
PER_COPY = COPY // TILE
SLOTS = 3
BODY = 16
FOLD = 4
WIDE = LANES // FOLD
PIECES = 4

ridge = 0.5


def near_clusters(devices, per_dev, slot_of_ref, cl_ref):
    clusters = devices * per_dev
    me = lax.axis_index("dev")
    near = lax.broadcasted_iota(jnp.int32, (ROWS, clusters), 0)
    slots = (me + devices - REACH) * per_dev + near
    slots = lax.rem(slots, clusters)
    number = lax.broadcasted_iota(jnp.int32, (ROWS, clusters), 1)
    hit = (slot_of_ref[...] == slots) & (near < NEAR * per_dev)
    found = jnp.sum(jnp.where(hit, number + 1, 0), axis=1, keepdims=True) - 1
    cl_ref[...] = jnp.broadcast_to(found, cl_ref.shape)


def near_rows(devices, per_dev, mixed_ref, rows_ref):
    me = lax.axis_index("dev")
    rows_ref[...] = jnp.zeros_like(rows_ref)
    for g in range(NEAR):
        owner = lax.rem(me + devices + g - REACH, devices)
        rows_ref[g * per_dev : (g + 1) * per_dev, :] = mixed_ref[owner].astype(jnp.float32)


def put_sums(per_dev, sum_ref, out_ref):
    for g in range(NEAR):
        out_ref[:, g * LANES : (g + 1) * LANES] = sum_ref[g * per_dev : (g + 1) * per_dev, :].astype(jnp.bfloat16)


def slot_copy(basis_hbm, slots_ref, sem, c):
    slot = lax.rem(c, SLOTS)
    rows = pl.ds(pl.multiple_of(c * COPY, COPY), COPY)
    return pltpu.make_async_copy(basis_hbm.at[rows, :], slots_ref.at[slot], sem.at[slot])


def tile_at(t):
    return pl.ds(pl.multiple_of(t * TILE, TILE), TILE)


def row_at(t, i):
    return pl.ds(t * (TILE // LANES) + i, 1)


def coef_kernel(
    devices, per_dev, slot_of_hbm, assign_hbm, vector_hbm, basis_hbm,
    out_ref, turned_ref, assign_ref,
    slot_of_ref, cl_ref, sum_ref, vector_ref, x_ref, slots_ref, small_sem, basis_sem,
):
    copies = basis_hbm.shape[0] // COPY

    def basis_copy(c):
        return slot_copy(basis_hbm, slots_ref, basis_sem, c)

    slot_of_copy = pltpu.make_async_copy(slot_of_hbm, slot_of_ref, small_sem.at[2])
    assign_copy = pltpu.make_async_copy(assign_hbm, assign_ref, small_sem.at[0])
    vector_copy = pltpu.make_async_copy(vector_hbm, vector_ref, small_sem.at[1])
    slot_of_copy.start()
    assign_copy.start()
    vector_copy.start()
    for c in range(SLOTS):
        basis_copy(c).start()
    slot_of_copy.wait()
    near_clusters(devices, per_dev, slot_of_ref, cl_ref)
    sum_ref[...] = jnp.zeros_like(sum_ref)
    assign_copy.wait()
    vector_copy.wait()
    x_ref[...] = vector_ref[...].astype(jnp.float32)
    cl = cl_ref[...]

    @pl.loop(0, copies)
    def _(c):
        basis_copy(c).wait()
        total = sum_ref[...]
        for p in range(PER_COPY):
            t = c * PER_COPY + p
            parts = []
            for i in range(TILE // LANES):
                hit = assign_ref[row_at(t, i), :] == cl
                parts.append(jnp.where(hit, x_ref[row_at(t, i), :], 0.0).astype(jnp.bfloat16))
            left = jnp.concatenate(parts, axis=1)
            block = slots_ref[lax.rem(c, SLOTS), p * TILE : (p + 1) * TILE, :]
            turned_ref[:, tile_at(t)] = block.T
            total += jnp.dot(left, block, preferred_element_type=jnp.float32)
        sum_ref[...] = total

        @pl.when(c + SLOTS < copies)
        def _():
            basis_copy(c + SLOTS).start()

    put_sums(per_dev, sum_ref, out_ref)


def link_kernel(norm, devices, per_dev, first_time, slot_of_ref, partners_ref, parts_ref, *refs):
    if first_time:
        links_hbm, out_ref, links_ref, scaled_ref, mixed_ref, links_sem = refs
    else:
        links_ref, out_ref, scaled_ref, mixed_ref = refs
    n_links = links_ref.shape[1]
    piece = n_links // PIECES

    def piece_copy(j, h):
        ks = pl.ds(h * piece, piece)
        return pltpu.make_async_copy(links_hbm.at[j, ks], links_ref.at[j, ks], links_sem.at[PIECES * j + h])

    if first_time:
        for j in range(per_dev):
            for h in range(PIECES):
                piece_copy(j, h).start()
    for owner in range(devices):
        coef = parts_ref[(owner + REACH) % devices, :, :LANES].astype(jnp.float32)
        for g in range(1, NEAR):
            coef += parts_ref[(owner + REACH - g) % devices, :, g * LANES : (g + 1) * LANES].astype(jnp.float32)
        scaled_ref[owner * per_dev : (owner + 1) * per_dev, :] = (coef * norm).astype(jnp.bfloat16).astype(jnp.float32)
    mixed_ref[...] = jnp.zeros_like(mixed_ref)
    for j in range(per_dev):
        def body(k, acc):
            s = slot_of_ref[partners_ref[j, k]]
            return acc + links_ref[j, k].astype(jnp.float32) * scaled_ref[pl.ds(s, 1), :]

        acc = jnp.zeros(links_ref.shape[2:], jnp.float32)
        for h in range(PIECES):
            if first_time:
                piece_copy(j, h).wait()
            acc = lax.fori_loop(h * piece, (h + 1) * piece, body, acc, unroll=8)
        mixed_ref[j : j + 1, :] = jnp.sum(acc.T, axis=0, keepdims=True)
    out_ref[...] = mixed_ref[:per_dev, :].astype(jnp.bfloat16)


def own_product(hit, products):
    return jnp.sum(jnp.where(hit, products, 0.0), axis=0, keepdims=True)


def side_by_side(rows_ref, table_ref):
    rank = rows_ref.shape[1]
    for q in range(FOLD):
        pads = [jnp.zeros((q * WIDE, rank), jnp.float32), rows_ref[...], jnp.zeros((LANES - q * WIDE - ROWS, rank), jnp.float32)]
        tall = jnp.concatenate([p for p in pads if p.shape[0]], axis=0)
        table_ref[q * rank : (q + 1) * rank, :] = tall.T.astype(jnp.bfloat16)


def both_kernel(
    devices, per_dev, slot_of_ref, mixed_ref, assign_ref, scores_ref, basis_hbm,
    first_ref, out_ref, cl_ref, rows_ref, sum_ref, slope_ref, table_ref,
    even_ref, odd_ref, even_left, odd_left, slots_ref, basis_sem,
):
    copies = basis_hbm.shape[0] // COPY

    def basis_copy(c):
        return slot_copy(basis_hbm, slots_ref, basis_sem, c)

    for c in range(SLOTS):
        basis_copy(c).start()
    near_clusters(devices, per_dev, slot_of_ref, cl_ref)
    near_rows(devices, per_dev, mixed_ref, rows_ref)
    side_by_side(rows_ref, table_ref)
    sum_ref[...] = jnp.zeros_like(sum_ref)
    sig = jax.nn.sigmoid(scores_ref[...])
    slope_ref[...] = sig * (1.0 - sig)
    cl = cl_ref[...]
    products_of = (even_ref, odd_ref)
    left_of = (even_left, odd_left)

    def multiply(c, p):
        c, p = c + p // PER_COPY, p % PER_COPY
        slot = lax.rem(c, SLOTS)
        lefts = []
        for b in range(TILE // (FOLD * LANES)):
            at = p * TILE + b * FOLD * LANES
            blocks = [slots_ref[slot, at + q * LANES : at + (q + 1) * LANES, :] for q in range(FOLD)]
            lefts.append(jnp.concatenate(blocks, axis=1))
        out = jnp.dot(jnp.concatenate(lefts, axis=0), table_ref[...], preferred_element_type=jnp.float32)
        for b in range(TILE // (FOLD * LANES)):
            turned = out[b * LANES : (b + 1) * LANES, :].T
            for q in range(FOLD):
                at = (b * FOLD + q) * LANES
                products_of[p % 2][:, at : at + LANES] = turned[q * WIDE : q * WIDE + ROWS, :]

    def select(t, side):
        for i in range(TILE // LANES):
            at = slice(i * LANES, (i + 1) * LANES)
            hit = assign_ref[row_at(t, i), :] == cl
            first = own_product(hit, products_of[side][:, at])
            first_ref[row_at(t, i), :] = first
            weighted = slope_ref[row_at(t, i), :] * first
            left_of[side][:, at] = jnp.where(hit, weighted, 0.0).astype(jnp.bfloat16)

    def add_up(c, p):
        block = slots_ref[lax.rem(c, SLOTS), p * TILE : (p + 1) * TILE, :]
        sum_ref[...] += jnp.dot(left_of[p % 2][...], block, preferred_element_type=jnp.float32)

    basis_copy(0).wait()
    multiply(0, 0)
    select(0, 0)
    multiply(0, 1)

    @pl.loop(0, copies - 1)
    def _(c):
        basis_copy(c + 1).wait()
        for p in range(PER_COPY):
            add_up(c, p)
            multiply(c, p + 2)
            select(c * PER_COPY + p + 1, (p + 1) % 2)

        @pl.when(c + SLOTS < copies)
        def _():
            basis_copy(c + SLOTS).start()

    for p in range(PER_COPY):
        add_up(copies - 1, p)
        if p + 2 < PER_COPY:
            multiply(copies - 1, p + 2)
        if p + 1 < PER_COPY:
            select((copies - 1) * PER_COPY + p + 1, (p + 1) % 2)
    put_sums(per_dev, sum_ref, out_ref)


def chip_clusters(devices, per_dev, slot_of_ref, cl_ref):
    clusters = devices * per_dev
    me = lax.axis_index("dev")
    core = lax.rem(me, 2)
    row = lax.broadcasted_iota(jnp.int32, (ROWS, clusters), 0)
    group = row // per_dev
    there = lax.rem(group, 2)
    owner = me - core + devices - 2 + (group - there) + jnp.where(there == core, 0, 1)
    slots = lax.rem(owner, devices) * per_dev + lax.rem(row, per_dev)
    number = lax.broadcasted_iota(jnp.int32, (ROWS, clusters), 1)
    hit = slot_of_ref[...] == slots
    found = jnp.sum(jnp.where(hit, number + 1, 0), axis=1, keepdims=True) - 1
    cl_ref[...] = jnp.broadcast_to(found, cl_ref.shape)


def last_kernel(
    devices, per_dev, slot_of_ref, behind_ref, own_ref, ahead_ref, assign_ref, first_ref, turned_ref,
    out_ref, cl_ref, even_ref, odd_ref,
):
    tiles = turned_ref.shape[1] // TILE
    chip_clusters(devices, per_dev, slot_of_ref, cl_ref)
    around = [ref[...].astype(jnp.float32) for ref in (behind_ref, own_ref, ahead_ref)]
    rows = jnp.concatenate(around, axis=0).astype(jnp.bfloat16)
    cl = cl_ref[...]
    products_of = (even_ref, odd_ref)

    def multiply(t, side):
        products_of[side][...] = jnp.dot(rows, turned_ref[:, tile_at(t)], preferred_element_type=jnp.float32)

    def select(t, side):
        for i in range(TILE // LANES):
            hit = assign_ref[row_at(t, i), :] == cl
            second = own_product(hit, products_of[side][:, i * LANES : (i + 1) * LANES])
            out_ref[row_at(t, i), :] = second + ridge * first_ref[row_at(t, i), :]

    multiply(0, 0)

    @pl.loop(0, tiles // BODY)
    def _(c):
        for p in range(BODY):
            t = c * BODY + p
            multiply(lax.rem(t + 1, tiles), (p + 1) % 2)
            select(t, p % 2)


def shards(basis_rows, vector, scores, assign, slot_of, partners, link_blocks):
    devices = lax.axis_size("dev")
    clusters = slot_of.shape[0]
    per_dev, n_links, rank, _ = link_blocks.shape
    samples = assign.shape[0]
    norm = 1.0 / math.sqrt(S_DEV // CL_DEV)
    high = samples // LANES
    f32, bf16 = jnp.float32, jnp.bfloat16

    vector = vector.reshape(high, LANES)
    scores = scores.reshape(high, LANES)
    assign = assign.reshape(high, LANES)
    slot_row = slot_of.reshape(1, clusters)

    far = lambda x: pltpu.with_memory_space_constraint(x, pltpu.HBM)
    close = lambda x: pltpu.with_memory_space_constraint(x, pltpu.VMEM)
    vmem = pl.BlockSpec(memory_space=pltpu.VMEM)
    smem = pl.BlockSpec(memory_space=pltpu.SMEM)
    hbm = pl.BlockSpec(memory_space=pltpu.HBM)
    coef_shape = jax.ShapeDtypeStruct((per_dev, NEAR * rank), bf16)
    params = pltpu.CompilerParams(vmem_limit_bytes=10 * 1024 * 1024)

    coef1, turned_v, assign_v = pl.pallas_call(
        functools.partial(coef_kernel, devices, per_dev),
        in_specs=[hbm] * 4,
        out_specs=[vmem] * 3,
        out_shape=[
            coef_shape,
            pltpu.VMEM((rank, samples), bf16),
            pltpu.VMEM((high, LANES), jnp.int32),
        ],
        scratch_shapes=[
            pltpu.VMEM((1, clusters), jnp.int32),
            pltpu.VMEM((ROWS, LANES), jnp.int32),
            pltpu.VMEM((ROWS, rank), f32),
            pltpu.VMEM((high, LANES), bf16),
            pltpu.VMEM((high, LANES), f32),
            pltpu.VMEM((SLOTS, COPY, rank), bf16),
            pltpu.SemaphoreType.DMA((3,)),
            pltpu.SemaphoreType.DMA((SLOTS,)),
        ],
        compiler_params=params,
        name="coef_pass",
    )(far(slot_row), far(assign), far(vector), far(basis_rows))

    def to_all(block):
        copies = jnp.broadcast_to(block[None], (devices,) + block.shape)
        return lax.all_to_all(copies, "dev", 0, 0, tiled=True)

    def from_device(block, source):
        return lax.ppermute(block, "dev", [(source(i) % devices, i) for i in range(devices)])

    def to_chips(mixed):
        own = jnp.concatenate([mixed, from_device(mixed, lambda i: i ^ 1)], axis=0)
        return from_device(own, lambda i: i - 2), own, from_device(own, lambda i: i + 2)

    def mix(coef, links, first_time):
        out = pl.pallas_call(
            functools.partial(link_kernel, norm, devices, per_dev, first_time),
            in_specs=[smem, smem, vmem, hbm if first_time else vmem],
            out_specs=[vmem, vmem] if first_time else [vmem],
            out_shape=[jax.ShapeDtypeStruct((per_dev, rank), bf16)] + [pltpu.VMEM(links.shape, bf16)] * first_time,
            scratch_shapes=[
                pltpu.VMEM((clusters, rank), f32),
                pltpu.VMEM((8, rank), f32),
            ]
            + [pltpu.SemaphoreType.DMA((PIECES * per_dev,))] * first_time,
            compiler_params=params,
            name="link_product",
        )(slot_of, partners, to_all(coef), links)
        return out

    mixed1, links_v = mix(coef1, far(link_blocks), True)
    first, coef2 = pl.pallas_call(
        functools.partial(both_kernel, devices, per_dev),
        in_specs=[vmem] * 4 + [hbm],
        out_specs=[vmem, vmem],
        out_shape=[pltpu.VMEM((high, LANES), f32), coef_shape],
        scratch_shapes=[
            pltpu.VMEM((ROWS, LANES), jnp.int32),
            pltpu.VMEM((ROWS, rank), f32),
            pltpu.VMEM((ROWS, rank), f32),
            pltpu.VMEM((high, LANES), f32),
            pltpu.VMEM((FOLD * rank, LANES), bf16),
            pltpu.VMEM((ROWS, TILE), f32),
            pltpu.VMEM((ROWS, TILE), f32),
            pltpu.VMEM((ROWS, TILE), bf16),
            pltpu.VMEM((ROWS, TILE), bf16),
            pltpu.VMEM((SLOTS, COPY, rank), bf16),
            pltpu.SemaphoreType.DMA((SLOTS,)),
        ],
        compiler_params=params,
        name="first_and_coef_pass",
    )(slot_row, to_all(mixed1), close(assign_v), scores, far(basis_rows))
    (mixed2,) = mix(coef2, close(links_v), False)

    out = pl.pallas_call(
        functools.partial(last_kernel, devices, per_dev),
        in_specs=[vmem] * 7,
        out_specs=vmem,
        out_shape=jax.ShapeDtypeStruct((high, LANES), f32),
        scratch_shapes=[
            pltpu.VMEM((ROWS, LANES), jnp.int32),
            pltpu.VMEM((ROWS, TILE), f32),
            pltpu.VMEM((ROWS, TILE), f32),
        ],
        compiler_params=params,
        name="last_pass",
    )(slot_row, *to_chips(mixed2), close(assign_v), close(first), close(turned_v))
    return out.reshape(samples)


def solution(mesh):
    in_specs = (
        P(("groups", "dev"), None),
        P(("groups", "dev")),
        P(("groups", "dev")),
        P(("groups", "dev")),
        P("groups"),
        P(("groups", "dev"), None),
        P(("groups", "dev"), None, None, None),
    )
    out_specs = P(("groups", "dev"))
    return jax.shard_map(shards, mesh=mesh, in_specs=in_specs, out_specs=out_specs, check_vma=False)
```

```python
import functools
import math

import jax
import jax.numpy as jnp
from jax import lax
from jax.experimental import pallas as pl
from jax.experimental.pallas import tpu as pltpu
from jax.sharding import PartitionSpec as P

REACH = 2
NEAR = 2 * REACH + 1
CL_DEV = 4
S_DEV = 65536
LANES = 128
ROWS = 24

COPY = 8192
TILE = 2048
PER_COPY = COPY // TILE
SLOTS = 3
BODY = 16
HALF = TILE // 2
PAIR = 64
PIECES = 4

ridge = 0.5


def near_clusters(devices, per_dev, slot_of_ref, cl_ref):
    clusters = devices * per_dev
    me = lax.axis_index("dev")
    near = lax.broadcasted_iota(jnp.int32, (ROWS, clusters), 0)
    slots = (me + devices - REACH) * per_dev + near
    slots = lax.rem(slots, clusters)
    number = lax.broadcasted_iota(jnp.int32, (ROWS, clusters), 1)
    hit = (slot_of_ref[...] == slots) & (near < NEAR * per_dev)
    found = jnp.sum(jnp.where(hit, number + 1, 0), axis=1, keepdims=True) - 1
    cl_ref[...] = jnp.broadcast_to(found, cl_ref.shape)


def near_rows(per_dev, chips, rows_ref):
    even_core = lax.rem(lax.axis_index("dev"), 2) == 0
    chips = [chip[...].astype(jnp.float32) for chip in chips]
    rank = rows_ref.shape[1] // 2
    rows_ref[...] = jnp.zeros_like(rows_ref)
    for g in range(NEAR):
        if g % 2 == 0:
            rows = chips[g // 2][:per_dev, :]
        else:
            rows = jnp.where(even_core, chips[g // 2][per_dev:, :], chips[g // 2 + 1][per_dev:, :])
        for h in range(2):
            at = h * (PAIR // 2) + g * per_dev
            rows_ref[at : at + per_dev, h * rank : (h + 1) * rank] = rows


def first_product(rows, turned_ref, t, out_ref):
    at = [pl.ds(pl.multiple_of(t * TILE + h * HALF, HALF), HALF) for h in range(2)]
    both = jnp.concatenate([turned_ref[:, at[0]], turned_ref[:, at[1]]], axis=0)
    out = jnp.dot(rows, both, preferred_element_type=jnp.float32)
    for h in range(2):
        out_ref[:, h * HALF : (h + 1) * HALF] = out[h * (PAIR // 2) : h * (PAIR // 2) + ROWS, :]


def second_product(left, block):
    rank = block.shape[1]
    both = jnp.concatenate([block[:HALF, :], block[HALF:, :]], axis=1)
    out = jnp.dot(left, both, preferred_element_type=jnp.float32)
    return out[:ROWS, :rank] + out[PAIR // 2 : PAIR // 2 + ROWS, rank:]


def half_left(hit, x):
    pad = jnp.zeros((PAIR // 2 - ROWS, LANES), jnp.float32)
    return jnp.concatenate([jnp.where(hit, x, 0.0), pad], axis=0).astype(jnp.bfloat16)


def put_sums(per_dev, sum_ref, out_ref):
    for g in range(NEAR):
        out_ref[:, g * LANES : (g + 1) * LANES] = sum_ref[g * per_dev : (g + 1) * per_dev, :].astype(jnp.bfloat16)


def slot_copy(basis_hbm, slots_ref, sem, c):
    slot = lax.rem(c, SLOTS)
    rows = pl.ds(pl.multiple_of(c * COPY, COPY), COPY)
    return pltpu.make_async_copy(basis_hbm.at[rows, :], slots_ref.at[slot], sem.at[slot])


def tile_at(t):
    return pl.ds(pl.multiple_of(t * TILE, TILE), TILE)


def row_at(t, i):
    return pl.ds(t * (TILE // LANES) + i, 1)


def coef_kernel(
    devices, per_dev, slot_of_hbm, assign_hbm, vector_hbm, basis_hbm,
    out_ref, turned_ref, assign_ref,
    slot_of_ref, cl_ref, sum_ref, vector_ref, x_ref, slots_ref, small_sem, basis_sem,
):
    copies = basis_hbm.shape[0] // COPY

    def basis_copy(c):
        return slot_copy(basis_hbm, slots_ref, basis_sem, c)

    slot_of_copy = pltpu.make_async_copy(slot_of_hbm, slot_of_ref, small_sem.at[2])
    assign_copy = pltpu.make_async_copy(assign_hbm, assign_ref, small_sem.at[0])
    vector_copy = pltpu.make_async_copy(vector_hbm, vector_ref, small_sem.at[1])
    slot_of_copy.start()
    assign_copy.start()
    vector_copy.start()
    for c in range(SLOTS):
        basis_copy(c).start()
    slot_of_copy.wait()
    near_clusters(devices, per_dev, slot_of_ref, cl_ref)
    sum_ref[...] = jnp.zeros_like(sum_ref)
    assign_copy.wait()
    vector_copy.wait()
    x_ref[...] = vector_ref[...].astype(jnp.float32)
    cl = cl_ref[...]

    @pl.loop(0, copies)
    def _(c):
        basis_copy(c).wait()
        total = sum_ref[...]
        for p in range(PER_COPY):
            t = c * PER_COPY + p
            parts = [half_left(assign_ref[row_at(t, i), :] == cl, x_ref[row_at(t, i), :]) for i in range(TILE // LANES)]
            half = len(parts) // 2
            left = jnp.concatenate([jnp.concatenate(parts[:half], axis=1), jnp.concatenate(parts[half:], axis=1)], axis=0)
            block = slots_ref[lax.rem(c, SLOTS), p * TILE : (p + 1) * TILE, :]
            turned_ref[:, tile_at(t)] = block.T
            total += second_product(left, block)
        sum_ref[...] = total

        @pl.when(c + SLOTS < copies)
        def _():
            basis_copy(c + SLOTS).start()

    put_sums(per_dev, sum_ref, out_ref)


def link_kernel(norm, devices, per_dev, first_time, slot_of_ref, partners_ref, parts_ref, *refs):
    if first_time:
        links_hbm, out_ref, links_ref, scaled_ref, mixed_ref, links_sem = refs
    else:
        links_ref, out_ref, scaled_ref, mixed_ref = refs
    n_links = links_ref.shape[1]
    piece = n_links // PIECES

    def piece_copy(j, h):
        ks = pl.ds(h * piece, piece)
        return pltpu.make_async_copy(links_hbm.at[j, ks], links_ref.at[j, ks], links_sem.at[PIECES * j + h])

    if first_time:
        for j in range(per_dev):
            for h in range(PIECES):
                piece_copy(j, h).start()
    for owner in range(devices):
        coef = parts_ref[(owner + REACH) % devices, :, :LANES].astype(jnp.float32)
        for g in range(1, NEAR):
            coef += parts_ref[(owner + REACH - g) % devices, :, g * LANES : (g + 1) * LANES].astype(jnp.float32)
        scaled_ref[owner * per_dev : (owner + 1) * per_dev, :] = (coef * norm).astype(jnp.bfloat16).astype(jnp.float32)
    mixed_ref[...] = jnp.zeros_like(mixed_ref)
    for j in range(per_dev):
        def body(k, acc):
            s = slot_of_ref[partners_ref[j, k]]
            return acc + links_ref[j, k].astype(jnp.float32) * scaled_ref[pl.ds(s, 1), :]

        acc = jnp.zeros(links_ref.shape[2:], jnp.float32)
        for h in range(PIECES):
            if first_time:
                piece_copy(j, h).wait()
            acc = lax.fori_loop(h * piece, (h + 1) * piece, body, acc, unroll=8)
        mixed_ref[j : j + 1, :] = jnp.sum(acc.T, axis=0, keepdims=True)
    out_ref[...] = mixed_ref[:per_dev, :].astype(jnp.bfloat16)


def own_product(hit, products):
    return jnp.sum(jnp.where(hit, products, 0.0), axis=0, keepdims=True)


def both_kernel(
    devices, per_dev, slot_of_ref, behind_ref, own_ref, ahead_ref, assign_ref, scores_ref, turned_ref, basis_hbm,
    first_ref, out_ref, cl_ref, rows_ref, sum_ref, slope_ref, even_ref, odd_ref, even_left, odd_left, slots_ref, basis_sem,
):
    tiles = turned_ref.shape[1] // TILE
    copies = tiles // PER_COPY

    def basis_copy(c):
        return slot_copy(basis_hbm, slots_ref, basis_sem, c)

    for c in range(SLOTS):
        basis_copy(c).start()
    near_clusters(devices, per_dev, slot_of_ref, cl_ref)
    near_rows(per_dev, (behind_ref, own_ref, ahead_ref), rows_ref)
    sum_ref[...] = jnp.zeros_like(sum_ref)
    sig = jax.nn.sigmoid(scores_ref[...])
    slope_ref[...] = sig * (1.0 - sig)
    cl = cl_ref[...]
    rows = rows_ref[...].astype(jnp.bfloat16)
    products_of = (even_ref, odd_ref)
    left_of = (even_left, odd_left)

    def multiply(t, side):
        first_product(rows, turned_ref, t, products_of[side])

    def select(t, side):
        for i in range(TILE // LANES):
            at = slice(i * LANES, (i + 1) * LANES)
            hit = assign_ref[row_at(t, i), :] == cl
            first = own_product(hit, products_of[side][:, at])
            first_ref[row_at(t, i), :] = first
            weighted = slope_ref[row_at(t, i), :] * first
            half, col = divmod(i * LANES, HALF)
            left_of[side][half * (PAIR // 2) : (half + 1) * (PAIR // 2), col : col + LANES] = half_left(hit, weighted)

    def add_up(c, p):
        block = slots_ref[lax.rem(c, SLOTS), p * TILE : (p + 1) * TILE, :]
        sum_ref[...] += second_product(left_of[p % 2][...], block)

    multiply(0, 0)
    select(0, 0)
    multiply(1, 1)

    @pl.loop(0, copies - 1)
    def _(c):
        basis_copy(c).wait()
        for p in range(PER_COPY):
            t = c * PER_COPY + p
            add_up(c, p)
            multiply(t + 2, p % 2)
            select(t + 1, (p + 1) % 2)

        @pl.when(c + SLOTS < copies)
        def _():
            basis_copy(c + SLOTS).start()

    basis_copy(copies - 1).wait()
    for p in range(PER_COPY):
        t = (copies - 1) * PER_COPY + p
        add_up(copies - 1, p)
        if p + 2 < PER_COPY:
            multiply(t + 2, p % 2)
        if p + 1 < PER_COPY:
            select(t + 1, (p + 1) % 2)
    put_sums(per_dev, sum_ref, out_ref)


def last_kernel(
    devices, per_dev, slot_of_ref, behind_ref, own_ref, ahead_ref, assign_ref, first_ref, turned_ref, out_ref, cl_ref, rows_ref, even_ref, odd_ref
):
    tiles = turned_ref.shape[1] // TILE
    near_clusters(devices, per_dev, slot_of_ref, cl_ref)
    near_rows(per_dev, (behind_ref, own_ref, ahead_ref), rows_ref)
    cl = cl_ref[...]
    rows = rows_ref[...].astype(jnp.bfloat16)
    products_of = (even_ref, odd_ref)

    def multiply(t, side):
        first_product(rows, turned_ref, t, products_of[side])

    def select(t, side):
        for i in range(TILE // LANES):
            hit = assign_ref[row_at(t, i), :] == cl
            second = own_product(hit, products_of[side][:, i * LANES : (i + 1) * LANES])
            out_ref[row_at(t, i), :] = second + ridge * first_ref[row_at(t, i), :]

    multiply(0, 0)

    @pl.loop(0, tiles // BODY)
    def _(c):
        for p in range(BODY):
            t = c * BODY + p
            multiply(lax.rem(t + 1, tiles), (p + 1) % 2)
            select(t, p % 2)


def shards(basis_rows, vector, scores, assign, slot_of, partners, link_blocks):
    devices = lax.axis_size("dev")
    clusters = slot_of.shape[0]
    per_dev, n_links, rank, _ = link_blocks.shape
    samples = assign.shape[0]
    norm = 1.0 / math.sqrt(S_DEV // CL_DEV)
    high = samples // LANES
    f32, bf16 = jnp.float32, jnp.bfloat16

    vector = vector.reshape(high, LANES)
    scores = scores.reshape(high, LANES)
    assign = assign.reshape(high, LANES)
    slot_row = slot_of.reshape(1, clusters)

    far = lambda x: pltpu.with_memory_space_constraint(x, pltpu.HBM)
    close = lambda x: pltpu.with_memory_space_constraint(x, pltpu.VMEM)
    vmem = pl.BlockSpec(memory_space=pltpu.VMEM)
    smem = pl.BlockSpec(memory_space=pltpu.SMEM)
    hbm = pl.BlockSpec(memory_space=pltpu.HBM)
    coef_shape = jax.ShapeDtypeStruct((per_dev, NEAR * rank), bf16)
    params = pltpu.CompilerParams(vmem_limit_bytes=10 * 1024 * 1024)

    coef1, turned_v, assign_v = pl.pallas_call(
        functools.partial(coef_kernel, devices, per_dev),
        in_specs=[hbm] * 4,
        out_specs=[vmem] * 3,
        out_shape=[
            coef_shape,
            pltpu.VMEM((rank, samples), bf16),
            pltpu.VMEM((high, LANES), jnp.int32),
        ],
        scratch_shapes=[
            pltpu.VMEM((1, clusters), jnp.int32),
            pltpu.VMEM((ROWS, LANES), jnp.int32),
            pltpu.VMEM((ROWS, rank), f32),
            pltpu.VMEM((high, LANES), bf16),
            pltpu.VMEM((high, LANES), f32),
            pltpu.VMEM((SLOTS, COPY, rank), bf16),
            pltpu.SemaphoreType.DMA((3,)),
            pltpu.SemaphoreType.DMA((SLOTS,)),
        ],
        compiler_params=params,
        name="coef_pass",
    )(far(slot_row), far(assign), far(vector), far(basis_rows))

    def to_all(block):
        copies = jnp.broadcast_to(block[None], (devices,) + block.shape)
        return lax.all_to_all(copies, "dev", 0, 0, tiled=True)

    def from_device(block, source):
        return lax.ppermute(block, "dev", [(source(i) % devices, i) for i in range(devices)])

    def to_chips(mixed):
        own = jnp.concatenate([mixed, from_device(mixed, lambda i: i ^ 1)], axis=0)
        return from_device(own, lambda i: i - 2), own, from_device(own, lambda i: i + 2)

    def mix(coef, links, first_time):
        out = pl.pallas_call(
            functools.partial(link_kernel, norm, devices, per_dev, first_time),
            in_specs=[smem, smem, vmem, hbm if first_time else vmem],
            out_specs=[vmem, vmem] if first_time else [vmem],
            out_shape=[jax.ShapeDtypeStruct((per_dev, rank), bf16)] + [pltpu.VMEM(links.shape, bf16)] * first_time,
            scratch_shapes=[
                pltpu.VMEM((clusters, rank), f32),
                pltpu.VMEM((8, rank), f32),
            ]
            + [pltpu.SemaphoreType.DMA((PIECES * per_dev,))] * first_time,
            compiler_params=params,
            name="link_product",
        )(slot_of, partners, to_all(coef), links)
        return out

    mixed1, links_v = mix(coef1, far(link_blocks), True)
    first, coef2 = pl.pallas_call(
        functools.partial(both_kernel, devices, per_dev),
        in_specs=[vmem] * 7 + [hbm],
        out_specs=[vmem, vmem],
        out_shape=[pltpu.VMEM((high, LANES), f32), coef_shape],
        scratch_shapes=[
            pltpu.VMEM((ROWS, LANES), jnp.int32),
            pltpu.VMEM((PAIR, 2 * rank), f32),
            pltpu.VMEM((ROWS, rank), f32),
            pltpu.VMEM((high, LANES), f32),
            pltpu.VMEM((ROWS, TILE), f32),
            pltpu.VMEM((ROWS, TILE), f32),
            pltpu.VMEM((PAIR, HALF), bf16),
            pltpu.VMEM((PAIR, HALF), bf16),
            pltpu.VMEM((SLOTS, COPY, rank), bf16),
            pltpu.SemaphoreType.DMA((SLOTS,)),
        ],
        compiler_params=params,
        name="first_and_coef_pass",
    )(slot_row, *to_chips(mixed1), close(assign_v), scores, close(turned_v), far(basis_rows))
    (mixed2,) = mix(coef2, close(links_v), False)

    out = pl.pallas_call(
        functools.partial(last_kernel, devices, per_dev),
        in_specs=[vmem] * 7,
        out_specs=vmem,
        out_shape=jax.ShapeDtypeStruct((high, LANES), f32),
        scratch_shapes=[
            pltpu.VMEM((ROWS, LANES), jnp.int32),
            pltpu.VMEM((PAIR, 2 * rank), f32),
            pltpu.VMEM((ROWS, TILE), f32),
            pltpu.VMEM((ROWS, TILE), f32),
        ],
        compiler_params=params,
        name="last_pass",
    )(slot_row, *to_chips(mixed2), close(assign_v), close(first), close(turned_v))
    return out.reshape(samples)


def solution(mesh):
    in_specs = (
        P(("groups", "dev"), None),
        P(("groups", "dev")),
        P(("groups", "dev")),
        P(("groups", "dev")),
        P("groups"),
        P(("groups", "dev"), None),
        P(("groups", "dev"), None, None, None),
    )
    out_specs = P(("groups", "dev"))
    return jax.shard_map(shards, mesh=mesh, in_specs=in_specs, out_specs=out_specs, check_vma=False)
```

```python
import functools
import math

import jax
import jax.numpy as jnp
from jax import lax
from jax.experimental import pallas as pl
from jax.experimental.pallas import tpu as pltpu
from jax.sharding import PartitionSpec as P

REACH = 2
NEAR = 2 * REACH + 1
CL_DEV = 4
S_DEV = 65536
LANES = 128
ROWS = 24

COPY = 8192
TILE = 2048
PER_COPY = COPY // TILE
SLOTS = 3
BODY = 16
PIECE = 512
GROUP = 8

ridge = 0.5


def near_clusters(devices, per_dev, slot_of_ref, cl_ref):
    clusters = devices * per_dev
    me = lax.axis_index("dev")
    near = lax.broadcasted_iota(jnp.int32, (ROWS, clusters), 0)
    slots = (me + devices - REACH) * per_dev + near
    slots = lax.rem(slots, clusters)
    number = lax.broadcasted_iota(jnp.int32, (ROWS, clusters), 1)
    hit = (slot_of_ref[...] == slots) & (near < NEAR * per_dev)
    found = jnp.sum(jnp.where(hit, number + 1, 0), axis=1, keepdims=True) - 1
    cl_ref[...] = jnp.broadcast_to(found, cl_ref.shape)


def near_rows(per_dev, chips, rows_ref):
    even_core = lax.rem(lax.axis_index("dev"), 2) == 0
    chips = [chip[...].astype(jnp.float32) for chip in chips]
    rows_ref[...] = jnp.zeros_like(rows_ref)
    for g in range(NEAR):
        if g % 2 == 0:
            rows = chips[g // 2][:per_dev, :]
        else:
            rows = jnp.where(even_core, chips[g // 2][per_dev:, :], chips[g // 2 + 1][per_dev:, :])
        rows_ref[g * per_dev : (g + 1) * per_dev, :] = rows


def put_sums(per_dev, sum_ref, out_ref):
    for g in range(NEAR):
        out_ref[:, g * LANES : (g + 1) * LANES] = sum_ref[g * per_dev : (g + 1) * per_dev, :].astype(jnp.bfloat16)


def spread_sums(devices, per_dev, sum_ref, out_ref):
    me = lax.axis_index("dev")
    out_ref[...] = jnp.zeros_like(out_ref)
    for g in range(NEAR):
        owner = lax.rem(me + devices + g - REACH, devices)
        out_ref[owner] = sum_ref[g * per_dev : (g + 1) * per_dev, :]


def slot_copy(basis_hbm, slots_ref, sem, c):
    slot = lax.rem(c, SLOTS)
    rows = pl.ds(pl.multiple_of(c * COPY, COPY), COPY)
    return pltpu.make_async_copy(basis_hbm.at[rows, :], slots_ref.at[slot], sem.at[slot])


def tile_at(t):
    return pl.ds(pl.multiple_of(t * TILE, TILE), TILE)


def row_at(t, i):
    return pl.ds(t * (TILE // LANES) + i, 1)


def coef_kernel(
    devices, per_dev, slot_of_hbm, assign_hbm, vector_hbm, basis_hbm,
    out_ref, turned_ref, assign_ref,
    slot_of_ref, cl_ref, sum_ref, vector_ref, x_ref, slots_ref, small_sem, basis_sem,
):
    copies = basis_hbm.shape[0] // COPY

    def basis_copy(c):
        return slot_copy(basis_hbm, slots_ref, basis_sem, c)

    slot_of_copy = pltpu.make_async_copy(slot_of_hbm, slot_of_ref, small_sem.at[2])
    assign_copy = pltpu.make_async_copy(assign_hbm, assign_ref, small_sem.at[0])
    vector_copy = pltpu.make_async_copy(vector_hbm, vector_ref, small_sem.at[1])
    slot_of_copy.start()
    assign_copy.start()
    vector_copy.start()
    for c in range(SLOTS):
        basis_copy(c).start()
    slot_of_copy.wait()
    near_clusters(devices, per_dev, slot_of_ref, cl_ref)
    sum_ref[...] = jnp.zeros_like(sum_ref)
    assign_copy.wait()
    vector_copy.wait()
    x_ref[...] = vector_ref[...].astype(jnp.float32)
    cl = cl_ref[...]

    @pl.loop(0, copies)
    def _(c):
        basis_copy(c).wait()
        total = sum_ref[...]
        for p in range(PER_COPY):
            t = c * PER_COPY + p
            parts = []
            for i in range(TILE // LANES):
                hit = assign_ref[row_at(t, i), :] == cl
                parts.append(jnp.where(hit, x_ref[row_at(t, i), :], 0.0).astype(jnp.bfloat16))
            left = jnp.concatenate(parts, axis=1)
            block = slots_ref[lax.rem(c, SLOTS), p * TILE : (p + 1) * TILE, :]
            turned_ref[:, tile_at(t)] = block.T
            total += jnp.dot(left, block, preferred_element_type=jnp.float32)
        sum_ref[...] = total

        @pl.when(c + SLOTS < copies)
        def _():
            basis_copy(c + SLOTS).start()

    put_sums(per_dev, sum_ref, out_ref)


def link_kernel(norm, devices, per_dev, first_time, slot_of_ref, partners_ref, coef_ref, *refs):
    if first_time:
        links_hbm, out_ref, links_ref, scaled_ref, picked_ref, mixed_ref, links_sem = refs
    else:
        links_ref, out_ref, scaled_ref, picked_ref, mixed_ref = refs
    n_links, rank = links_ref.shape[1:3]
    step = 2 * GROUP

    def piece_copy(j, k):
        ks = pl.ds(k, step)
        return pltpu.make_async_copy(links_hbm.at[j, ks], links_ref.at[j, ks], links_sem.at[(j * n_links + k) // step])

    if first_time:
        for j in range(per_dev):
            for k in range(0, n_links, step):
                piece_copy(j, k).start()
        for owner in range(devices):
            coef = coef_ref[(owner + REACH) % devices, :, :LANES].astype(jnp.float32)
            for g in range(1, NEAR):
                coef += coef_ref[(owner + REACH - g) % devices, :, g * LANES : (g + 1) * LANES].astype(jnp.float32)
            scaled_ref[owner * per_dev : (owner + 1) * per_dev, :] = (coef * norm).astype(jnp.bfloat16).astype(jnp.float32)
    else:
        scaled_ref[...] = (coef_ref[...] * norm).astype(jnp.bfloat16).astype(jnp.float32)

    def partner(j, k):
        return scaled_ref[pl.ds(slot_of_ref[partners_ref[j, k]], 1), :]

    row = lax.broadcasted_iota(jnp.int32, (GROUP, rank), 0)
    mixed_ref[...] = jnp.zeros_like(mixed_ref)
    for j in range(per_dev):
        acc = jnp.zeros((rank, rank), jnp.float32)
        few = jnp.zeros((GROUP, rank), jnp.float32)
        for k in range(0, n_links, step):
            if first_time:
                piece_copy(j, k).wait()
            at = (j * n_links + k) // 2
            for u in range(GROUP):
                picked_ref[at + u : at + u + 1, :] = partner(j, k + GROUP + u)
            blocks = links_ref[j, k + GROUP : k + step].reshape(GROUP * rank, rank)
            picked = picked_ref[at : at + GROUP, :].astype(jnp.bfloat16)
            products = lax.dot_general(picked, blocks, (((1,), (1,)), ((), ())), preferred_element_type=jnp.float32)
            for u in range(GROUP):
                acc += links_ref[j, k + u].astype(jnp.float32) * partner(j, k + u)
            for u in range(GROUP):
                few += jnp.where(row == u, products[:, u * rank : (u + 1) * rank], 0.0)
        mixed_ref[j : j + 1, :] = jnp.sum(acc.T, axis=0, keepdims=True) + jnp.sum(few, axis=0, keepdims=True)
    out_ref[...] = mixed_ref[:per_dev, :].astype(jnp.bfloat16)


def own_product(hit, products):
    return jnp.sum(jnp.where(hit, products, 0.0), axis=0, keepdims=True)


def both_kernel(
    devices, per_dev, slot_of_ref, behind_ref, own_ref, ahead_ref, assign_ref, scores_ref, turned_ref, basis_hbm,
    first_ref, out_ref, cl_ref, rows_ref, sum_ref, slope_ref, even_left, odd_left, slots_ref, basis_sem,
):
    tiles = turned_ref.shape[1] // TILE
    copies = tiles // PER_COPY

    def basis_copy(c):
        return slot_copy(basis_hbm, slots_ref, basis_sem, c)

    for c in range(SLOTS):
        basis_copy(c).start()
    near_clusters(devices, per_dev, slot_of_ref, cl_ref)
    near_rows(per_dev, (behind_ref, own_ref, ahead_ref), rows_ref)
    sum_ref[...] = jnp.zeros_like(sum_ref)
    sig = jax.nn.sigmoid(scores_ref[...])
    slope_ref[...] = sig * (1.0 - sig)
    cl = cl_ref[...]
    rows = rows_ref[...].astype(jnp.bfloat16)
    left_of = (even_left, odd_left)

    def select(t, side):
        for piece in range(TILE // PIECE):
            at = pl.ds(pl.multiple_of(t * TILE + piece * PIECE, PIECE), PIECE)
            products = jnp.dot(rows, turned_ref[:, at], preferred_element_type=jnp.float32)
            for k in range(PIECE // LANES):
                i = piece * (PIECE // LANES) + k
                hit = assign_ref[row_at(t, i), :] == cl
                first = own_product(hit, products[:, k * LANES : (k + 1) * LANES])
                first_ref[row_at(t, i), :] = first
                weighted = slope_ref[row_at(t, i), :] * first
                left_of[side][:, i * LANES : (i + 1) * LANES] = jnp.where(hit, weighted, 0.0).astype(jnp.bfloat16)

    def add_up(c, p):
        block = slots_ref[lax.rem(c, SLOTS), p * TILE : (p + 1) * TILE, :]
        sum_ref[...] += jnp.dot(left_of[p % 2][...], block, preferred_element_type=jnp.float32)

    select(0, 0)

    @pl.loop(0, copies - 1)
    def _(c):
        basis_copy(c).wait()
        for p in range(PER_COPY):
            add_up(c, p)
            select(c * PER_COPY + p + 1, (p + 1) % 2)

        @pl.when(c + SLOTS < copies)
        def _():
            basis_copy(c + SLOTS).start()

    basis_copy(copies - 1).wait()
    for p in range(PER_COPY):
        add_up(copies - 1, p)
        if p + 1 < PER_COPY:
            select((copies - 1) * PER_COPY + p + 1, (p + 1) % 2)
    spread_sums(devices, per_dev, sum_ref, out_ref)


def last_kernel(
    devices, per_dev, slot_of_ref, behind_ref, own_ref, ahead_ref, assign_ref, first_ref, turned_ref, out_ref, cl_ref, rows_ref
):
    near_clusters(devices, per_dev, slot_of_ref, cl_ref)
    near_rows(per_dev, (behind_ref, own_ref, ahead_ref), rows_ref)
    cl = cl_ref[...]
    rows = rows_ref[...].astype(jnp.bfloat16)

    @pl.loop(0, turned_ref.shape[1] // (BODY * TILE))
    def _(c):
        for piece in range(BODY * TILE // PIECE):
            at = pl.ds(pl.multiple_of(c * (BODY * TILE) + piece * PIECE, PIECE), PIECE)
            products = jnp.dot(rows, turned_ref[:, at], preferred_element_type=jnp.float32)
            for k in range(PIECE // LANES):
                row = row_at(c * BODY, piece * (PIECE // LANES) + k)
                hit = assign_ref[row, :] == cl
                second = own_product(hit, products[:, k * LANES : (k + 1) * LANES])
                out_ref[row, :] = second + ridge * first_ref[row, :]


def shards(basis_rows, vector, scores, assign, slot_of, partners, link_blocks):
    devices = lax.axis_size("dev")
    clusters = slot_of.shape[0]
    per_dev, n_links, rank, _ = link_blocks.shape
    samples = assign.shape[0]
    norm = 1.0 / math.sqrt(S_DEV // CL_DEV)
    high = samples // LANES
    f32, bf16 = jnp.float32, jnp.bfloat16

    vector = vector.reshape(high, LANES)
    scores = scores.reshape(high, LANES)
    assign = assign.reshape(high, LANES)
    slot_row = slot_of.reshape(1, clusters)

    far = lambda x: pltpu.with_memory_space_constraint(x, pltpu.HBM)
    close = lambda x: pltpu.with_memory_space_constraint(x, pltpu.VMEM)
    vmem = pl.BlockSpec(memory_space=pltpu.VMEM)
    smem = pl.BlockSpec(memory_space=pltpu.SMEM)
    hbm = pl.BlockSpec(memory_space=pltpu.HBM)
    coef_shape = jax.ShapeDtypeStruct((per_dev, NEAR * rank), bf16)
    params = pltpu.CompilerParams(vmem_limit_bytes=10 * 1024 * 1024)

    coef1, turned_v, assign_v = pl.pallas_call(
        functools.partial(coef_kernel, devices, per_dev),
        in_specs=[hbm] * 4,
        out_specs=[vmem] * 3,
        out_shape=[
            coef_shape,
            pltpu.VMEM((rank, samples), bf16),
            pltpu.VMEM((high, LANES), jnp.int32),
        ],
        scratch_shapes=[
            pltpu.VMEM((1, clusters), jnp.int32),
            pltpu.VMEM((ROWS, LANES), jnp.int32),
            pltpu.VMEM((ROWS, rank), f32),
            pltpu.VMEM((high, LANES), bf16),
            pltpu.VMEM((high, LANES), f32),
            pltpu.VMEM((SLOTS, COPY, rank), bf16),
            pltpu.SemaphoreType.DMA((3,)),
            pltpu.SemaphoreType.DMA((SLOTS,)),
        ],
        compiler_params=params,
        name="coef_pass",
    )(far(slot_row), far(assign), far(vector), far(basis_rows))

    def to_all(block):
        copies = jnp.broadcast_to(block[None], (devices,) + block.shape)
        return lax.all_to_all(copies, "dev", 0, 0, tiled=True)

    def from_device(block, source):
        return lax.ppermute(block, "dev", [(source(i) % devices, i) for i in range(devices)])

    def sum_over_devices(x):
        distance = 1
        while distance < devices:
            x = x + from_device(x, lambda i: i ^ distance)
            distance *= 2
        return x

    def to_chips(mixed):
        own = jnp.concatenate([mixed, from_device(mixed, lambda i: i ^ 1)], axis=0)
        return from_device(own, lambda i: i - 2), own, from_device(own, lambda i: i + 2)

    def mix(coef, links, first_time):
        out = pl.pallas_call(
            functools.partial(link_kernel, norm, devices, per_dev, first_time),
            in_specs=[smem, smem, vmem, hbm if first_time else vmem],
            out_specs=[vmem, vmem] if first_time else [vmem],
            out_shape=[jax.ShapeDtypeStruct((per_dev, rank), bf16)] + [pltpu.VMEM(links.shape, bf16)] * first_time,
            scratch_shapes=[
                pltpu.VMEM((clusters, rank), f32),
                pltpu.VMEM((per_dev * n_links // 2, rank), f32),
                pltpu.VMEM((8, rank), f32),
            ]
            + [pltpu.SemaphoreType.DMA((per_dev * n_links // (2 * GROUP),))] * first_time,
            compiler_params=params,
            name="link_product",
        )(slot_of, partners, coef, links)
        return out

    mixed1, links_v = mix(to_all(coef1), far(link_blocks), True)
    first, coef2 = pl.pallas_call(
        functools.partial(both_kernel, devices, per_dev),
        in_specs=[vmem] * 7 + [hbm],
        out_specs=[vmem, vmem],
        out_shape=[pltpu.VMEM((high, LANES), f32), jax.ShapeDtypeStruct((devices, per_dev, rank), f32)],
        scratch_shapes=[
            pltpu.VMEM((ROWS, LANES), jnp.int32),
            pltpu.VMEM((ROWS, rank), f32),
            pltpu.VMEM((ROWS, rank), f32),
            pltpu.VMEM((high, LANES), f32),
            pltpu.VMEM((ROWS, TILE), bf16),
            pltpu.VMEM((ROWS, TILE), bf16),
            pltpu.VMEM((SLOTS, COPY, rank), bf16),
            pltpu.SemaphoreType.DMA((SLOTS,)),
        ],
        compiler_params=params,
        name="first_and_coef_pass",
    )(slot_row, *to_chips(mixed1), close(assign_v), scores, close(turned_v), far(basis_rows))
    (mixed2,) = mix(sum_over_devices(coef2).reshape(clusters, rank), close(links_v), False)

    out = pl.pallas_call(
        functools.partial(last_kernel, devices, per_dev),
        in_specs=[vmem] * 7,
        out_specs=vmem,
        out_shape=jax.ShapeDtypeStruct((high, LANES), f32),
        scratch_shapes=[
            pltpu.VMEM((ROWS, LANES), jnp.int32),
            pltpu.VMEM((ROWS, rank), f32),
        ],
        compiler_params=params,
        name="last_pass",
    )(slot_row, *to_chips(mixed2), close(assign_v), close(first), close(turned_v))
    return out.reshape(samples)


def solution(mesh):
    in_specs = (
        P(("groups", "dev"), None),
        P(("groups", "dev")),
        P(("groups", "dev")),
        P(("groups", "dev")),
        P("groups"),
        P(("groups", "dev"), None),
        P(("groups", "dev"), None, None, None),
    )
    out_specs = P(("groups", "dev"))
    return jax.shard_map(shards, mesh=mesh, in_specs=in_specs, out_specs=out_specs, check_vma=False)
```

```python
import functools
import math

import jax
import jax.numpy as jnp
from jax import lax
from jax.experimental import pallas as pl
from jax.experimental.pallas import tpu as pltpu
from jax.sharding import PartitionSpec as P

REACH = 2
NEAR = 2 * REACH + 1
CL_DEV = 4
S_DEV = 65536
LANES = 128
ROWS = 24

COPY = 8192
TILE = 2048
PER_COPY = COPY // TILE
SLOTS = 3
BODY = 16
PIECE = 512
GROUP = 8
LINKS = 32

ridge = 0.5


def near_clusters(devices, per_dev, slot_of_ref, cl_ref):
    clusters = devices * per_dev
    me = lax.axis_index("dev")
    near = lax.broadcasted_iota(jnp.int32, (ROWS, clusters), 0)
    slots = (me + devices - REACH) * per_dev + near
    slots = lax.rem(slots, clusters)
    number = lax.broadcasted_iota(jnp.int32, (ROWS, clusters), 1)
    hit = (slot_of_ref[...] == slots) & (near < NEAR * per_dev)
    found = jnp.sum(jnp.where(hit, number + 1, 0), axis=1, keepdims=True) - 1
    cl_ref[...] = jnp.broadcast_to(found, cl_ref.shape)


def near_rows(per_dev, chips, rows_ref):
    even_core = lax.rem(lax.axis_index("dev"), 2) == 0
    chips = [chip[...].astype(jnp.float32) for chip in chips]
    rows_ref[...] = jnp.zeros_like(rows_ref)
    for g in range(NEAR):
        if g % 2 == 0:
            rows = chips[g // 2][:per_dev, :]
        else:
            rows = jnp.where(even_core, chips[g // 2][per_dev:, :], chips[g // 2 + 1][per_dev:, :])
        rows_ref[g * per_dev : (g + 1) * per_dev, :] = rows


def put_sums(per_dev, sum_ref, out_ref):
    for g in range(NEAR):
        out_ref[:, g * LANES : (g + 1) * LANES] = sum_ref[g * per_dev : (g + 1) * per_dev, :].astype(jnp.bfloat16)


def slot_copy(basis_hbm, slots_ref, sem, c):
    slot = lax.rem(c, SLOTS)
    rows = pl.ds(pl.multiple_of(c * COPY, COPY), COPY)
    return pltpu.make_async_copy(basis_hbm.at[rows, :], slots_ref.at[slot], sem.at[slot])


def tile_at(t):
    return pl.ds(pl.multiple_of(t * TILE, TILE), TILE)


def row_at(t, i):
    return pl.ds(t * (TILE // LANES) + i, 1)


def coef_kernel(
    devices, per_dev, slot_of_hbm, assign_hbm, vector_hbm, basis_hbm,
    out_ref, assign_ref,
    slot_of_ref, cl_ref, sum_ref, vector_ref, x_ref, slots_ref, small_sem, basis_sem,
):
    copies = basis_hbm.shape[0] // COPY

    def basis_copy(c):
        return slot_copy(basis_hbm, slots_ref, basis_sem, c)

    slot_of_copy = pltpu.make_async_copy(slot_of_hbm, slot_of_ref, small_sem.at[2])
    assign_copy = pltpu.make_async_copy(assign_hbm, assign_ref, small_sem.at[0])
    vector_copy = pltpu.make_async_copy(vector_hbm, vector_ref, small_sem.at[1])
    slot_of_copy.start()
    assign_copy.start()
    vector_copy.start()
    for c in range(SLOTS):
        basis_copy(c).start()
    slot_of_copy.wait()
    near_clusters(devices, per_dev, slot_of_ref, cl_ref)
    sum_ref[...] = jnp.zeros_like(sum_ref)
    assign_copy.wait()
    vector_copy.wait()
    x_ref[...] = vector_ref[...].astype(jnp.float32)
    cl = cl_ref[...]

    @pl.loop(0, copies)
    def _(c):
        basis_copy(c).wait()
        total = sum_ref[...]
        for p in range(PER_COPY):
            t = c * PER_COPY + p
            parts = []
            for i in range(TILE // LANES):
                hit = assign_ref[row_at(t, i), :] == cl
                parts.append(jnp.where(hit, x_ref[row_at(t, i), :], 0.0).astype(jnp.bfloat16))
            left = jnp.concatenate(parts, axis=1)
            block = slots_ref[lax.rem(c, SLOTS), p * TILE : (p + 1) * TILE, :]
            total += jnp.dot(left, block, preferred_element_type=jnp.float32)
        sum_ref[...] = total

        @pl.when(c + SLOTS < copies)
        def _():
            basis_copy(c + SLOTS).start()

    put_sums(per_dev, sum_ref, out_ref)


def turn_kernel(after_ref, basis_hbm, turned_ref, slots_ref, basis_sem):
    copies = basis_hbm.shape[0] // COPY

    def basis_copy(c):
        return slot_copy(basis_hbm, slots_ref, basis_sem, c)

    for c in range(SLOTS):
        basis_copy(c).start()

    @pl.loop(0, copies)
    def _(c):
        basis_copy(c).wait()
        for p in range(PER_COPY):
            turned_ref[:, tile_at(c * PER_COPY + p)] = slots_ref[lax.rem(c, SLOTS), p * TILE : (p + 1) * TILE, :].T

        @pl.when(c + SLOTS < copies)
        def _():
            basis_copy(c + SLOTS).start()


def link_kernel(norm, devices, per_dev, first_time, slot_of_ref, partners_ref, parts_ref, *refs):
    if first_time:
        links_hbm, out_ref, links_ref, scaled_ref, picked_ref, mixed_ref, links_sem = refs
    else:
        links_ref, out_ref, scaled_ref, picked_ref, mixed_ref = refs
    n_links, rank = links_ref.shape[1:3]
    step = 2 * GROUP

    def piece_copy(j, k):
        ks = pl.ds(k, LINKS)
        return pltpu.make_async_copy(links_hbm.at[j, ks], links_ref.at[j, ks], links_sem.at[(j * n_links + k) // LINKS])

    if first_time:
        for j in range(per_dev):
            for k in range(0, n_links, LINKS):
                piece_copy(j, k).start()
    for owner in range(devices):
        coef = parts_ref[(owner + REACH) % devices, :, :LANES].astype(jnp.float32)
        for g in range(1, NEAR):
            coef += parts_ref[(owner + REACH - g) % devices, :, g * LANES : (g + 1) * LANES].astype(jnp.float32)
        scaled_ref[owner * per_dev : (owner + 1) * per_dev, :] = (coef * norm).astype(jnp.bfloat16).astype(jnp.float32)

    def partner(j, k):
        return scaled_ref[pl.ds(slot_of_ref[partners_ref[j, k]], 1), :]

    row = lax.broadcasted_iota(jnp.int32, (GROUP, rank), 0)
    mixed_ref[...] = jnp.zeros_like(mixed_ref)
    for j in range(per_dev):
        acc = jnp.zeros((rank, rank), jnp.float32)
        few = jnp.zeros((GROUP, rank), jnp.float32)
        for k in range(0, n_links, step):
            if first_time and k % LINKS == 0:
                piece_copy(j, k).wait()
            at = (j * n_links + k) // 2
            for u in range(GROUP):
                picked_ref[at + u : at + u + 1, :] = partner(j, k + GROUP + u)
            blocks = links_ref[j, k + GROUP : k + step].reshape(GROUP * rank, rank)
            picked = picked_ref[at : at + GROUP, :].astype(jnp.bfloat16)
            products = lax.dot_general(picked, blocks, (((1,), (1,)), ((), ())), preferred_element_type=jnp.float32)
            for u in range(GROUP):
                acc += links_ref[j, k + u].astype(jnp.float32) * partner(j, k + u)
            for u in range(GROUP):
                few += jnp.where(row == u, products[:, u * rank : (u + 1) * rank], 0.0)
        mixed_ref[j : j + 1, :] = jnp.sum(acc.T, axis=0, keepdims=True) + jnp.sum(few, axis=0, keepdims=True)
    out_ref[...] = mixed_ref[:per_dev, :].astype(jnp.bfloat16)


def own_product(hit, products):
    return jnp.sum(jnp.where(hit, products, 0.0), axis=0, keepdims=True)


def both_kernel(
    devices, per_dev, slot_of_ref, behind_ref, own_ref, ahead_ref, assign_ref, scores_ref, turned_ref, basis_hbm,
    first_ref, out_ref, cl_ref, rows_ref, sum_ref, slope_ref, even_ref, odd_ref, even_left, odd_left, slots_ref, basis_sem,
):
    tiles = turned_ref.shape[1] // TILE
    copies = tiles // PER_COPY

    def basis_copy(c):
        return slot_copy(basis_hbm, slots_ref, basis_sem, c)

    for c in range(SLOTS):
        basis_copy(c).start()
    near_clusters(devices, per_dev, slot_of_ref, cl_ref)
    near_rows(per_dev, (behind_ref, own_ref, ahead_ref), rows_ref)
    sum_ref[...] = jnp.zeros_like(sum_ref)
    sig = jax.nn.sigmoid(scores_ref[...])
    slope_ref[...] = sig * (1.0 - sig)
    cl = cl_ref[...]
    rows = rows_ref[...].astype(jnp.bfloat16)
    products_of = (even_ref, odd_ref)
    left_of = (even_left, odd_left)

    def multiply(t, side):
        products_of[side][...] = jnp.dot(rows, turned_ref[:, tile_at(t)], preferred_element_type=jnp.float32)

    def select(t, side):
        for i in range(TILE // LANES):
            at = slice(i * LANES, (i + 1) * LANES)
            hit = assign_ref[row_at(t, i), :] == cl
            first = own_product(hit, products_of[side][:, at])
            first_ref[row_at(t, i), :] = first
            weighted = slope_ref[row_at(t, i), :] * first
            left_of[side][:, at] = jnp.where(hit, weighted, 0.0).astype(jnp.bfloat16)

    def add_up(c, p):
        block = slots_ref[lax.rem(c, SLOTS), p * TILE : (p + 1) * TILE, :]
        sum_ref[...] += jnp.dot(left_of[p % 2][...], block, preferred_element_type=jnp.float32)

    multiply(0, 0)
    select(0, 0)
    multiply(1, 1)

    @pl.loop(0, copies - 1)
    def _(c):
        basis_copy(c).wait()
        for p in range(PER_COPY):
            t = c * PER_COPY + p
            add_up(c, p)
            multiply(t + 2, p % 2)
            select(t + 1, (p + 1) % 2)

        @pl.when(c + SLOTS < copies)
        def _():
            basis_copy(c + SLOTS).start()

    basis_copy(copies - 1).wait()
    for p in range(PER_COPY):
        t = (copies - 1) * PER_COPY + p
        add_up(copies - 1, p)
        if p + 2 < PER_COPY:
            multiply(t + 2, p % 2)
        if p + 1 < PER_COPY:
            select(t + 1, (p + 1) % 2)
    put_sums(per_dev, sum_ref, out_ref)


def last_kernel(
    devices, per_dev, slot_of_ref, behind_ref, own_ref, ahead_ref, assign_ref, first_ref, turned_ref, out_ref, cl_ref, rows_ref
):
    near_clusters(devices, per_dev, slot_of_ref, cl_ref)
    near_rows(per_dev, (behind_ref, own_ref, ahead_ref), rows_ref)
    cl = cl_ref[...]
    rows = rows_ref[...].astype(jnp.bfloat16)

    @pl.loop(0, turned_ref.shape[1] // (BODY * TILE))
    def _(c):
        for piece in range(BODY * TILE // PIECE):
            at = pl.ds(pl.multiple_of(c * (BODY * TILE) + piece * PIECE, PIECE), PIECE)
            products = jnp.dot(rows, turned_ref[:, at], preferred_element_type=jnp.float32)
            for k in range(PIECE // LANES):
                row = row_at(c * BODY, piece * (PIECE // LANES) + k)
                hit = assign_ref[row, :] == cl
                second = own_product(hit, products[:, k * LANES : (k + 1) * LANES])
                out_ref[row, :] = second + ridge * first_ref[row, :]


def shards(basis_rows, vector, scores, assign, slot_of, partners, link_blocks):
    devices = lax.axis_size("dev")
    clusters = slot_of.shape[0]
    per_dev, n_links, rank, _ = link_blocks.shape
    samples = assign.shape[0]
    norm = 1.0 / math.sqrt(S_DEV // CL_DEV)
    high = samples // LANES
    f32, bf16 = jnp.float32, jnp.bfloat16

    vector = vector.reshape(high, LANES)
    scores = scores.reshape(high, LANES)
    assign = assign.reshape(high, LANES)
    slot_row = slot_of.reshape(1, clusters)

    far = lambda x: pltpu.with_memory_space_constraint(x, pltpu.HBM)
    close = lambda x: pltpu.with_memory_space_constraint(x, pltpu.VMEM)
    vmem = pl.BlockSpec(memory_space=pltpu.VMEM)
    smem = pl.BlockSpec(memory_space=pltpu.SMEM)
    hbm = pl.BlockSpec(memory_space=pltpu.HBM)
    coef_shape = jax.ShapeDtypeStruct((per_dev, NEAR * rank), bf16)
    params = pltpu.CompilerParams(vmem_limit_bytes=10 * 1024 * 1024)

    coef1, assign_v = pl.pallas_call(
        functools.partial(coef_kernel, devices, per_dev),
        in_specs=[hbm] * 4,
        out_specs=[vmem] * 2,
        out_shape=[
            coef_shape,
            pltpu.VMEM((high, LANES), jnp.int32),
        ],
        scratch_shapes=[
            pltpu.VMEM((1, clusters), jnp.int32),
            pltpu.VMEM((ROWS, LANES), jnp.int32),
            pltpu.VMEM((ROWS, rank), f32),
            pltpu.VMEM((high, LANES), bf16),
            pltpu.VMEM((high, LANES), f32),
            pltpu.VMEM((SLOTS, COPY, rank), bf16),
            pltpu.SemaphoreType.DMA((3,)),
            pltpu.SemaphoreType.DMA((SLOTS,)),
        ],
        compiler_params=params,
        name="coef_pass",
    )(far(slot_row), far(assign), far(vector), far(basis_rows))

    def to_all(block):
        copies = jnp.broadcast_to(block[None], (devices,) + block.shape)
        return lax.all_to_all(copies, "dev", 0, 0, tiled=True)

    def from_device(block, source):
        return lax.ppermute(block, "dev", [(source(i) % devices, i) for i in range(devices)])

    def to_chips(mixed):
        own = jnp.concatenate([mixed, from_device(mixed, lambda i: i ^ 1)], axis=0)
        return from_device(own, lambda i: i - 2), own, from_device(own, lambda i: i + 2)

    def mix(coef, links, first_time):
        out = pl.pallas_call(
            functools.partial(link_kernel, norm, devices, per_dev, first_time),
            in_specs=[smem, smem, vmem, hbm if first_time else vmem],
            out_specs=[vmem, vmem] if first_time else [vmem],
            out_shape=[jax.ShapeDtypeStruct((per_dev, rank), bf16)] + [pltpu.VMEM(links.shape, bf16)] * first_time,
            scratch_shapes=[
                pltpu.VMEM((clusters, rank), f32),
                pltpu.VMEM((per_dev * n_links // 2, rank), f32),
                pltpu.VMEM((8, rank), f32),
            ]
            + [pltpu.SemaphoreType.DMA((per_dev * n_links // LINKS,))] * first_time,
            compiler_params=params,
            name="link_product",
        )(slot_of, partners, coef, links)
        return out

    mixed1, links_v = mix(to_all(coef1), far(link_blocks), True)
    chips1 = to_chips(mixed1)
    turned_v = pl.pallas_call(
        turn_kernel,
        in_specs=[vmem, hbm],
        out_specs=vmem,
        out_shape=pltpu.VMEM((rank, samples), bf16),
        scratch_shapes=[
            pltpu.VMEM((SLOTS, COPY, rank), bf16),
            pltpu.SemaphoreType.DMA((SLOTS,)),
        ],
        compiler_params=params,
        cost_estimate=pl.CostEstimate(flops=0, bytes_accessed=4 * basis_rows.size, transcendentals=0),
        name="turn_basis",
    )(chips1[1], far(basis_rows))

    first, coef2 = pl.pallas_call(
        functools.partial(both_kernel, devices, per_dev),
        in_specs=[vmem] * 7 + [hbm],
        out_specs=[vmem, vmem],
        out_shape=[pltpu.VMEM((high, LANES), f32), coef_shape],
        scratch_shapes=[
            pltpu.VMEM((ROWS, LANES), jnp.int32),
            pltpu.VMEM((ROWS, rank), f32),
            pltpu.VMEM((ROWS, rank), f32),
            pltpu.VMEM((high, LANES), f32),
            pltpu.VMEM((ROWS, TILE), f32),
            pltpu.VMEM((ROWS, TILE), f32),
            pltpu.VMEM((ROWS, TILE), bf16),
            pltpu.VMEM((ROWS, TILE), bf16),
            pltpu.VMEM((SLOTS, COPY, rank), bf16),
            pltpu.SemaphoreType.DMA((SLOTS,)),
        ],
        compiler_params=params,
        name="first_and_coef_pass",
    )(slot_row, *chips1, close(assign_v), scores, close(turned_v), far(basis_rows))
    (mixed2,) = mix(to_all(coef2), close(links_v), False)

    out = pl.pallas_call(
        functools.partial(last_kernel, devices, per_dev),
        in_specs=[vmem] * 7,
        out_specs=vmem,
        out_shape=jax.ShapeDtypeStruct((high, LANES), f32),
        scratch_shapes=[
            pltpu.VMEM((ROWS, LANES), jnp.int32),
            pltpu.VMEM((ROWS, rank), f32),
        ],
        compiler_params=params,
        name="last_pass",
    )(slot_row, *to_chips(mixed2), close(assign_v), close(first), close(turned_v))
    return out.reshape(samples)


def solution(mesh):
    in_specs = (
        P(("groups", "dev"), None),
        P(("groups", "dev")),
        P(("groups", "dev")),
        P(("groups", "dev")),
        P("groups"),
        P(("groups", "dev"), None),
        P(("groups", "dev"), None, None, None),
    )
    out_specs = P(("groups", "dev"))
    return jax.shard_map(shards, mesh=mesh, in_specs=in_specs, out_specs=out_specs, check_vma=False)
```

```python
import functools
import math

import jax
import jax.numpy as jnp
from jax import lax
from jax.experimental import pallas as pl
from jax.experimental.pallas import tpu as pltpu
from jax.sharding import PartitionSpec as P

REACH = 2
NEAR = 2 * REACH + 1
CL_DEV = 4
S_DEV = 65536
LANES = 128
ROWS = 24

COPY = 8192
TILE = 2048
PER_COPY = COPY // TILE
SLOTS = 3
BODY = 16
PIECE = 512
GROUP = 8
BODY2 = 8
LINKS = 32

ridge = 0.5


def near_clusters(devices, per_dev, slot_of_ref, cl_ref):
    clusters = devices * per_dev
    me = lax.axis_index("dev")
    near = lax.broadcasted_iota(jnp.int32, (ROWS, clusters), 0)
    slots = (me + devices - REACH) * per_dev + near
    slots = lax.rem(slots, clusters)
    number = lax.broadcasted_iota(jnp.int32, (ROWS, clusters), 1)
    hit = (slot_of_ref[...] == slots) & (near < NEAR * per_dev)
    found = jnp.sum(jnp.where(hit, number + 1, 0), axis=1, keepdims=True) - 1
    cl_ref[...] = jnp.broadcast_to(found, cl_ref.shape)


def near_rows(per_dev, chips, rows_ref):
    even_core = lax.rem(lax.axis_index("dev"), 2) == 0
    chips = [chip[...].astype(jnp.float32) for chip in chips]
    rows_ref[...] = jnp.zeros_like(rows_ref)
    for g in range(NEAR):
        if g % 2 == 0:
            rows = chips[g // 2][:per_dev, :]
        else:
            rows = jnp.where(even_core, chips[g // 2][per_dev:, :], chips[g // 2 + 1][per_dev:, :])
        rows_ref[g * per_dev : (g + 1) * per_dev, :] = rows


def put_sums(per_dev, sum_ref, out_ref):
    for g in range(NEAR):
        out_ref[:, g * LANES : (g + 1) * LANES] = sum_ref[g * per_dev : (g + 1) * per_dev, :].astype(jnp.bfloat16)


def slot_copy(basis_hbm, slots_ref, sem, c):
    slot = lax.rem(c, SLOTS)
    rows = pl.ds(pl.multiple_of(c * COPY, COPY), COPY)
    return pltpu.make_async_copy(basis_hbm.at[rows, :], slots_ref.at[slot], sem.at[slot])


def tile_at(t):
    return pl.ds(pl.multiple_of(t * TILE, TILE), TILE)


def row_at(t, i):
    return pl.ds(t * (TILE // LANES) + i, 1)


def coef_kernel(
    devices, per_dev, slot_of_hbm, assign_hbm, vector_hbm, basis_hbm,
    out_ref, turned_ref, assign_ref,
    slot_of_ref, cl_ref, sum_ref, vector_ref, x_ref, slots_ref, small_sem, basis_sem,
):
    copies = basis_hbm.shape[0] // COPY

    def basis_copy(c):
        return slot_copy(basis_hbm, slots_ref, basis_sem, c)

    slot_of_copy = pltpu.make_async_copy(slot_of_hbm, slot_of_ref, small_sem.at[2])
    assign_copy = pltpu.make_async_copy(assign_hbm, assign_ref, small_sem.at[0])
    vector_copy = pltpu.make_async_copy(vector_hbm, vector_ref, small_sem.at[1])
    slot_of_copy.start()
    assign_copy.start()
    vector_copy.start()
    for c in range(SLOTS):
        basis_copy(c).start()
    slot_of_copy.wait()
    near_clusters(devices, per_dev, slot_of_ref, cl_ref)
    sum_ref[...] = jnp.zeros_like(sum_ref)
    assign_copy.wait()
    vector_copy.wait()
    x_ref[...] = vector_ref[...].astype(jnp.float32)
    cl = cl_ref[...]

    @pl.loop(0, copies)
    def _(c):
        basis_copy(c).wait()
        total = sum_ref[...]
        for p in range(PER_COPY):
            t = c * PER_COPY + p
            parts = []
            for i in range(TILE // LANES):
                hit = assign_ref[row_at(t, i), :] == cl
                parts.append(jnp.where(hit, x_ref[row_at(t, i), :], 0.0).astype(jnp.bfloat16))
            left = jnp.concatenate(parts, axis=1)
            block = slots_ref[lax.rem(c, SLOTS), p * TILE : (p + 1) * TILE, :]
            turned_ref[:, tile_at(t)] = block.T
            total += jnp.dot(left, block, preferred_element_type=jnp.float32)
        sum_ref[...] = total

        @pl.when(c + SLOTS < copies)
        def _():
            basis_copy(c + SLOTS).start()

    put_sums(per_dev, sum_ref, out_ref)


def link_kernel(norm, devices, per_dev, first_time, slot_of_ref, partners_ref, parts_ref, *refs):
    if first_time:
        links_hbm, out_ref, links_ref, scaled_ref, picked_ref, mixed_ref, links_sem = refs
    else:
        links_ref, out_ref, scaled_ref, picked_ref, mixed_ref = refs
    n_links, rank = links_ref.shape[1:3]
    step = 2 * GROUP

    def piece_copy(j, k):
        ks = pl.ds(k, LINKS)
        return pltpu.make_async_copy(links_hbm.at[j, ks], links_ref.at[j, ks], links_sem.at[(j * n_links + k) // LINKS])

    if first_time:
        for j in range(per_dev):
            for k in range(0, n_links, LINKS):
                piece_copy(j, k).start()
    for owner in range(devices):
        coef = parts_ref[(owner + REACH) % devices, :, :LANES].astype(jnp.float32)
        for g in range(1, NEAR):
            coef += parts_ref[(owner + REACH - g) % devices, :, g * LANES : (g + 1) * LANES].astype(jnp.float32)
        scaled_ref[owner * per_dev : (owner + 1) * per_dev, :] = (coef * norm).astype(jnp.bfloat16).astype(jnp.float32)

    def partner(j, k):
        return scaled_ref[pl.ds(slot_of_ref[partners_ref[j, k]], 1), :]

    row = lax.broadcasted_iota(jnp.int32, (GROUP, rank), 0)
    mixed_ref[...] = jnp.zeros_like(mixed_ref)
    for j in range(per_dev):
        acc = jnp.zeros((rank, rank), jnp.float32)
        few = jnp.zeros((GROUP, rank), jnp.float32)
        for k in range(0, n_links, step):
            if first_time and k % LINKS == 0:
                piece_copy(j, k).wait()
            at = (j * n_links + k) // 2
            for u in range(GROUP):
                picked_ref[at + u : at + u + 1, :] = partner(j, k + GROUP + u)
            blocks = links_ref[j, k + GROUP : k + step].reshape(GROUP * rank, rank)
            picked = picked_ref[at : at + GROUP, :].astype(jnp.bfloat16)
            products = lax.dot_general(picked, blocks, (((1,), (1,)), ((), ())), preferred_element_type=jnp.float32)
            for u in range(GROUP):
                acc += links_ref[j, k + u].astype(jnp.float32) * partner(j, k + u)
            for u in range(GROUP):
                few += jnp.where(row == u, products[:, u * rank : (u + 1) * rank], 0.0)
        mixed_ref[j : j + 1, :] = jnp.sum(acc.T, axis=0, keepdims=True) + jnp.sum(few, axis=0, keepdims=True)
    out_ref[...] = mixed_ref[:per_dev, :].astype(jnp.bfloat16)


def own_product(hit, products):
    return jnp.sum(jnp.where(hit, products, 0.0), axis=0, keepdims=True)


def both_kernel(
    devices, per_dev, slot_of_ref, behind_ref, own_ref, ahead_ref, assign_ref, scores_ref, turned_ref,
    first_ref, out_ref, cl_ref, rows_ref, sum_ref, tall_ref, slope_ref, even_ref, odd_ref, even_left, odd_left,
):
    tiles = turned_ref.shape[1] // TILE
    near_clusters(devices, per_dev, slot_of_ref, cl_ref)
    near_rows(per_dev, (behind_ref, own_ref, ahead_ref), rows_ref)
    sum_ref[...] = jnp.zeros_like(sum_ref)
    sig = jax.nn.sigmoid(scores_ref[...])
    slope_ref[...] = sig * (1.0 - sig)
    cl = cl_ref[...]
    rows = rows_ref[...].astype(jnp.bfloat16)
    products_of = (even_ref, odd_ref)
    left_of = (even_left, odd_left)

    def multiply(t, side):
        products_of[side][...] = jnp.dot(rows, turned_ref[:, tile_at(t)], preferred_element_type=jnp.float32)

    def select(t, side):
        for i in range(TILE // LANES):
            at = slice(i * LANES, (i + 1) * LANES)
            hit = assign_ref[row_at(t, i), :] == cl
            first = own_product(hit, products_of[side][:, at])
            first_ref[row_at(t, i), :] = first
            weighted = slope_ref[row_at(t, i), :] * first
            left_of[side][:, at] = jnp.where(hit, weighted, 0.0).astype(jnp.bfloat16)

    def add_up(t, side):
        return lax.dot_general(
            turned_ref[:, tile_at(t)], left_of[side][...], (((1,), (1,)), ((), ())), preferred_element_type=jnp.float32
        )

    multiply(0, 0)
    select(0, 0)
    multiply(1, 1)
    tall_ref[...] = jnp.zeros_like(tall_ref)

    @pl.loop(0, tiles // BODY2)
    def _(c):
        total = tall_ref[...]
        for p in range(BODY2):
            t = c * BODY2 + p
            total += add_up(t, p % 2)
            multiply(lax.rem(t + 2, tiles), p % 2)
            select(lax.rem(t + 1, tiles), (p + 1) % 2)
        tall_ref[...] = total

    rank = sum_ref.shape[1]
    wide = jnp.concatenate([tall_ref[...], jnp.zeros((rank, rank - ROWS), jnp.float32)], axis=1)
    sum_ref[...] = wide.T[:ROWS, :]
    put_sums(per_dev, sum_ref, out_ref)


def last_kernel(
    devices, per_dev, slot_of_ref, behind_ref, own_ref, ahead_ref, assign_ref, first_ref, turned_ref, out_ref, cl_ref, rows_ref
):
    near_clusters(devices, per_dev, slot_of_ref, cl_ref)
    near_rows(per_dev, (behind_ref, own_ref, ahead_ref), rows_ref)
    cl = cl_ref[...]
    rows = rows_ref[...].astype(jnp.bfloat16)

    @pl.loop(0, turned_ref.shape[1] // (BODY * TILE))
    def _(c):
        for piece in range(BODY * TILE // PIECE):
            at = pl.ds(pl.multiple_of(c * (BODY * TILE) + piece * PIECE, PIECE), PIECE)
            products = jnp.dot(rows, turned_ref[:, at], preferred_element_type=jnp.float32)
            for k in range(PIECE // LANES):
                row = row_at(c * BODY, piece * (PIECE // LANES) + k)
                hit = assign_ref[row, :] == cl
                second = own_product(hit, products[:, k * LANES : (k + 1) * LANES])
                out_ref[row, :] = second + ridge * first_ref[row, :]


def shards(basis_rows, vector, scores, assign, slot_of, partners, link_blocks):
    devices = lax.axis_size("dev")
    clusters = slot_of.shape[0]
    per_dev, n_links, rank, _ = link_blocks.shape
    samples = assign.shape[0]
    norm = 1.0 / math.sqrt(S_DEV // CL_DEV)
    high = samples // LANES
    f32, bf16 = jnp.float32, jnp.bfloat16

    vector = vector.reshape(high, LANES)
    scores = scores.reshape(high, LANES)
    assign = assign.reshape(high, LANES)
    slot_row = slot_of.reshape(1, clusters)

    far = lambda x: pltpu.with_memory_space_constraint(x, pltpu.HBM)
    close = lambda x: pltpu.with_memory_space_constraint(x, pltpu.VMEM)
    vmem = pl.BlockSpec(memory_space=pltpu.VMEM)
    smem = pl.BlockSpec(memory_space=pltpu.SMEM)
    hbm = pl.BlockSpec(memory_space=pltpu.HBM)
    coef_shape = jax.ShapeDtypeStruct((per_dev, NEAR * rank), bf16)
    params = pltpu.CompilerParams(vmem_limit_bytes=10 * 1024 * 1024)

    coef1, turned_v, assign_v = pl.pallas_call(
        functools.partial(coef_kernel, devices, per_dev),
        in_specs=[hbm] * 4,
        out_specs=[vmem] * 3,
        out_shape=[
            coef_shape,
            pltpu.VMEM((rank, samples), bf16),
            pltpu.VMEM((high, LANES), jnp.int32),
        ],
        scratch_shapes=[
            pltpu.VMEM((1, clusters), jnp.int32),
            pltpu.VMEM((ROWS, LANES), jnp.int32),
            pltpu.VMEM((ROWS, rank), f32),
            pltpu.VMEM((high, LANES), bf16),
            pltpu.VMEM((high, LANES), f32),
            pltpu.VMEM((SLOTS, COPY, rank), bf16),
            pltpu.SemaphoreType.DMA((3,)),
            pltpu.SemaphoreType.DMA((SLOTS,)),
        ],
        compiler_params=params,
        name="coef_pass",
    )(far(slot_row), far(assign), far(vector), far(basis_rows))

    def to_all(block):
        copies = jnp.broadcast_to(block[None], (devices,) + block.shape)
        return lax.all_to_all(copies, "dev", 0, 0, tiled=True)

    def from_device(block, source):
        return lax.ppermute(block, "dev", [(source(i) % devices, i) for i in range(devices)])

    def to_chips(mixed):
        own = jnp.concatenate([mixed, from_device(mixed, lambda i: i ^ 1)], axis=0)
        return from_device(own, lambda i: i - 2), own, from_device(own, lambda i: i + 2)

    def mix(coef, links, first_time):
        out = pl.pallas_call(
            functools.partial(link_kernel, norm, devices, per_dev, first_time),
            in_specs=[smem, smem, vmem, hbm if first_time else vmem],
            out_specs=[vmem, vmem] if first_time else [vmem],
            out_shape=[jax.ShapeDtypeStruct((per_dev, rank), bf16)] + [pltpu.VMEM(links.shape, bf16)] * first_time,
            scratch_shapes=[
                pltpu.VMEM((clusters, rank), f32),
                pltpu.VMEM((per_dev * n_links // 2, rank), f32),
                pltpu.VMEM((8, rank), f32),
            ]
            + [pltpu.SemaphoreType.DMA((per_dev * n_links // LINKS,))] * first_time,
            compiler_params=params,
            name="link_product",
        )(slot_of, partners, coef, links)
        return out

    mixed1, links_v = mix(to_all(coef1), far(link_blocks), True)
    first, coef2 = pl.pallas_call(
        functools.partial(both_kernel, devices, per_dev),
        in_specs=[vmem] * 7,
        out_specs=[vmem, vmem],
        out_shape=[pltpu.VMEM((high, LANES), f32), coef_shape],
        scratch_shapes=[
            pltpu.VMEM((ROWS, LANES), jnp.int32),
            pltpu.VMEM((ROWS, rank), f32),
            pltpu.VMEM((ROWS, rank), f32),
            pltpu.VMEM((rank, ROWS), f32),
            pltpu.VMEM((high, LANES), f32),
            pltpu.VMEM((ROWS, TILE), f32),
            pltpu.VMEM((ROWS, TILE), f32),
            pltpu.VMEM((ROWS, TILE), bf16),
            pltpu.VMEM((ROWS, TILE), bf16),
        ],
        compiler_params=params,
        name="first_and_coef_pass",
    )(slot_row, *to_chips(mixed1), close(assign_v), scores, close(turned_v))
    (mixed2,) = mix(to_all(coef2), close(links_v), False)

    out = pl.pallas_call(
        functools.partial(last_kernel, devices, per_dev),
        in_specs=[vmem] * 7,
        out_specs=vmem,
        out_shape=jax.ShapeDtypeStruct((high, LANES), f32),
        scratch_shapes=[
            pltpu.VMEM((ROWS, LANES), jnp.int32),
            pltpu.VMEM((ROWS, rank), f32),
        ],
        compiler_params=params,
        name="last_pass",
    )(slot_row, *to_chips(mixed2), close(assign_v), close(first), close(turned_v))
    return out.reshape(samples)


def solution(mesh):
    in_specs = (
        P(("groups", "dev"), None),
        P(("groups", "dev")),
        P(("groups", "dev")),
        P(("groups", "dev")),
        P("groups"),
        P(("groups", "dev"), None),
        P(("groups", "dev"), None, None, None),
    )
    out_specs = P(("groups", "dev"))
    return jax.shard_map(shards, mesh=mesh, in_specs=in_specs, out_specs=out_specs, check_vma=False)
```

```python
import functools
import math

import jax
import jax.numpy as jnp
from jax import lax
from jax.experimental import pallas as pl
from jax.experimental.pallas import tpu as pltpu
from jax.sharding import PartitionSpec as P

REACH = 2
NEAR = 2 * REACH + 1
CL_DEV = 4
S_DEV = 65536
LANES = 128
ROWS = 24

COPY = 8192
TILE = 2048
PER_COPY = COPY // TILE
SLOTS = 3
BODY = 16
PIECE = 512
GROUP = 8
LINKS = 32

ridge = 0.5


def near_clusters(devices, per_dev, slot_of_ref, cl_ref):
    clusters = devices * per_dev
    me = lax.axis_index("dev")
    near = lax.broadcasted_iota(jnp.int32, (ROWS, clusters), 0)
    slots = (me + devices - REACH) * per_dev + near
    slots = lax.rem(slots, clusters)
    number = lax.broadcasted_iota(jnp.int32, (ROWS, clusters), 1)
    hit = (slot_of_ref[...] == slots) & (near < NEAR * per_dev)
    found = jnp.sum(jnp.where(hit, number + 1, 0), axis=1, keepdims=True) - 1
    cl_ref[...] = jnp.broadcast_to(found, cl_ref.shape)


def near_rows(per_dev, chips, rows_ref):
    even_core = lax.rem(lax.axis_index("dev"), 2) == 0
    chips = [chip[...].astype(jnp.float32) for chip in chips]
    rows_ref[...] = jnp.zeros_like(rows_ref)
    for g in range(NEAR):
        if g % 2 == 0:
            rows = chips[g // 2][:per_dev, :]
        else:
            rows = jnp.where(even_core, chips[g // 2][per_dev:, :], chips[g // 2 + 1][per_dev:, :])
        rows_ref[g * per_dev : (g + 1) * per_dev, :] = rows


def put_sums(per_dev, sum_ref, out_ref):
    for g in range(NEAR):
        out_ref[:, g * LANES : (g + 1) * LANES] = sum_ref[g * per_dev : (g + 1) * per_dev, :].astype(jnp.bfloat16)


def slot_copy(basis_hbm, slots_ref, sem, c):
    slot = lax.rem(c, SLOTS)
    rows = pl.ds(pl.multiple_of(c * COPY, COPY), COPY)
    return pltpu.make_async_copy(basis_hbm.at[rows, :], slots_ref.at[slot], sem.at[slot])


def tile_at(t):
    return pl.ds(pl.multiple_of(t * TILE, TILE), TILE)


def row_at(t, i):
    return pl.ds(t * (TILE // LANES) + i, 1)


def coef_kernel(
    devices, per_dev, slot_of_hbm, assign_hbm, vector_hbm, basis_hbm,
    out_ref, turned_ref, assign_ref, cl_ref,
    slot_of_ref, sum_ref, vector_ref, x_ref, slots_ref, small_sem, basis_sem, last_sem,
):
    copies = basis_hbm.shape[0] // COPY

    def basis_copy(c):
        return slot_copy(basis_hbm, slots_ref, basis_sem, c)

    slot_of_copy = pltpu.make_async_copy(slot_of_hbm, slot_of_ref, small_sem.at[2])
    assign_copy = pltpu.make_async_copy(assign_hbm, assign_ref, small_sem.at[0])
    vector_copy = pltpu.make_async_copy(vector_hbm, vector_ref, small_sem.at[1])
    slot_of_copy.start()
    assign_copy.start()
    vector_copy.start()
    for c in range(SLOTS):
        basis_copy(c).start()
    slot_of_copy.wait()
    near_clusters(devices, per_dev, slot_of_ref, cl_ref)
    sum_ref[...] = jnp.zeros_like(sum_ref)
    assign_copy.wait()
    vector_copy.wait()
    x_ref[...] = vector_ref[...].astype(jnp.float32)
    cl = cl_ref[...]

    last = copies - 1

    def last_copy(p):
        rows = pl.ds(last * COPY + p * TILE, TILE)
        return pltpu.make_async_copy(
            basis_hbm.at[rows, :], slots_ref.at[last % SLOTS, pl.ds(p * TILE, TILE)], last_sem.at[p]
        )

    def add_up(c, p, total):
        t = c * PER_COPY + p
        parts = []
        for i in range(TILE // LANES):
            hit = assign_ref[row_at(t, i), :] == cl
            parts.append(jnp.where(hit, x_ref[row_at(t, i), :], 0.0).astype(jnp.bfloat16))
        left = jnp.concatenate(parts, axis=1)
        block = slots_ref[lax.rem(c, SLOTS), p * TILE : (p + 1) * TILE, :]
        turned_ref[:, tile_at(t)] = block.T
        return total + jnp.dot(left, block, preferred_element_type=jnp.float32)

    @pl.loop(0, last)
    def _(c):
        basis_copy(c).wait()
        total = sum_ref[...]
        for p in range(PER_COPY):
            total = add_up(c, p, total)
        sum_ref[...] = total

        @pl.when(c + SLOTS < last)
        def _():
            basis_copy(c + SLOTS).start()

        @pl.when(c + SLOTS == last)
        def _():
            for p in range(PER_COPY):
                last_copy(p).start()

    total = sum_ref[...]
    for p in range(PER_COPY):
        last_copy(p).wait()
        total = add_up(last, p, total)
    sum_ref[...] = total
    put_sums(per_dev, sum_ref, out_ref)


def link_kernel(norm, devices, per_dev, first_time, slot_of_ref, partners_ref, parts_ref, *refs):
    if first_time:
        links_hbm, out_ref, links_ref, scaled_ref, picked_ref, mixed_ref, links_sem = refs
    else:
        links_ref, out_ref, scaled_ref, picked_ref, mixed_ref = refs
    n_links, rank = links_ref.shape[1:3]
    step = 2 * GROUP

    def piece_copy(j, k):
        ks = pl.ds(k, LINKS)
        return pltpu.make_async_copy(links_hbm.at[j, ks], links_ref.at[j, ks], links_sem.at[(j * n_links + k) // LINKS])

    if first_time:
        for j in range(per_dev):
            for k in range(0, n_links, LINKS):
                piece_copy(j, k).start()
    for owner in range(devices):
        coef = parts_ref[(owner + REACH) % devices, :, :LANES].astype(jnp.float32)
        for g in range(1, NEAR):
            coef += parts_ref[(owner + REACH - g) % devices, :, g * LANES : (g + 1) * LANES].astype(jnp.float32)
        scaled_ref[owner * per_dev : (owner + 1) * per_dev, :] = (coef * norm).astype(jnp.bfloat16).astype(jnp.float32)

    def partner(j, k):
        return scaled_ref[pl.ds(slot_of_ref[partners_ref[j, k]], 1), :]

    row = lax.broadcasted_iota(jnp.int32, (GROUP, rank), 0)
    mixed_ref[...] = jnp.zeros_like(mixed_ref)
    for j in range(per_dev):
        acc = jnp.zeros((rank, rank), jnp.float32)
        few = jnp.zeros((GROUP, rank), jnp.float32)
        for k in range(0, n_links, step):
            if first_time and k % LINKS == 0:
                piece_copy(j, k).wait()
            at = (j * n_links + k) // 2
            for u in range(GROUP):
                picked_ref[at + u : at + u + 1, :] = partner(j, k + GROUP + u)
            blocks = links_ref[j, k + GROUP : k + step].reshape(GROUP * rank, rank)
            picked = picked_ref[at : at + GROUP, :].astype(jnp.bfloat16)
            products = lax.dot_general(picked, blocks, (((1,), (1,)), ((), ())), preferred_element_type=jnp.float32)
            for u in range(GROUP):
                acc += links_ref[j, k + u].astype(jnp.float32) * partner(j, k + u)
            for u in range(GROUP):
                few += jnp.where(row == u, products[:, u * rank : (u + 1) * rank], 0.0)
        mixed_ref[j : j + 1, :] = jnp.sum(acc.T, axis=0, keepdims=True) + jnp.sum(few, axis=0, keepdims=True)
    out_ref[...] = mixed_ref[:per_dev, :].astype(jnp.bfloat16)


def own_product(hit, products):
    return jnp.sum(jnp.where(hit, products, 0.0), axis=0, keepdims=True)


def both_kernel(
    per_dev, cl_ref, ahead_ref, own_ref, behind_ref, assign_ref, scores_ref, turned_ref, basis_hbm,
    first_ref, out_ref, rows_ref, sum_ref, slope_ref, even_ref, odd_ref, even_left, odd_left, slots_ref, basis_sem,
):
    tiles = turned_ref.shape[1] // TILE
    copies = tiles // PER_COPY

    def basis_copy(c):
        return slot_copy(basis_hbm, slots_ref, basis_sem, c)

    for c in range(SLOTS):
        basis_copy(c).start()
    near_rows(per_dev, (behind_ref, own_ref, ahead_ref), rows_ref)
    sum_ref[...] = jnp.zeros_like(sum_ref)
    sig = jax.nn.sigmoid(scores_ref[...])
    slope_ref[...] = sig * (1.0 - sig)
    cl = cl_ref[...]
    rows = rows_ref[...].astype(jnp.bfloat16)
    products_of = (even_ref, odd_ref)
    left_of = (even_left, odd_left)

    def multiply(t, side):
        products_of[side][...] = jnp.dot(rows, turned_ref[:, tile_at(t)], preferred_element_type=jnp.float32)

    def select(t, side):
        for i in range(TILE // LANES):
            at = slice(i * LANES, (i + 1) * LANES)
            hit = assign_ref[row_at(t, i), :] == cl
            first = own_product(hit, products_of[side][:, at])
            first_ref[row_at(t, i), :] = first
            weighted = slope_ref[row_at(t, i), :] * first
            left_of[side][:, at] = jnp.where(hit, weighted, 0.0).astype(jnp.bfloat16)

    def add_up(c, p):
        block = slots_ref[lax.rem(c, SLOTS), p * TILE : (p + 1) * TILE, :]
        sum_ref[...] += jnp.dot(left_of[p % 2][...], block, preferred_element_type=jnp.float32)

    multiply(0, 0)
    select(0, 0)
    multiply(1, 1)

    @pl.loop(0, copies - 1)
    def _(c):
        basis_copy(c).wait()
        for p in range(PER_COPY):
            t = c * PER_COPY + p
            add_up(c, p)
            multiply(t + 2, p % 2)
            select(t + 1, (p + 1) % 2)

        @pl.when(c + SLOTS < copies)
        def _():
            basis_copy(c + SLOTS).start()

    basis_copy(copies - 1).wait()
    for p in range(PER_COPY):
        t = (copies - 1) * PER_COPY + p
        add_up(copies - 1, p)
        if p + 2 < PER_COPY:
            multiply(t + 2, p % 2)
        if p + 1 < PER_COPY:
            select(t + 1, (p + 1) % 2)
    put_sums(per_dev, sum_ref, out_ref)


def last_kernel(
    per_dev, cl_ref, ahead_ref, own_ref, behind_ref, assign_ref, first_ref, turned_ref, out_ref, rows_ref
):
    near_rows(per_dev, (behind_ref, own_ref, ahead_ref), rows_ref)
    cl = cl_ref[...]
    rows = rows_ref[...].astype(jnp.bfloat16)

    @pl.loop(0, turned_ref.shape[1] // (BODY * TILE))
    def _(c):
        for piece in range(BODY * TILE // PIECE):
            at = pl.ds(pl.multiple_of(c * (BODY * TILE) + piece * PIECE, PIECE), PIECE)
            products = jnp.dot(rows, turned_ref[:, at], preferred_element_type=jnp.float32)
            for k in range(PIECE // LANES):
                row = row_at(c * BODY, piece * (PIECE // LANES) + k)
                hit = assign_ref[row, :] == cl
                second = own_product(hit, products[:, k * LANES : (k + 1) * LANES])
                out_ref[row, :] = second + ridge * first_ref[row, :]


def shards(basis_rows, vector, scores, assign, slot_of, partners, link_blocks):
    devices = lax.axis_size("dev")
    clusters = slot_of.shape[0]
    per_dev, n_links, rank, _ = link_blocks.shape
    samples = assign.shape[0]
    norm = 1.0 / math.sqrt(S_DEV // CL_DEV)
    high = samples // LANES
    f32, bf16 = jnp.float32, jnp.bfloat16

    vector = vector.reshape(high, LANES)
    scores = scores.reshape(high, LANES)
    assign = assign.reshape(high, LANES)
    slot_row = slot_of.reshape(1, clusters)

    far = lambda x: pltpu.with_memory_space_constraint(x, pltpu.HBM)
    close = lambda x: pltpu.with_memory_space_constraint(x, pltpu.VMEM)
    vmem = pl.BlockSpec(memory_space=pltpu.VMEM)
    smem = pl.BlockSpec(memory_space=pltpu.SMEM)
    hbm = pl.BlockSpec(memory_space=pltpu.HBM)
    coef_shape = jax.ShapeDtypeStruct((per_dev, NEAR * rank), bf16)
    params = pltpu.CompilerParams(vmem_limit_bytes=10 * 1024 * 1024)

    coef1, turned_v, assign_v, cl_v = pl.pallas_call(
        functools.partial(coef_kernel, devices, per_dev),
        in_specs=[hbm] * 4,
        out_specs=[vmem] * 4,
        out_shape=[
            coef_shape,
            pltpu.VMEM((rank, samples), bf16),
            pltpu.VMEM((high, LANES), jnp.int32),
            pltpu.VMEM((ROWS, LANES), jnp.int32),
        ],
        scratch_shapes=[
            pltpu.VMEM((1, clusters), jnp.int32),
            pltpu.VMEM((ROWS, rank), f32),
            pltpu.VMEM((high, LANES), bf16),
            pltpu.VMEM((high, LANES), f32),
            pltpu.VMEM((SLOTS, COPY, rank), bf16),
            pltpu.SemaphoreType.DMA((3,)),
            pltpu.SemaphoreType.DMA((SLOTS,)),
            pltpu.SemaphoreType.DMA((PER_COPY,)),
        ],
        compiler_params=params,
        name="coef_pass",
    )(far(slot_row), far(assign), far(vector), far(basis_rows))

    def to_all(block):
        copies = jnp.broadcast_to(block[None], (devices,) + block.shape)
        return lax.all_to_all(copies, "dev", 0, 0, tiled=True)

    def from_device(block, source):
        return lax.ppermute(block, "dev", [(source(i) % devices, i) for i in range(devices)])

    def to_chips(mixed):
        own = jnp.concatenate([mixed, from_device(mixed, lambda i: i ^ 1)], axis=0)
        ahead = from_device(own, lambda i: i + 2)
        behind = from_device(own, lambda i: i - 2)
        return ahead, own, behind

    def mix(coef, links, first_time):
        out = pl.pallas_call(
            functools.partial(link_kernel, norm, devices, per_dev, first_time),
            in_specs=[smem, smem, vmem, hbm if first_time else vmem],
            out_specs=[vmem, vmem] if first_time else [vmem],
            out_shape=[jax.ShapeDtypeStruct((per_dev, rank), bf16)] + [pltpu.VMEM(links.shape, bf16)] * first_time,
            scratch_shapes=[
                pltpu.VMEM((clusters, rank), f32),
                pltpu.VMEM((per_dev * n_links // 2, rank), f32),
                pltpu.VMEM((8, rank), f32),
            ]
            + [pltpu.SemaphoreType.DMA((per_dev * n_links // LINKS,))] * first_time,
            compiler_params=params,
            name="link_product",
        )(slot_of, partners, coef, links)
        return out

    mixed1, links_v = mix(to_all(coef1), far(link_blocks), True)
    first, coef2 = pl.pallas_call(
        functools.partial(both_kernel, per_dev),
        in_specs=[vmem] * 7 + [hbm],
        out_specs=[vmem, vmem],
        out_shape=[pltpu.VMEM((high, LANES), f32), coef_shape],
        scratch_shapes=[
            pltpu.VMEM((ROWS, rank), f32),
            pltpu.VMEM((ROWS, rank), f32),
            pltpu.VMEM((high, LANES), f32),
            pltpu.VMEM((ROWS, TILE), f32),
            pltpu.VMEM((ROWS, TILE), f32),
            pltpu.VMEM((ROWS, TILE), bf16),
            pltpu.VMEM((ROWS, TILE), bf16),
            pltpu.VMEM((SLOTS, COPY, rank), bf16),
            pltpu.SemaphoreType.DMA((SLOTS,)),
        ],
        compiler_params=params,
        name="first_and_coef_pass",
    )(close(cl_v), *to_chips(mixed1), close(assign_v), scores, close(turned_v), far(basis_rows))
    (mixed2,) = mix(to_all(coef2), close(links_v), False)

    out = pl.pallas_call(
        functools.partial(last_kernel, per_dev),
        in_specs=[vmem] * 7,
        out_specs=vmem,
        out_shape=jax.ShapeDtypeStruct((high, LANES), f32),
        scratch_shapes=[
            pltpu.VMEM((ROWS, rank), f32),
        ],
        compiler_params=params,
        name="last_pass",
    )(close(cl_v), *to_chips(mixed2), close(assign_v), close(first), close(turned_v))
    return out.reshape(samples)


def solution(mesh):
    in_specs = (
        P(("groups", "dev"), None),
        P(("groups", "dev")),
        P(("groups", "dev")),
        P(("groups", "dev")),
        P("groups"),
        P(("groups", "dev"), None),
        P(("groups", "dev"), None, None, None),
    )
    out_specs = P(("groups", "dev"))
    return jax.shard_map(shards, mesh=mesh, in_specs=in_specs, out_specs=out_specs, check_vma=False)
```

```python
import functools
import math

import jax
import jax.numpy as jnp
from jax import lax
from jax.experimental import pallas as pl
from jax.experimental.pallas import tpu as pltpu
from jax.sharding import PartitionSpec as P

REACH = 2
NEAR = 2 * REACH + 1
CL_DEV = 4
S_DEV = 65536
LANES = 128
ROWS = 24

COPY = 8192
TILE = 2048
PER_COPY = COPY // TILE
SLOTS = 3
BODY = 16
PIECE = 512
GROUP = 8
LINKS = 32

ridge = 0.5


def near_clusters(devices, per_dev, slot_of_ref, cl_ref):
    clusters = devices * per_dev
    me = lax.axis_index("dev")
    near = lax.broadcasted_iota(jnp.int32, (ROWS, clusters), 0)
    slots = (me + devices - REACH) * per_dev + near
    slots = lax.rem(slots, clusters)
    number = lax.broadcasted_iota(jnp.int32, (ROWS, clusters), 1)
    hit = (slot_of_ref[...] == slots) & (near < NEAR * per_dev)
    found = jnp.sum(jnp.where(hit, number + 1, 0), axis=1, keepdims=True) - 1
    cl_ref[...] = jnp.broadcast_to(found, cl_ref.shape)


def near_rows(devices, per_dev, chips, wrap_ref, rows_ref):
    me = lax.axis_index("dev")
    even_core = lax.rem(me, 2) == 0
    behind, own, ahead, wrap = [chip[...].astype(jnp.float32) for chip in (*chips, wrap_ref)]
    chips = [jnp.where(me < 2, wrap, behind), own, jnp.where(me >= devices - 2, wrap, ahead)]
    rows_ref[...] = jnp.zeros_like(rows_ref)
    for g in range(NEAR):
        if g % 2 == 0:
            rows = chips[g // 2][:per_dev, :]
        else:
            rows = jnp.where(even_core, chips[g // 2][per_dev:, :], chips[g // 2 + 1][per_dev:, :])
        rows_ref[g * per_dev : (g + 1) * per_dev, :] = rows


def put_sums(per_dev, sum_ref, out_ref):
    for g in range(NEAR):
        out_ref[:, g * LANES : (g + 1) * LANES] = sum_ref[g * per_dev : (g + 1) * per_dev, :].astype(jnp.bfloat16)


def slot_copy(basis_hbm, slots_ref, sem, c):
    slot = lax.rem(c, SLOTS)
    rows = pl.ds(pl.multiple_of(c * COPY, COPY), COPY)
    return pltpu.make_async_copy(basis_hbm.at[rows, :], slots_ref.at[slot], sem.at[slot])


def tile_at(t):
    return pl.ds(pl.multiple_of(t * TILE, TILE), TILE)


def row_at(t, i):
    return pl.ds(t * (TILE // LANES) + i, 1)


def coef_kernel(
    devices, per_dev, slot_of_hbm, assign_hbm, vector_hbm, basis_hbm,
    out_ref, turned_ref, assign_ref, cl_ref,
    slot_of_ref, sum_ref, vector_ref, x_ref, slots_ref, small_sem, basis_sem,
):
    copies = basis_hbm.shape[0] // COPY

    def basis_copy(c):
        return slot_copy(basis_hbm, slots_ref, basis_sem, c)

    slot_of_copy = pltpu.make_async_copy(slot_of_hbm, slot_of_ref, small_sem.at[2])
    assign_copy = pltpu.make_async_copy(assign_hbm, assign_ref, small_sem.at[0])
    vector_copy = pltpu.make_async_copy(vector_hbm, vector_ref, small_sem.at[1])
    slot_of_copy.start()
    assign_copy.start()
    vector_copy.start()
    for c in range(SLOTS):
        basis_copy(c).start()
    slot_of_copy.wait()
    near_clusters(devices, per_dev, slot_of_ref, cl_ref)
    sum_ref[...] = jnp.zeros_like(sum_ref)
    assign_copy.wait()
    vector_copy.wait()
    x_ref[...] = vector_ref[...].astype(jnp.float32)
    cl = cl_ref[...]

    @pl.loop(0, copies)
    def _(c):
        basis_copy(c).wait()
        total = sum_ref[...]
        for p in range(PER_COPY):
            t = c * PER_COPY + p
            parts = []
            for i in range(TILE // LANES):
                hit = assign_ref[row_at(t, i), :] == cl
                parts.append(jnp.where(hit, x_ref[row_at(t, i), :], 0.0).astype(jnp.bfloat16))
            left = jnp.concatenate(parts, axis=1)
            block = slots_ref[lax.rem(c, SLOTS), p * TILE : (p + 1) * TILE, :]
            turned_ref[:, tile_at(t)] = block.T
            total += jnp.dot(left, block, preferred_element_type=jnp.float32)
        sum_ref[...] = total

        @pl.when(c + SLOTS < copies)
        def _():
            basis_copy(c + SLOTS).start()

    put_sums(per_dev, sum_ref, out_ref)


def link_kernel(norm, devices, per_dev, first_time, slot_of_ref, partners_ref, parts_ref, *refs):
    if first_time:
        links_hbm, out_ref, links_ref, scaled_ref, picked_ref, mixed_ref, links_sem = refs
    else:
        links_ref, out_ref, scaled_ref, picked_ref, mixed_ref = refs
    n_links, rank = links_ref.shape[1:3]
    step = 2 * GROUP

    def piece_copy(j, k):
        ks = pl.ds(k, LINKS)
        return pltpu.make_async_copy(links_hbm.at[j, ks], links_ref.at[j, ks], links_sem.at[(j * n_links + k) // LINKS])

    if first_time:
        for j in range(per_dev):
            for k in range(0, n_links, LINKS):
                piece_copy(j, k).start()
    for owner in range(devices):
        coef = parts_ref[(owner + REACH) % devices, :, :LANES].astype(jnp.float32)
        for g in range(1, NEAR):
            coef += parts_ref[(owner + REACH - g) % devices, :, g * LANES : (g + 1) * LANES].astype(jnp.float32)
        scaled_ref[owner * per_dev : (owner + 1) * per_dev, :] = (coef * norm).astype(jnp.bfloat16).astype(jnp.float32)

    def partner(j, k):
        return scaled_ref[pl.ds(slot_of_ref[partners_ref[j, k]], 1), :]

    row = lax.broadcasted_iota(jnp.int32, (GROUP, rank), 0)
    mixed_ref[...] = jnp.zeros_like(mixed_ref)
    for j in range(per_dev):
        acc = jnp.zeros((rank, rank), jnp.float32)
        few = jnp.zeros((GROUP, rank), jnp.float32)
        for k in range(0, n_links, step):
            if first_time and k % LINKS == 0:
                piece_copy(j, k).wait()
            at = (j * n_links + k) // 2
            for u in range(GROUP):
                picked_ref[at + u : at + u + 1, :] = partner(j, k + GROUP + u)
            blocks = links_ref[j, k + GROUP : k + step].reshape(GROUP * rank, rank)
            picked = picked_ref[at : at + GROUP, :].astype(jnp.bfloat16)
            products = lax.dot_general(picked, blocks, (((1,), (1,)), ((), ())), preferred_element_type=jnp.float32)
            for u in range(GROUP):
                acc += links_ref[j, k + u].astype(jnp.float32) * partner(j, k + u)
            for u in range(GROUP):
                few += jnp.where(row == u, products[:, u * rank : (u + 1) * rank], 0.0)
        mixed_ref[j : j + 1, :] = jnp.sum(acc.T, axis=0, keepdims=True) + jnp.sum(few, axis=0, keepdims=True)
    out_ref[...] = mixed_ref[:per_dev, :].astype(jnp.bfloat16)


def own_product(hit, products):
    return jnp.sum(jnp.where(hit, products, 0.0), axis=0, keepdims=True)


def both_kernel(
    devices, per_dev, cl_ref, behind_ref, own_ref, ahead_ref, wrap_ref, assign_ref, scores_ref, turned_ref, basis_hbm,
    first_ref, out_ref, rows_ref, sum_ref, slope_ref, even_ref, odd_ref, even_left, odd_left, slots_ref, basis_sem,
):
    tiles = turned_ref.shape[1] // TILE
    copies = tiles // PER_COPY

    def basis_copy(c):
        return slot_copy(basis_hbm, slots_ref, basis_sem, c)

    for c in range(SLOTS):
        basis_copy(c).start()
    near_rows(devices, per_dev, (behind_ref, own_ref, ahead_ref), wrap_ref, rows_ref)
    sum_ref[...] = jnp.zeros_like(sum_ref)
    sig = jax.nn.sigmoid(scores_ref[...])
    slope_ref[...] = sig * (1.0 - sig)
    cl = cl_ref[...]
    rows = rows_ref[...].astype(jnp.bfloat16)
    products_of = (even_ref, odd_ref)
    left_of = (even_left, odd_left)

    def multiply(t, side):
        products_of[side][...] = jnp.dot(rows, turned_ref[:, tile_at(t)], preferred_element_type=jnp.float32)

    def select(t, side):
        for i in range(TILE // LANES):
            at = slice(i * LANES, (i + 1) * LANES)
            hit = assign_ref[row_at(t, i), :] == cl
            first = own_product(hit, products_of[side][:, at])
            first_ref[row_at(t, i), :] = first
            weighted = slope_ref[row_at(t, i), :] * first
            left_of[side][:, at] = jnp.where(hit, weighted, 0.0).astype(jnp.bfloat16)

    def add_up(c, p):
        block = slots_ref[lax.rem(c, SLOTS), p * TILE : (p + 1) * TILE, :]
        sum_ref[...] += jnp.dot(left_of[p % 2][...], block, preferred_element_type=jnp.float32)

    multiply(0, 0)
    select(0, 0)
    multiply(1, 1)

    @pl.loop(0, copies - 1)
    def _(c):
        basis_copy(c).wait()
        for p in range(PER_COPY):
            t = c * PER_COPY + p
            add_up(c, p)
            multiply(t + 2, p % 2)
            select(t + 1, (p + 1) % 2)

        @pl.when(c + SLOTS < copies)
        def _():
            basis_copy(c + SLOTS).start()

    basis_copy(copies - 1).wait()
    for p in range(PER_COPY):
        t = (copies - 1) * PER_COPY + p
        add_up(copies - 1, p)
        if p + 2 < PER_COPY:
            multiply(t + 2, p % 2)
        if p + 1 < PER_COPY:
            select(t + 1, (p + 1) % 2)
    put_sums(per_dev, sum_ref, out_ref)


def last_kernel(
    devices, per_dev, cl_ref, behind_ref, own_ref, ahead_ref, wrap_ref, assign_ref, first_ref, turned_ref, out_ref, rows_ref
):
    near_rows(devices, per_dev, (behind_ref, own_ref, ahead_ref), wrap_ref, rows_ref)
    cl = cl_ref[...]
    rows = rows_ref[...].astype(jnp.bfloat16)

    @pl.loop(0, turned_ref.shape[1] // (BODY * TILE))
    def _(c):
        for piece in range(BODY * TILE // PIECE):
            at = pl.ds(pl.multiple_of(c * (BODY * TILE) + piece * PIECE, PIECE), PIECE)
            products = jnp.dot(rows, turned_ref[:, at], preferred_element_type=jnp.float32)
            for k in range(PIECE // LANES):
                row = row_at(c * BODY, piece * (PIECE // LANES) + k)
                hit = assign_ref[row, :] == cl
                second = own_product(hit, products[:, k * LANES : (k + 1) * LANES])
                out_ref[row, :] = second + ridge * first_ref[row, :]


def shards(basis_rows, vector, scores, assign, slot_of, partners, link_blocks):
    devices = lax.axis_size("dev")
    clusters = slot_of.shape[0]
    per_dev, n_links, rank, _ = link_blocks.shape
    samples = assign.shape[0]
    norm = 1.0 / math.sqrt(S_DEV // CL_DEV)
    high = samples // LANES
    f32, bf16 = jnp.float32, jnp.bfloat16

    vector = vector.reshape(high, LANES)
    scores = scores.reshape(high, LANES)
    assign = assign.reshape(high, LANES)
    slot_row = slot_of.reshape(1, clusters)

    far = lambda x: pltpu.with_memory_space_constraint(x, pltpu.HBM)
    close = lambda x: pltpu.with_memory_space_constraint(x, pltpu.VMEM)
    vmem = pl.BlockSpec(memory_space=pltpu.VMEM)
    smem = pl.BlockSpec(memory_space=pltpu.SMEM)
    hbm = pl.BlockSpec(memory_space=pltpu.HBM)
    coef_shape = jax.ShapeDtypeStruct((per_dev, NEAR * rank), bf16)
    params = pltpu.CompilerParams(vmem_limit_bytes=10 * 1024 * 1024)

    coef1, turned_v, assign_v, cl_v = pl.pallas_call(
        functools.partial(coef_kernel, devices, per_dev),
        in_specs=[hbm] * 4,
        out_specs=[vmem] * 4,
        out_shape=[
            coef_shape,
            pltpu.VMEM((rank, samples), bf16),
            pltpu.VMEM((high, LANES), jnp.int32),
            pltpu.VMEM((ROWS, LANES), jnp.int32),
        ],
        scratch_shapes=[
            pltpu.VMEM((1, clusters), jnp.int32),
            pltpu.VMEM((ROWS, rank), f32),
            pltpu.VMEM((high, LANES), bf16),
            pltpu.VMEM((high, LANES), f32),
            pltpu.VMEM((SLOTS, COPY, rank), bf16),
            pltpu.SemaphoreType.DMA((3,)),
            pltpu.SemaphoreType.DMA((SLOTS,)),
        ],
        compiler_params=params,
        name="coef_pass",
    )(far(slot_row), far(assign), far(vector), far(basis_rows))

    def to_all(block):
        copies = jnp.broadcast_to(block[None], (devices,) + block.shape)
        return lax.all_to_all(copies, "dev", 0, 0, tiled=True)

    def permute(block, pairs):
        return lax.ppermute(block, "dev", pairs)

    def to_chips(mixed):
        sibling = permute(mixed, [(i ^ 1, i) for i in range(devices)])
        own = jnp.concatenate([mixed, sibling], axis=0)
        behind = permute(own, [(i - 2, i) for i in range(2, devices)])
        ahead = permute(own, [(i + 2, i) for i in range(devices - 2)])
        ends = [(i, devices - 2 + i) for i in range(2)]
        wrap = permute(own, ends + [(j, i) for i, j in ends])
        return behind, own, ahead, wrap

    def mix(coef, links, first_time):
        out = pl.pallas_call(
            functools.partial(link_kernel, norm, devices, per_dev, first_time),
            in_specs=[smem, smem, vmem, hbm if first_time else vmem],
            out_specs=[vmem, vmem] if first_time else [vmem],
            out_shape=[jax.ShapeDtypeStruct((per_dev, rank), bf16)] + [pltpu.VMEM(links.shape, bf16)] * first_time,
            scratch_shapes=[
                pltpu.VMEM((clusters, rank), f32),
                pltpu.VMEM((per_dev * n_links // 2, rank), f32),
                pltpu.VMEM((8, rank), f32),
            ]
            + [pltpu.SemaphoreType.DMA((per_dev * n_links // LINKS,))] * first_time,
            compiler_params=params,
            name="link_product",
        )(slot_of, partners, coef, links)
        return out

    mixed1, links_v = mix(to_all(coef1), far(link_blocks), True)
    first, coef2 = pl.pallas_call(
        functools.partial(both_kernel, devices, per_dev),
        in_specs=[vmem] * 8 + [hbm],
        out_specs=[vmem, vmem],
        out_shape=[pltpu.VMEM((high, LANES), f32), coef_shape],
        scratch_shapes=[
            pltpu.VMEM((ROWS, rank), f32),
            pltpu.VMEM((ROWS, rank), f32),
            pltpu.VMEM((high, LANES), f32),
            pltpu.VMEM((ROWS, TILE), f32),
            pltpu.VMEM((ROWS, TILE), f32),
            pltpu.VMEM((ROWS, TILE), bf16),
            pltpu.VMEM((ROWS, TILE), bf16),
            pltpu.VMEM((SLOTS, COPY, rank), bf16),
            pltpu.SemaphoreType.DMA((SLOTS,)),
        ],
        compiler_params=params,
        name="first_and_coef_pass",
    )(close(cl_v), *to_chips(mixed1), close(assign_v), scores, close(turned_v), far(basis_rows))
    (mixed2,) = mix(to_all(coef2), close(links_v), False)

    out = pl.pallas_call(
        functools.partial(last_kernel, devices, per_dev),
        in_specs=[vmem] * 8,
        out_specs=vmem,
        out_shape=jax.ShapeDtypeStruct((high, LANES), f32),
        scratch_shapes=[
            pltpu.VMEM((ROWS, rank), f32),
        ],
        compiler_params=params,
        name="last_pass",
    )(close(cl_v), *to_chips(mixed2), close(assign_v), close(first), close(turned_v))
    return out.reshape(samples)


def solution(mesh):
    in_specs = (
        P(("groups", "dev"), None),
        P(("groups", "dev")),
        P(("groups", "dev")),
        P(("groups", "dev")),
        P("groups"),
        P(("groups", "dev"), None),
        P(("groups", "dev"), None, None, None),
    )
    out_specs = P(("groups", "dev"))
    return jax.shard_map(shards, mesh=mesh, in_specs=in_specs, out_specs=out_specs, check_vma=False)
```

```python
import functools
import math

import jax
import jax.numpy as jnp
from jax import lax
from jax.experimental import pallas as pl
from jax.experimental.pallas import tpu as pltpu
from jax.sharding import PartitionSpec as P

REACH = 2
NEAR = 2 * REACH + 1
CL_DEV = 4
S_DEV = 65536
LANES = 128
ROWS = 24

COPY = 8192
TILE = 2048
PER_COPY = COPY // TILE
SLOTS = 3
BODY = 16
PIECE = 512
GROUP = 8

ridge = 0.5


def near_clusters(devices, per_dev, slot_of_ref, cl_ref):
    clusters = devices * per_dev
    me = lax.axis_index("dev")
    near = lax.broadcasted_iota(jnp.int32, (ROWS, clusters), 0)
    slots = (me + devices - REACH) * per_dev + near
    slots = lax.rem(slots, clusters)
    number = lax.broadcasted_iota(jnp.int32, (ROWS, clusters), 1)
    hit = (slot_of_ref[...] == slots) & (near < NEAR * per_dev)
    found = jnp.sum(jnp.where(hit, number + 1, 0), axis=1, keepdims=True) - 1
    cl_ref[...] = jnp.broadcast_to(found, cl_ref.shape)


def near_rows(per_dev, chips, rows_ref):
    even_core = lax.rem(lax.axis_index("dev"), 2) == 0
    chips = [chip[...].astype(jnp.float32) for chip in chips]
    rows_ref[...] = jnp.zeros_like(rows_ref)
    for g in range(NEAR):
        if g % 2 == 0:
            rows = chips[g // 2][:per_dev, :]
        else:
            rows = jnp.where(even_core, chips[g // 2][per_dev:, :], chips[g // 2 + 1][per_dev:, :])
        rows_ref[g * per_dev : (g + 1) * per_dev, :] = rows


def put_sums(per_dev, sum_ref, out_ref):
    for g in range(NEAR):
        out_ref[:, g * LANES : (g + 1) * LANES] = sum_ref[g * per_dev : (g + 1) * per_dev, :].astype(jnp.bfloat16)


def slot_copy(basis_hbm, slots_ref, sem, c):
    slot = lax.rem(c, SLOTS)
    rows = pl.ds(pl.multiple_of(c * COPY, COPY), COPY)
    return pltpu.make_async_copy(basis_hbm.at[rows, :], slots_ref.at[slot], sem.at[slot])


def tile_at(t):
    return pl.ds(pl.multiple_of(t * TILE, TILE), TILE)


def row_at(t, i):
    return pl.ds(t * (TILE // LANES) + i, 1)


def coef_kernel(
    devices, per_dev, slot_of_hbm, assign_hbm, vector_hbm, basis_hbm, links_hbm,
    out_ref, turned_ref, assign_ref, cl_ref, links_ref,
    slot_of_ref, sum_ref, vector_ref, x_ref, slots_ref, small_sem, basis_sem, links_sem,
):
    copies = basis_hbm.shape[0] // COPY

    def basis_copy(c):
        return slot_copy(basis_hbm, slots_ref, basis_sem, c)

    def links_copy(j):
        return pltpu.make_async_copy(links_hbm.at[j], links_ref.at[j], links_sem.at[j])

    slot_of_copy = pltpu.make_async_copy(slot_of_hbm, slot_of_ref, small_sem.at[2])
    assign_copy = pltpu.make_async_copy(assign_hbm, assign_ref, small_sem.at[0])
    vector_copy = pltpu.make_async_copy(vector_hbm, vector_ref, small_sem.at[1])
    slot_of_copy.start()
    assign_copy.start()
    vector_copy.start()
    for c in range(SLOTS):
        basis_copy(c).start()
    slot_of_copy.wait()
    near_clusters(devices, per_dev, slot_of_ref, cl_ref)
    sum_ref[...] = jnp.zeros_like(sum_ref)
    assign_copy.wait()
    vector_copy.wait()
    x_ref[...] = vector_ref[...].astype(jnp.float32)
    cl = cl_ref[...]

    @pl.loop(0, copies)
    def _(c):
        basis_copy(c).wait()

        @pl.when(c < per_dev)
        def _():
            links_copy(c).start()

        total = sum_ref[...]
        for p in range(PER_COPY):
            t = c * PER_COPY + p
            parts = []
            for i in range(TILE // LANES):
                hit = assign_ref[row_at(t, i), :] == cl
                parts.append(jnp.where(hit, x_ref[row_at(t, i), :], 0.0).astype(jnp.bfloat16))
            left = jnp.concatenate(parts, axis=1)
            block = slots_ref[lax.rem(c, SLOTS), p * TILE : (p + 1) * TILE, :]
            turned_ref[:, tile_at(t)] = block.T
            total += jnp.dot(left, block, preferred_element_type=jnp.float32)
        sum_ref[...] = total

        @pl.when(c + SLOTS < copies)
        def _():
            basis_copy(c + SLOTS).start()

    put_sums(per_dev, sum_ref, out_ref)
    for j in range(per_dev):
        links_copy(j).wait()


def link_kernel(
    norm, devices, per_dev, slot_of_ref, partners_ref, parts_ref, links_ref, out_ref, scaled_ref, picked_ref, mixed_ref
):
    n_links, rank = links_ref.shape[1:3]
    step = 2 * GROUP
    for owner in range(devices):
        coef = parts_ref[(owner + REACH) % devices, :, :LANES].astype(jnp.float32)
        for g in range(1, NEAR):
            coef += parts_ref[(owner + REACH - g) % devices, :, g * LANES : (g + 1) * LANES].astype(jnp.float32)
        scaled_ref[owner * per_dev : (owner + 1) * per_dev, :] = (coef * norm).astype(jnp.bfloat16).astype(jnp.float32)

    def partner(j, k):
        return scaled_ref[pl.ds(slot_of_ref[partners_ref[j, k]], 1), :]

    row = lax.broadcasted_iota(jnp.int32, (GROUP, rank), 0)
    mixed_ref[...] = jnp.zeros_like(mixed_ref)
    for j in range(per_dev):
        acc = jnp.zeros((rank, rank), jnp.float32)
        few = jnp.zeros((GROUP, rank), jnp.float32)
        for k in range(0, n_links, step):
            at = (j * n_links + k) // 2
            for u in range(GROUP):
                picked_ref[at + u : at + u + 1, :] = partner(j, k + GROUP + u)
            blocks = links_ref[j, k + GROUP : k + step].reshape(GROUP * rank, rank)
            picked = picked_ref[at : at + GROUP, :].astype(jnp.bfloat16)
            products = lax.dot_general(picked, blocks, (((1,), (1,)), ((), ())), preferred_element_type=jnp.float32)
            for u in range(GROUP):
                acc += links_ref[j, k + u].astype(jnp.float32) * partner(j, k + u)
            for u in range(GROUP):
                few += jnp.where(row == u, products[:, u * rank : (u + 1) * rank], 0.0)
        mixed_ref[j : j + 1, :] = jnp.sum(acc.T, axis=0, keepdims=True) + jnp.sum(few, axis=0, keepdims=True)
    out_ref[...] = mixed_ref[:per_dev, :].astype(jnp.bfloat16)


def own_product(hit, products):
    return jnp.sum(jnp.where(hit, products, 0.0), axis=0, keepdims=True)


def both_kernel(
    per_dev, cl_ref, behind_ref, own_ref, ahead_ref, assign_ref, scores_ref, turned_ref, basis_hbm,
    first_ref, out_ref, rows_ref, sum_ref, slope_ref, even_ref, odd_ref, even_left, odd_left, slots_ref, basis_sem,
):
    tiles = turned_ref.shape[1] // TILE
    copies = tiles // PER_COPY

    def basis_copy(c):
        return slot_copy(basis_hbm, slots_ref, basis_sem, c)

    for c in range(SLOTS):
        basis_copy(c).start()
    near_rows(per_dev, (behind_ref, own_ref, ahead_ref), rows_ref)
    sum_ref[...] = jnp.zeros_like(sum_ref)
    sig = jax.nn.sigmoid(scores_ref[...])
    slope_ref[...] = sig * (1.0 - sig)
    cl = cl_ref[...]
    rows = rows_ref[...].astype(jnp.bfloat16)
    products_of = (even_ref, odd_ref)
    left_of = (even_left, odd_left)

    def multiply(t, side):
        products_of[side][...] = jnp.dot(rows, turned_ref[:, tile_at(t)], preferred_element_type=jnp.float32)

    def select(t, side):
        for i in range(TILE // LANES):
            at = slice(i * LANES, (i + 1) * LANES)
            hit = assign_ref[row_at(t, i), :] == cl
            first = own_product(hit, products_of[side][:, at])
            first_ref[row_at(t, i), :] = first
            weighted = slope_ref[row_at(t, i), :] * first
            left_of[side][:, at] = jnp.where(hit, weighted, 0.0).astype(jnp.bfloat16)

    def add_up(c, p):
        block = slots_ref[lax.rem(c, SLOTS), p * TILE : (p + 1) * TILE, :]
        sum_ref[...] += jnp.dot(left_of[p % 2][...], block, preferred_element_type=jnp.float32)

    multiply(0, 0)
    select(0, 0)
    multiply(1, 1)

    @pl.loop(0, copies - 1)
    def _(c):
        basis_copy(c).wait()
        for p in range(PER_COPY):
            t = c * PER_COPY + p
            add_up(c, p)
            multiply(t + 2, p % 2)
            select(t + 1, (p + 1) % 2)

        @pl.when(c + SLOTS < copies)
        def _():
            basis_copy(c + SLOTS).start()

    basis_copy(copies - 1).wait()
    for p in range(PER_COPY):
        t = (copies - 1) * PER_COPY + p
        add_up(copies - 1, p)
        if p + 2 < PER_COPY:
            multiply(t + 2, p % 2)
        if p + 1 < PER_COPY:
            select(t + 1, (p + 1) % 2)
    put_sums(per_dev, sum_ref, out_ref)


def last_kernel(
    per_dev, cl_ref, behind_ref, own_ref, ahead_ref, assign_ref, first_ref, turned_ref, out_ref, rows_ref
):
    near_rows(per_dev, (behind_ref, own_ref, ahead_ref), rows_ref)
    cl = cl_ref[...]
    rows = rows_ref[...].astype(jnp.bfloat16)

    @pl.loop(0, turned_ref.shape[1] // (BODY * TILE))
    def _(c):
        for piece in range(BODY * TILE // PIECE):
            at = pl.ds(pl.multiple_of(c * (BODY * TILE) + piece * PIECE, PIECE), PIECE)
            products = jnp.dot(rows, turned_ref[:, at], preferred_element_type=jnp.float32)
            for k in range(PIECE // LANES):
                row = row_at(c * BODY, piece * (PIECE // LANES) + k)
                hit = assign_ref[row, :] == cl
                second = own_product(hit, products[:, k * LANES : (k + 1) * LANES])
                out_ref[row, :] = second + ridge * first_ref[row, :]


def shards(basis_rows, vector, scores, assign, slot_of, partners, link_blocks):
    devices = lax.axis_size("dev")
    clusters = slot_of.shape[0]
    per_dev, n_links, rank, _ = link_blocks.shape
    samples = assign.shape[0]
    norm = 1.0 / math.sqrt(S_DEV // CL_DEV)
    high = samples // LANES
    f32, bf16 = jnp.float32, jnp.bfloat16

    vector = vector.reshape(high, LANES)
    scores = scores.reshape(high, LANES)
    assign = assign.reshape(high, LANES)
    slot_row = slot_of.reshape(1, clusters)

    far = lambda x: pltpu.with_memory_space_constraint(x, pltpu.HBM)
    close = lambda x: pltpu.with_memory_space_constraint(x, pltpu.VMEM)
    vmem = pl.BlockSpec(memory_space=pltpu.VMEM)
    smem = pl.BlockSpec(memory_space=pltpu.SMEM)
    hbm = pl.BlockSpec(memory_space=pltpu.HBM)
    coef_shape = jax.ShapeDtypeStruct((per_dev, NEAR * rank), bf16)
    params = pltpu.CompilerParams(vmem_limit_bytes=10 * 1024 * 1024)

    coef1, turned_v, assign_v, cl_v, links_v = pl.pallas_call(
        functools.partial(coef_kernel, devices, per_dev),
        in_specs=[hbm] * 5,
        out_specs=[vmem] * 5,
        out_shape=[
            coef_shape,
            pltpu.VMEM((rank, samples), bf16),
            pltpu.VMEM((high, LANES), jnp.int32),
            pltpu.VMEM((ROWS, LANES), jnp.int32),
            pltpu.VMEM(link_blocks.shape, bf16),
        ],
        scratch_shapes=[
            pltpu.VMEM((1, clusters), jnp.int32),
            pltpu.VMEM((ROWS, rank), f32),
            pltpu.VMEM((high, LANES), bf16),
            pltpu.VMEM((high, LANES), f32),
            pltpu.VMEM((SLOTS, COPY, rank), bf16),
            pltpu.SemaphoreType.DMA((3,)),
            pltpu.SemaphoreType.DMA((SLOTS,)),
            pltpu.SemaphoreType.DMA((per_dev,)),
        ],
        compiler_params=params,
        name="coef_pass",
    )(far(slot_row), far(assign), far(vector), far(basis_rows), far(link_blocks))

    def to_all(block):
        copies = jnp.broadcast_to(block[None], (devices,) + block.shape)
        return lax.all_to_all(copies, "dev", 0, 0, tiled=True)

    def permute(block, pairs):
        return lax.ppermute(block, "dev", pairs)

    def to_chips(mixed):
        sibling = permute(mixed, [(i ^ 1, i) for i in range(devices)])
        own = jnp.concatenate([mixed, sibling], axis=0)
        behind = permute(own, [((i - 2) % devices, i) for i in range(devices)])
        ahead = permute(own, [((i + 2) % devices, i) for i in range(devices)])
        return behind, own, ahead

    def mix(coef):
        return pl.pallas_call(
            functools.partial(link_kernel, norm, devices, per_dev),
            in_specs=[smem, smem, vmem, vmem],
            out_specs=vmem,
            out_shape=jax.ShapeDtypeStruct((per_dev, rank), bf16),
            scratch_shapes=[
                pltpu.VMEM((clusters, rank), f32),
                pltpu.VMEM((per_dev * n_links // 2, rank), f32),
                pltpu.VMEM((8, rank), f32),
            ],
            compiler_params=params,
            name="link_product",
        )(slot_of, partners, to_all(coef), close(links_v))

    first, coef2 = pl.pallas_call(
        functools.partial(both_kernel, per_dev),
        in_specs=[vmem] * 7 + [hbm],
        out_specs=[vmem, vmem],
        out_shape=[pltpu.VMEM((high, LANES), f32), coef_shape],
        scratch_shapes=[
            pltpu.VMEM((ROWS, rank), f32),
            pltpu.VMEM((ROWS, rank), f32),
            pltpu.VMEM((high, LANES), f32),
            pltpu.VMEM((ROWS, TILE), f32),
            pltpu.VMEM((ROWS, TILE), f32),
            pltpu.VMEM((ROWS, TILE), bf16),
            pltpu.VMEM((ROWS, TILE), bf16),
            pltpu.VMEM((SLOTS, COPY, rank), bf16),
            pltpu.SemaphoreType.DMA((SLOTS,)),
        ],
        compiler_params=params,
        name="first_and_coef_pass",
    )(close(cl_v), *to_chips(mix(coef1)), close(assign_v), scores, close(turned_v), far(basis_rows))

    out = pl.pallas_call(
        functools.partial(last_kernel, per_dev),
        in_specs=[vmem] * 7,
        out_specs=vmem,
        out_shape=jax.ShapeDtypeStruct((high, LANES), f32),
        scratch_shapes=[
            pltpu.VMEM((ROWS, rank), f32),
        ],
        compiler_params=params,
        name="last_pass",
    )(close(cl_v), *to_chips(mix(coef2)), close(assign_v), close(first), close(turned_v))
    return out.reshape(samples)


def solution(mesh):
    in_specs = (
        P(("groups", "dev"), None),
        P(("groups", "dev")),
        P(("groups", "dev")),
        P(("groups", "dev")),
        P("groups"),
        P(("groups", "dev"), None),
        P(("groups", "dev"), None, None, None),
    )
    out_specs = P(("groups", "dev"))
    return jax.shard_map(shards, mesh=mesh, in_specs=in_specs, out_specs=out_specs, check_vma=False)
```

```python
import functools
import math

import jax
import jax.numpy as jnp
from jax import lax
from jax.experimental import pallas as pl
from jax.experimental.pallas import tpu as pltpu
from jax.sharding import PartitionSpec as P

REACH = 2
NEAR = 2 * REACH + 1
CL_DEV = 4
S_DEV = 65536
LANES = 128
ROWS = 24

COPY = 8192
TILE = 2048
PER_COPY = COPY // TILE
SLOTS = 4
BODY = 16
PIECE = 512
GROUP = 8

ridge = 0.5


def near_clusters(devices, per_dev, slot_of_ref, cl_ref):
    clusters = devices * per_dev
    me = lax.axis_index("dev")
    near = lax.broadcasted_iota(jnp.int32, (ROWS, clusters), 0)
    slots = (me + devices - REACH) * per_dev + near
    slots = lax.rem(slots, clusters)
    number = lax.broadcasted_iota(jnp.int32, (ROWS, clusters), 1)
    hit = (slot_of_ref[...] == slots) & (near < NEAR * per_dev)
    found = jnp.sum(jnp.where(hit, number + 1, 0), axis=1, keepdims=True) - 1
    cl_ref[...] = jnp.broadcast_to(found, cl_ref.shape)


def near_rows(per_dev, chips, rows_ref):
    even_core = lax.rem(lax.axis_index("dev"), 2) == 0
    chips = [chip[...].astype(jnp.float32) for chip in chips]
    rows_ref[...] = jnp.zeros_like(rows_ref)
    for g in range(NEAR):
        if g % 2 == 0:
            rows = chips[g // 2][:per_dev, :]
        else:
            rows = jnp.where(even_core, chips[g // 2][per_dev:, :], chips[g // 2 + 1][per_dev:, :])
        rows_ref[g * per_dev : (g + 1) * per_dev, :] = rows


def put_sums(per_dev, sum_ref, out_ref):
    for g in range(NEAR):
        out_ref[:, g * LANES : (g + 1) * LANES] = sum_ref[g * per_dev : (g + 1) * per_dev, :].astype(jnp.bfloat16)


def slot_copy(basis_hbm, slots_ref, sem, c):
    slot = lax.rem(c, SLOTS)
    rows = pl.ds(pl.multiple_of(c * COPY, COPY), COPY)
    return pltpu.make_async_copy(basis_hbm.at[rows, :], slots_ref.at[slot], sem.at[slot])


def tile_at(t):
    return pl.ds(pl.multiple_of(t * TILE, TILE), TILE)


def row_at(t, i):
    return pl.ds(t * (TILE // LANES) + i, 1)


def coef_kernel(
    devices, per_dev, slot_of_hbm, assign_hbm, vector_hbm, basis_hbm, links_hbm,
    out_ref, turned_ref, assign_ref, cl_ref, links_ref,
    slot_of_ref, sum_ref, vector_ref, x_ref, slots_ref, small_sem, basis_sem, links_sem,
):
    copies = basis_hbm.shape[0] // COPY

    def basis_copy(c):
        return slot_copy(basis_hbm, slots_ref, basis_sem, c)

    def links_copy(j):
        return pltpu.make_async_copy(links_hbm.at[j], links_ref.at[j], links_sem.at[j])

    slot_of_copy = pltpu.make_async_copy(slot_of_hbm, slot_of_ref, small_sem.at[2])
    assign_copy = pltpu.make_async_copy(assign_hbm, assign_ref, small_sem.at[0])
    vector_copy = pltpu.make_async_copy(vector_hbm, vector_ref, small_sem.at[1])
    slot_of_copy.start()
    assign_copy.start()
    vector_copy.start()
    for c in range(SLOTS):
        basis_copy(c).start()
    slot_of_copy.wait()
    near_clusters(devices, per_dev, slot_of_ref, cl_ref)
    sum_ref[...] = jnp.zeros_like(sum_ref)
    assign_copy.wait()
    vector_copy.wait()
    x_ref[...] = vector_ref[...].astype(jnp.float32)
    cl = cl_ref[...]

    @pl.loop(0, copies)
    def _(c):
        basis_copy(c).wait()

        @pl.when(c < per_dev)
        def _():
            links_copy(c).start()

        total = sum_ref[...]
        for p in range(PER_COPY):
            t = c * PER_COPY + p
            parts = []
            for i in range(TILE // LANES):
                hit = assign_ref[row_at(t, i), :] == cl
                parts.append(jnp.where(hit, x_ref[row_at(t, i), :], 0.0).astype(jnp.bfloat16))
            left = jnp.concatenate(parts, axis=1)
            block = slots_ref[lax.rem(c, SLOTS), p * TILE : (p + 1) * TILE, :]
            turned_ref[:, tile_at(t)] = block.T
            total += jnp.dot(left, block, preferred_element_type=jnp.float32)
        sum_ref[...] = total

        @pl.when(c + SLOTS < copies)
        def _():
            basis_copy(c + SLOTS).start()

    put_sums(per_dev, sum_ref, out_ref)
    for j in range(per_dev):
        links_copy(j).wait()


def link_kernel(
    norm, devices, per_dev, slot_of_ref, partners_ref, parts_ref, links_ref, out_ref, scaled_ref, picked_ref, mixed_ref
):
    n_links, rank = links_ref.shape[1:3]
    step = 2 * GROUP
    for owner in range(devices):
        coef = parts_ref[(owner + REACH) % devices, :, :LANES].astype(jnp.float32)
        for g in range(1, NEAR):
            coef += parts_ref[(owner + REACH - g) % devices, :, g * LANES : (g + 1) * LANES].astype(jnp.float32)
        scaled_ref[owner * per_dev : (owner + 1) * per_dev, :] = (coef * norm).astype(jnp.bfloat16).astype(jnp.float32)

    def partner(j, k):
        return scaled_ref[pl.ds(slot_of_ref[partners_ref[j, k]], 1), :]

    row = lax.broadcasted_iota(jnp.int32, (GROUP, rank), 0)
    mixed_ref[...] = jnp.zeros_like(mixed_ref)
    for j in range(per_dev):
        acc = jnp.zeros((rank, rank), jnp.float32)
        few = jnp.zeros((GROUP, rank), jnp.float32)
        for k in range(0, n_links, step):
            at = (j * n_links + k) // 2
            for u in range(GROUP):
                picked_ref[at + u : at + u + 1, :] = partner(j, k + GROUP + u)
            blocks = links_ref[j, k + GROUP : k + step].reshape(GROUP * rank, rank)
            picked = picked_ref[at : at + GROUP, :].astype(jnp.bfloat16)
            products = lax.dot_general(picked, blocks, (((1,), (1,)), ((), ())), preferred_element_type=jnp.float32)
            for u in range(GROUP):
                acc += links_ref[j, k + u].astype(jnp.float32) * partner(j, k + u)
            for u in range(GROUP):
                few += jnp.where(row == u, products[:, u * rank : (u + 1) * rank], 0.0)
        mixed_ref[j : j + 1, :] = jnp.sum(acc.T, axis=0, keepdims=True) + jnp.sum(few, axis=0, keepdims=True)
    out_ref[...] = mixed_ref[:per_dev, :].astype(jnp.bfloat16)


def own_product(hit, products):
    return jnp.sum(jnp.where(hit, products, 0.0), axis=0, keepdims=True)


def prepare_kernel(after_ref, scores_hbm, basis_hbm, slope_ref, head_ref, scores_ref, sems):
    scores_copy = pltpu.make_async_copy(scores_hbm, scores_ref, sems.at[0])
    head_copy = pltpu.make_async_copy(basis_hbm.at[pl.ds(0, COPY), :], head_ref, sems.at[1])
    scores_copy.start()
    head_copy.start()
    scores_copy.wait()
    sig = jax.nn.sigmoid(scores_ref[...])
    slope_ref[...] = sig * (1.0 - sig)
    head_copy.wait()


def both_kernel(
    per_dev, cl_ref, behind_ref, own_ref, ahead_ref, assign_ref, slope_ref, head_ref, turned_ref, basis_hbm,
    first_ref, out_ref, rows_ref, sum_ref, even_ref, odd_ref, even_left, odd_left, slots_ref, basis_sem,
):
    tiles = turned_ref.shape[1] // TILE
    copies = tiles // PER_COPY

    def basis_copy(c):
        return slot_copy(basis_hbm, slots_ref, basis_sem, c)

    for c in range(1, SLOTS + 1):
        basis_copy(c).start()
    near_rows(per_dev, (behind_ref, own_ref, ahead_ref), rows_ref)
    sum_ref[...] = jnp.zeros_like(sum_ref)
    cl = cl_ref[...]
    rows = rows_ref[...].astype(jnp.bfloat16)
    products_of = (even_ref, odd_ref)
    left_of = (even_left, odd_left)

    def multiply(t, side):
        products_of[side][...] = jnp.dot(rows, turned_ref[:, tile_at(t)], preferred_element_type=jnp.float32)

    def select(t, side):
        for i in range(TILE // LANES):
            at = slice(i * LANES, (i + 1) * LANES)
            hit = assign_ref[row_at(t, i), :] == cl
            first = own_product(hit, products_of[side][:, at])
            first_ref[row_at(t, i), :] = first
            weighted = slope_ref[row_at(t, i), :] * first
            left_of[side][:, at] = jnp.where(hit, weighted, 0.0).astype(jnp.bfloat16)

    def add_up(c, p):
        at = slice(p * TILE, (p + 1) * TILE)
        block = head_ref[at, :] if isinstance(c, int) and c == 0 else slots_ref[lax.rem(c, SLOTS), at, :]
        sum_ref[...] += jnp.dot(left_of[p % 2][...], block, preferred_element_type=jnp.float32)

    def body(c):
        for p in range(PER_COPY):
            t = c * PER_COPY + p
            add_up(c, p)
            multiply(t + 2, p % 2)
            select(t + 1, (p + 1) % 2)

    multiply(0, 0)
    select(0, 0)
    multiply(1, 1)
    body(0)

    @pl.loop(1, copies - 1)
    def _(c):
        basis_copy(c).wait()
        body(c)

        @pl.when(c + SLOTS < copies)
        def _():
            basis_copy(c + SLOTS).start()

    basis_copy(copies - 1).wait()
    for p in range(PER_COPY):
        t = (copies - 1) * PER_COPY + p
        add_up(copies - 1, p)
        if p + 2 < PER_COPY:
            multiply(t + 2, p % 2)
        if p + 1 < PER_COPY:
            select(t + 1, (p + 1) % 2)
    put_sums(per_dev, sum_ref, out_ref)


def last_kernel(
    per_dev, cl_ref, behind_ref, own_ref, ahead_ref, assign_ref, first_ref, turned_ref, out_ref, rows_ref
):
    near_rows(per_dev, (behind_ref, own_ref, ahead_ref), rows_ref)
    cl = cl_ref[...]
    rows = rows_ref[...].astype(jnp.bfloat16)

    @pl.loop(0, turned_ref.shape[1] // (BODY * TILE))
    def _(c):
        for piece in range(BODY * TILE // PIECE):
            at = pl.ds(pl.multiple_of(c * (BODY * TILE) + piece * PIECE, PIECE), PIECE)
            products = jnp.dot(rows, turned_ref[:, at], preferred_element_type=jnp.float32)
            for k in range(PIECE // LANES):
                row = row_at(c * BODY, piece * (PIECE // LANES) + k)
                hit = assign_ref[row, :] == cl
                second = own_product(hit, products[:, k * LANES : (k + 1) * LANES])
                out_ref[row, :] = second + ridge * first_ref[row, :]


def shards(basis_rows, vector, scores, assign, slot_of, partners, link_blocks):
    devices = lax.axis_size("dev")
    clusters = slot_of.shape[0]
    per_dev, n_links, rank, _ = link_blocks.shape
    samples = assign.shape[0]
    norm = 1.0 / math.sqrt(S_DEV // CL_DEV)
    high = samples // LANES
    f32, bf16 = jnp.float32, jnp.bfloat16

    vector = vector.reshape(high, LANES)
    scores = scores.reshape(high, LANES)
    assign = assign.reshape(high, LANES)
    slot_row = slot_of.reshape(1, clusters)

    far = lambda x: pltpu.with_memory_space_constraint(x, pltpu.HBM)
    close = lambda x: pltpu.with_memory_space_constraint(x, pltpu.VMEM)
    vmem = pl.BlockSpec(memory_space=pltpu.VMEM)
    smem = pl.BlockSpec(memory_space=pltpu.SMEM)
    hbm = pl.BlockSpec(memory_space=pltpu.HBM)
    coef_shape = jax.ShapeDtypeStruct((per_dev, NEAR * rank), bf16)
    params = pltpu.CompilerParams(vmem_limit_bytes=12 * 1024 * 1024)

    coef1, turned_v, assign_v, cl_v, links_v = pl.pallas_call(
        functools.partial(coef_kernel, devices, per_dev),
        in_specs=[hbm] * 5,
        out_specs=[vmem] * 5,
        out_shape=[
            coef_shape,
            pltpu.VMEM((rank, samples), bf16),
            pltpu.VMEM((high, LANES), jnp.int32),
            pltpu.VMEM((ROWS, LANES), jnp.int32),
            pltpu.VMEM(link_blocks.shape, bf16),
        ],
        scratch_shapes=[
            pltpu.VMEM((1, clusters), jnp.int32),
            pltpu.VMEM((ROWS, rank), f32),
            pltpu.VMEM((high, LANES), bf16),
            pltpu.VMEM((high, LANES), f32),
            pltpu.VMEM((SLOTS, COPY, rank), bf16),
            pltpu.SemaphoreType.DMA((3,)),
            pltpu.SemaphoreType.DMA((SLOTS,)),
            pltpu.SemaphoreType.DMA((per_dev,)),
        ],
        compiler_params=params,
        name="coef_pass",
    )(far(slot_row), far(assign), far(vector), far(basis_rows), far(link_blocks))

    def to_all(block):
        copies = jnp.broadcast_to(block[None], (devices,) + block.shape)
        return lax.all_to_all(copies, "dev", 0, 0, tiled=True)

    def permute(block, pairs):
        return lax.ppermute(block, "dev", pairs)

    def to_chips(mixed):
        sibling = permute(mixed, [(i ^ 1, i) for i in range(devices)])
        own = jnp.concatenate([mixed, sibling], axis=0)
        behind = permute(own, [((i - 2) % devices, i) for i in range(devices)])
        ahead = permute(own, [((i + 2) % devices, i) for i in range(devices)])
        return behind, own, ahead

    def mix(coef):
        return pl.pallas_call(
            functools.partial(link_kernel, norm, devices, per_dev),
            in_specs=[smem, smem, vmem, vmem],
            out_specs=vmem,
            out_shape=jax.ShapeDtypeStruct((per_dev, rank), bf16),
            scratch_shapes=[
                pltpu.VMEM((clusters, rank), f32),
                pltpu.VMEM((per_dev * n_links // 2, rank), f32),
                pltpu.VMEM((8, rank), f32),
            ],
            compiler_params=params,
            name="link_product",
        )(slot_of, partners, to_all(coef), close(links_v))

    chips1 = to_chips(mix(coef1))
    slope_v, head_v = pl.pallas_call(
        prepare_kernel,
        in_specs=[vmem, hbm, hbm],
        out_specs=[vmem, vmem],
        out_shape=[pltpu.VMEM((high, LANES), f32), pltpu.VMEM((COPY, rank), bf16)],
        scratch_shapes=[pltpu.VMEM((high, LANES), f32), pltpu.SemaphoreType.DMA((2,))],
        compiler_params=params,
        cost_estimate=pl.CostEstimate(flops=0, bytes_accessed=4 * COPY * rank, transcendentals=samples),
        name="prepare",
    )(chips1[1], far(scores), far(basis_rows))

    first, coef2 = pl.pallas_call(
        functools.partial(both_kernel, per_dev),
        in_specs=[vmem] * 8 + [hbm],
        out_specs=[vmem, vmem],
        out_shape=[pltpu.VMEM((high, LANES), f32), coef_shape],
        scratch_shapes=[
            pltpu.VMEM((ROWS, rank), f32),
            pltpu.VMEM((ROWS, rank), f32),
            pltpu.VMEM((ROWS, TILE), f32),
            pltpu.VMEM((ROWS, TILE), f32),
            pltpu.VMEM((ROWS, TILE), bf16),
            pltpu.VMEM((ROWS, TILE), bf16),
            pltpu.VMEM((SLOTS, COPY, rank), bf16),
            pltpu.SemaphoreType.DMA((SLOTS,)),
        ],
        compiler_params=params,
        name="first_and_coef_pass",
    )(close(cl_v), *chips1, close(assign_v), close(slope_v), close(head_v), close(turned_v), far(basis_rows))

    out = pl.pallas_call(
        functools.partial(last_kernel, per_dev),
        in_specs=[vmem] * 7,
        out_specs=vmem,
        out_shape=jax.ShapeDtypeStruct((high, LANES), f32),
        scratch_shapes=[
            pltpu.VMEM((ROWS, rank), f32),
        ],
        compiler_params=params,
        name="last_pass",
    )(close(cl_v), *to_chips(mix(coef2)), close(assign_v), close(first), close(turned_v))
    return out.reshape(samples)


def solution(mesh):
    in_specs = (
        P(("groups", "dev"), None),
        P(("groups", "dev")),
        P(("groups", "dev")),
        P(("groups", "dev")),
        P("groups"),
        P(("groups", "dev"), None),
        P(("groups", "dev"), None, None, None),
    )
    out_specs = P(("groups", "dev"))
    return jax.shard_map(shards, mesh=mesh, in_specs=in_specs, out_specs=out_specs, check_vma=False)
```

```python
import functools
import math

import jax
import jax.numpy as jnp
from jax import lax
from jax.experimental import pallas as pl
from jax.experimental.pallas import tpu as pltpu
from jax.sharding import PartitionSpec as P

REACH = 2
NEAR = 2 * REACH + 1
CL_DEV = 4
S_DEV = 65536
LANES = 128
ROWS = 24

COPY = 8192
TILE = 2048
PER_COPY = COPY // TILE
SLOTS = 4
BODY = 16
PIECE = 512
GROUP = 8
LINKS = 32

ridge = 0.5


def near_clusters(devices, per_dev, slot_of_ref, cl_ref):
    clusters = devices * per_dev
    me = lax.axis_index("dev")
    near = lax.broadcasted_iota(jnp.int32, (ROWS, clusters), 0)
    slots = (me + devices - REACH) * per_dev + near
    slots = lax.rem(slots, clusters)
    number = lax.broadcasted_iota(jnp.int32, (ROWS, clusters), 1)
    hit = (slot_of_ref[...] == slots) & (near < NEAR * per_dev)
    found = jnp.sum(jnp.where(hit, number + 1, 0), axis=1, keepdims=True) - 1
    cl_ref[...] = jnp.broadcast_to(found, cl_ref.shape)


def near_rows(per_dev, chips, rows_ref):
    even_core = lax.rem(lax.axis_index("dev"), 2) == 0
    chips = [chip[...].astype(jnp.float32) for chip in chips]
    rows_ref[...] = jnp.zeros_like(rows_ref)
    for g in range(NEAR):
        if g % 2 == 0:
            rows = chips[g // 2][:per_dev, :]
        else:
            rows = jnp.where(even_core, chips[g // 2][per_dev:, :], chips[g // 2 + 1][per_dev:, :])
        rows_ref[g * per_dev : (g + 1) * per_dev, :] = rows


def put_sums(per_dev, sum_ref, out_ref):
    for g in range(NEAR):
        out_ref[:, g * LANES : (g + 1) * LANES] = sum_ref[g * per_dev : (g + 1) * per_dev, :].astype(jnp.bfloat16)


def slot_copy(basis_hbm, slots_ref, sem, c):
    slot = lax.rem(c, SLOTS)
    rows = pl.ds(pl.multiple_of(c * COPY, COPY), COPY)
    return pltpu.make_async_copy(basis_hbm.at[rows, :], slots_ref.at[slot], sem.at[slot])


def tile_at(t):
    return pl.ds(pl.multiple_of(t * TILE, TILE), TILE)


def row_at(t, i):
    return pl.ds(t * (TILE // LANES) + i, 1)


def coef_kernel(
    devices, per_dev, slot_of_hbm, assign_hbm, vector_hbm, basis_hbm, links_hbm,
    out_ref, turned_ref, assign_ref, cl_ref, links_ref,
    slot_of_ref, sum_ref, vector_ref, x_ref, slots_ref, small_sem, basis_sem, links_sem,
):
    copies = basis_hbm.shape[0] // COPY

    def basis_copy(c):
        return slot_copy(basis_hbm, slots_ref, basis_sem, c)

    def links_copy(j):
        return pltpu.make_async_copy(links_hbm.at[j], links_ref.at[j], links_sem.at[j])

    slot_of_copy = pltpu.make_async_copy(slot_of_hbm, slot_of_ref, small_sem.at[2])
    assign_copy = pltpu.make_async_copy(assign_hbm, assign_ref, small_sem.at[0])
    vector_copy = pltpu.make_async_copy(vector_hbm, vector_ref, small_sem.at[1])
    slot_of_copy.start()
    assign_copy.start()
    vector_copy.start()
    for c in range(SLOTS):
        basis_copy(c).start()
    slot_of_copy.wait()
    near_clusters(devices, per_dev, slot_of_ref, cl_ref)
    sum_ref[...] = jnp.zeros_like(sum_ref)
    assign_copy.wait()
    vector_copy.wait()
    x_ref[...] = vector_ref[...].astype(jnp.float32)
    cl = cl_ref[...]

    @pl.loop(0, copies)
    def _(c):
        basis_copy(c).wait()

        @pl.when(c < links_ref.shape[0])
        def _():
            links_copy(c).start()

        total = sum_ref[...]
        for p in range(PER_COPY):
            t = c * PER_COPY + p
            parts = []
            for i in range(TILE // LANES):
                hit = assign_ref[row_at(t, i), :] == cl
                parts.append(jnp.where(hit, x_ref[row_at(t, i), :], 0.0).astype(jnp.bfloat16))
            left = jnp.concatenate(parts, axis=1)
            block = slots_ref[lax.rem(c, SLOTS), p * TILE : (p + 1) * TILE, :]
            turned_ref[:, tile_at(t)] = block.T
            total += jnp.dot(left, block, preferred_element_type=jnp.float32)
        sum_ref[...] = total

        @pl.when(c + SLOTS < copies)
        def _():
            basis_copy(c + SLOTS).start()

    put_sums(per_dev, sum_ref, out_ref)
    for j in range(links_ref.shape[0]):
        links_copy(j).wait()


def link_kernel(norm, devices, per_dev, first_time, slot_of_ref, partners_ref, parts_ref, links1_ref, *refs):
    if first_time:
        links_hbm, out_ref, links2_ref, scaled_ref, picked_ref, mixed_ref, links_sem = refs
    else:
        links2_ref, out_ref, scaled_ref, picked_ref, mixed_ref = refs
    n_links, rank = links1_ref.shape[1:3]
    step = 2 * GROUP
    half = per_dev // 2

    def piece_copy(j, k):
        ks = pl.ds(k, LINKS)
        sem = links_sem.at[((j - half) * n_links + k) // LINKS]
        return pltpu.make_async_copy(links_hbm.at[j, ks], links2_ref.at[j - half, ks], sem)

    if first_time:
        for j in range(half, per_dev):
            for k in range(0, n_links, LINKS):
                piece_copy(j, k).start()
    for owner in range(devices):
        coef = parts_ref[(owner + REACH) % devices, :, :LANES].astype(jnp.float32)
        for g in range(1, NEAR):
            coef += parts_ref[(owner + REACH - g) % devices, :, g * LANES : (g + 1) * LANES].astype(jnp.float32)
        scaled_ref[owner * per_dev : (owner + 1) * per_dev, :] = (coef * norm).astype(jnp.bfloat16).astype(jnp.float32)

    def partner(j, k):
        return scaled_ref[pl.ds(slot_of_ref[partners_ref[j, k]], 1), :]

    row = lax.broadcasted_iota(jnp.int32, (GROUP, rank), 0)
    mixed_ref[...] = jnp.zeros_like(mixed_ref)
    for j in range(per_dev):
        acc = jnp.zeros((rank, rank), jnp.float32)
        few = jnp.zeros((GROUP, rank), jnp.float32)
        links_ref = links1_ref.at[j] if j < half else links2_ref.at[j - half]
        for k in range(0, n_links, step):
            if first_time and j >= half and k % LINKS == 0:
                piece_copy(j, k).wait()
            at = (j * n_links + k) // 2
            for u in range(GROUP):
                picked_ref[at + u : at + u + 1, :] = partner(j, k + GROUP + u)
            blocks = links_ref[k + GROUP : k + step].reshape(GROUP * rank, rank)
            picked = picked_ref[at : at + GROUP, :].astype(jnp.bfloat16)
            products = lax.dot_general(picked, blocks, (((1,), (1,)), ((), ())), preferred_element_type=jnp.float32)
            for u in range(GROUP):
                acc += links_ref[k + u].astype(jnp.float32) * partner(j, k + u)
            for u in range(GROUP):
                few += jnp.where(row == u, products[:, u * rank : (u + 1) * rank], 0.0)
        mixed_ref[j : j + 1, :] = jnp.sum(acc.T, axis=0, keepdims=True) + jnp.sum(few, axis=0, keepdims=True)
    out_ref[...] = mixed_ref[:per_dev, :].astype(jnp.bfloat16)


def own_product(hit, products):
    return jnp.sum(jnp.where(hit, products, 0.0), axis=0, keepdims=True)


def prepare_kernel(after_ref, scores_hbm, basis_hbm, slope_ref, head_ref, scores_ref, sems):
    scores_copy = pltpu.make_async_copy(scores_hbm, scores_ref, sems.at[0])
    head_copy = pltpu.make_async_copy(basis_hbm.at[pl.ds(0, COPY), :], head_ref, sems.at[1])
    scores_copy.start()
    head_copy.start()
    scores_copy.wait()
    sig = jax.nn.sigmoid(scores_ref[...])
    slope_ref[...] = sig * (1.0 - sig)
    head_copy.wait()


def both_kernel(
    per_dev, cl_ref, behind_ref, own_ref, ahead_ref, assign_ref, slope_ref, head_ref, turned_ref, basis_hbm,
    first_ref, out_ref, rows_ref, sum_ref, even_ref, odd_ref, even_left, odd_left, slots_ref, basis_sem,
):
    tiles = turned_ref.shape[1] // TILE
    copies = tiles // PER_COPY

    def basis_copy(c):
        return slot_copy(basis_hbm, slots_ref, basis_sem, c)

    for c in range(1, SLOTS + 1):
        basis_copy(c).start()
    near_rows(per_dev, (behind_ref, own_ref, ahead_ref), rows_ref)
    sum_ref[...] = jnp.zeros_like(sum_ref)
    cl = cl_ref[...]
    rows = rows_ref[...].astype(jnp.bfloat16)
    products_of = (even_ref, odd_ref)
    left_of = (even_left, odd_left)

    def multiply(t, side):
        products_of[side][...] = jnp.dot(rows, turned_ref[:, tile_at(t)], preferred_element_type=jnp.float32)

    def select(t, side):
        for i in range(TILE // LANES):
            at = slice(i * LANES, (i + 1) * LANES)
            hit = assign_ref[row_at(t, i), :] == cl
            first = own_product(hit, products_of[side][:, at])
            first_ref[row_at(t, i), :] = first
            weighted = slope_ref[row_at(t, i), :] * first
            left_of[side][:, at] = jnp.where(hit, weighted, 0.0).astype(jnp.bfloat16)

    def add_up(c, p):
        at = slice(p * TILE, (p + 1) * TILE)
        block = head_ref[at, :] if isinstance(c, int) and c == 0 else slots_ref[lax.rem(c, SLOTS), at, :]
        sum_ref[...] += jnp.dot(left_of[p % 2][...], block, preferred_element_type=jnp.float32)

    def body(c):
        for p in range(PER_COPY):
            t = c * PER_COPY + p
            add_up(c, p)
            multiply(t + 2, p % 2)
            select(t + 1, (p + 1) % 2)

    multiply(0, 0)
    select(0, 0)
    multiply(1, 1)
    body(0)

    @pl.loop(1, copies - 1)
    def _(c):
        basis_copy(c).wait()
        body(c)

        @pl.when(c + SLOTS < copies)
        def _():
            basis_copy(c + SLOTS).start()

    basis_copy(copies - 1).wait()
    for p in range(PER_COPY):
        t = (copies - 1) * PER_COPY + p
        add_up(copies - 1, p)
        if p + 2 < PER_COPY:
            multiply(t + 2, p % 2)
        if p + 1 < PER_COPY:
            select(t + 1, (p + 1) % 2)
    put_sums(per_dev, sum_ref, out_ref)


def last_kernel(
    per_dev, cl_ref, behind_ref, own_ref, ahead_ref, assign_ref, first_ref, turned_ref, out_ref, rows_ref
):
    near_rows(per_dev, (behind_ref, own_ref, ahead_ref), rows_ref)
    cl = cl_ref[...]
    rows = rows_ref[...].astype(jnp.bfloat16)

    @pl.loop(0, turned_ref.shape[1] // (BODY * TILE))
    def _(c):
        for piece in range(BODY * TILE // PIECE):
            at = pl.ds(pl.multiple_of(c * (BODY * TILE) + piece * PIECE, PIECE), PIECE)
            products = jnp.dot(rows, turned_ref[:, at], preferred_element_type=jnp.float32)
            for k in range(PIECE // LANES):
                row = row_at(c * BODY, piece * (PIECE // LANES) + k)
                hit = assign_ref[row, :] == cl
                second = own_product(hit, products[:, k * LANES : (k + 1) * LANES])
                out_ref[row, :] = second + ridge * first_ref[row, :]


def shards(basis_rows, vector, scores, assign, slot_of, partners, link_blocks):
    devices = lax.axis_size("dev")
    clusters = slot_of.shape[0]
    per_dev, n_links, rank, _ = link_blocks.shape
    samples = assign.shape[0]
    norm = 1.0 / math.sqrt(S_DEV // CL_DEV)
    high = samples // LANES
    f32, bf16 = jnp.float32, jnp.bfloat16

    vector = vector.reshape(high, LANES)
    scores = scores.reshape(high, LANES)
    assign = assign.reshape(high, LANES)
    slot_row = slot_of.reshape(1, clusters)

    far = lambda x: pltpu.with_memory_space_constraint(x, pltpu.HBM)
    close = lambda x: pltpu.with_memory_space_constraint(x, pltpu.VMEM)
    vmem = pl.BlockSpec(memory_space=pltpu.VMEM)
    smem = pl.BlockSpec(memory_space=pltpu.SMEM)
    hbm = pl.BlockSpec(memory_space=pltpu.HBM)
    half_shape = (per_dev // 2,) + link_blocks.shape[1:]
    coef_shape = jax.ShapeDtypeStruct((per_dev, NEAR * rank), bf16)
    params = pltpu.CompilerParams(vmem_limit_bytes=12 * 1024 * 1024)

    coef1, turned_v, assign_v, cl_v, links1_v = pl.pallas_call(
        functools.partial(coef_kernel, devices, per_dev),
        in_specs=[hbm] * 5,
        out_specs=[vmem] * 5,
        out_shape=[
            coef_shape,
            pltpu.VMEM((rank, samples), bf16),
            pltpu.VMEM((high, LANES), jnp.int32),
            pltpu.VMEM((ROWS, LANES), jnp.int32),
            pltpu.VMEM(half_shape, bf16),
        ],
        scratch_shapes=[
            pltpu.VMEM((1, clusters), jnp.int32),
            pltpu.VMEM((ROWS, rank), f32),
            pltpu.VMEM((high, LANES), bf16),
            pltpu.VMEM((high, LANES), f32),
            pltpu.VMEM((SLOTS, COPY, rank), bf16),
            pltpu.SemaphoreType.DMA((3,)),
            pltpu.SemaphoreType.DMA((SLOTS,)),
            pltpu.SemaphoreType.DMA((per_dev // 2,)),
        ],
        compiler_params=params,
        name="coef_pass",
    )(far(slot_row), far(assign), far(vector), far(basis_rows), far(link_blocks))

    def to_all(block):
        copies = jnp.broadcast_to(block[None], (devices,) + block.shape)
        return lax.all_to_all(copies, "dev", 0, 0, tiled=True)

    def permute(block, pairs):
        return lax.ppermute(block, "dev", pairs)

    def to_chips(mixed):
        sibling = permute(mixed, [(i ^ 1, i) for i in range(devices)])
        own = jnp.concatenate([mixed, sibling], axis=0)
        behind = permute(own, [((i - 2) % devices, i) for i in range(devices)])
        ahead = permute(own, [((i + 2) % devices, i) for i in range(devices)])
        return behind, own, ahead

    def mix(coef, links2, first_time):
        return pl.pallas_call(
            functools.partial(link_kernel, norm, devices, per_dev, first_time),
            in_specs=[smem, smem, vmem, vmem, hbm if first_time else vmem],
            out_specs=[vmem, vmem] if first_time else [vmem],
            out_shape=[jax.ShapeDtypeStruct((per_dev, rank), bf16)] + [pltpu.VMEM(half_shape, bf16)] * first_time,
            scratch_shapes=[
                pltpu.VMEM((clusters, rank), f32),
                pltpu.VMEM((per_dev * n_links // 2, rank), f32),
                pltpu.VMEM((8, rank), f32),
            ]
            + [pltpu.SemaphoreType.DMA(((per_dev - per_dev // 2) * n_links // LINKS,))] * first_time,
            compiler_params=params,
            name="link_product",
        )(slot_of, partners, to_all(coef), close(links1_v), links2)

    mixed1, links2_v = mix(coef1, far(link_blocks), True)
    chips1 = to_chips(mixed1)
    slope_v, head_v = pl.pallas_call(
        prepare_kernel,
        in_specs=[vmem, hbm, hbm],
        out_specs=[vmem, vmem],
        out_shape=[pltpu.VMEM((high, LANES), f32), pltpu.VMEM((COPY, rank), bf16)],
        scratch_shapes=[pltpu.VMEM((high, LANES), f32), pltpu.SemaphoreType.DMA((2,))],
        compiler_params=params,
        cost_estimate=pl.CostEstimate(flops=0, bytes_accessed=4 * COPY * rank, transcendentals=samples),
        name="prepare",
    )(chips1[1], far(scores), far(basis_rows))

    first, coef2 = pl.pallas_call(
        functools.partial(both_kernel, per_dev),
        in_specs=[vmem] * 8 + [hbm],
        out_specs=[vmem, vmem],
        out_shape=[pltpu.VMEM((high, LANES), f32), coef_shape],
        scratch_shapes=[
            pltpu.VMEM((ROWS, rank), f32),
            pltpu.VMEM((ROWS, rank), f32),
            pltpu.VMEM((ROWS, TILE), f32),
            pltpu.VMEM((ROWS, TILE), f32),
            pltpu.VMEM((ROWS, TILE), bf16),
            pltpu.VMEM((ROWS, TILE), bf16),
            pltpu.VMEM((SLOTS, COPY, rank), bf16),
            pltpu.SemaphoreType.DMA((SLOTS,)),
        ],
        compiler_params=params,
        name="first_and_coef_pass",
    )(close(cl_v), *chips1, close(assign_v), close(slope_v), close(head_v), close(turned_v), far(basis_rows))

    (mixed2,) = mix(coef2, close(links2_v), False)
    out = pl.pallas_call(
        functools.partial(last_kernel, per_dev),
        in_specs=[vmem] * 7,
        out_specs=vmem,
        out_shape=jax.ShapeDtypeStruct((high, LANES), f32),
        scratch_shapes=[
            pltpu.VMEM((ROWS, rank), f32),
        ],
        compiler_params=params,
        name="last_pass",
    )(close(cl_v), *to_chips(mixed2), close(assign_v), close(first), close(turned_v))
    return out.reshape(samples)


def solution(mesh):
    in_specs = (
        P(("groups", "dev"), None),
        P(("groups", "dev")),
        P(("groups", "dev")),
        P(("groups", "dev")),
        P("groups"),
        P(("groups", "dev"), None),
        P(("groups", "dev"), None, None, None),
    )
    out_specs = P(("groups", "dev"))
    return jax.shard_map(shards, mesh=mesh, in_specs=in_specs, out_specs=out_specs, check_vma=False)
```

```python
import functools
import math

import jax
import jax.numpy as jnp
from jax import lax
from jax.experimental import pallas as pl
from jax.experimental.pallas import tpu as pltpu
from jax.sharding import PartitionSpec as P

REACH = 2
NEAR = 2 * REACH + 1
CL_DEV = 4
S_DEV = 65536
LANES = 128
ROWS = 24

COPY = 8192
TILE = 2048
PER_COPY = COPY // TILE
SLOTS = 4
BODY = 16
PIECE = 1024
GROUP = 8

ridge = 0.5


def near_clusters(devices, per_dev, slot_of_ref, cl_ref):
    clusters = devices * per_dev
    me = lax.axis_index("dev")
    near = lax.broadcasted_iota(jnp.int32, (ROWS, clusters), 0)
    slots = (me + devices - REACH) * per_dev + near
    slots = lax.rem(slots, clusters)
    number = lax.broadcasted_iota(jnp.int32, (ROWS, clusters), 1)
    hit = (slot_of_ref[...] == slots) & (near < NEAR * per_dev)
    found = jnp.sum(jnp.where(hit, number + 1, 0), axis=1, keepdims=True) - 1
    cl_ref[...] = jnp.broadcast_to(found, cl_ref.shape)


def near_rows(per_dev, chips, rows_ref):
    even_core = lax.rem(lax.axis_index("dev"), 2) == 0
    chips = [chip[...].astype(jnp.float32) for chip in chips]
    rows_ref[...] = jnp.zeros_like(rows_ref)
    for g in range(NEAR):
        if g % 2 == 0:
            rows = chips[g // 2][:per_dev, :]
        else:
            rows = jnp.where(even_core, chips[g // 2][per_dev:, :], chips[g // 2 + 1][per_dev:, :])
        rows_ref[g * per_dev : (g + 1) * per_dev, :] = rows


def put_sums(per_dev, sum_ref, out_ref):
    for g in range(NEAR):
        out_ref[:, g * LANES : (g + 1) * LANES] = sum_ref[g * per_dev : (g + 1) * per_dev, :].astype(jnp.bfloat16)


def slot_copy(basis_hbm, slots_ref, sem, c):
    slot = lax.rem(c, SLOTS)
    rows = pl.ds(pl.multiple_of(c * COPY, COPY), COPY)
    return pltpu.make_async_copy(basis_hbm.at[rows, :], slots_ref.at[slot], sem.at[slot])


def tile_at(t):
    return pl.ds(pl.multiple_of(t * TILE, TILE), TILE)


def row_at(t, i):
    return pl.ds(t * (TILE // LANES) + i, 1)


def coef_kernel(
    devices, per_dev, slot_of_hbm, assign_hbm, vector_hbm, basis_hbm, links_hbm,
    out_ref, turned_ref, assign_ref, cl_ref, links_ref,
    slot_of_ref, sum_ref, vector_ref, x_ref, slots_ref, small_sem, basis_sem, links_sem,
):
    copies = basis_hbm.shape[0] // COPY

    def basis_copy(c):
        return slot_copy(basis_hbm, slots_ref, basis_sem, c)

    links_from = copies - per_dev - 1

    def links_copy(j):
        return pltpu.make_async_copy(links_hbm.at[j], links_ref.at[j], links_sem.at[j])

    slot_of_copy = pltpu.make_async_copy(slot_of_hbm, slot_of_ref, small_sem.at[2])
    assign_copy = pltpu.make_async_copy(assign_hbm, assign_ref, small_sem.at[0])
    vector_copy = pltpu.make_async_copy(vector_hbm, vector_ref, small_sem.at[1])
    slot_of_copy.start()
    assign_copy.start()
    vector_copy.start()
    for c in range(SLOTS):
        basis_copy(c).start()
    slot_of_copy.wait()
    near_clusters(devices, per_dev, slot_of_ref, cl_ref)
    sum_ref[...] = jnp.zeros_like(sum_ref)
    assign_copy.wait()
    vector_copy.wait()
    x_ref[...] = vector_ref[...].astype(jnp.float32)
    cl = cl_ref[...]

    @pl.loop(0, copies)
    def _(c):
        basis_copy(c).wait()

        @pl.when((c >= links_from) & (c < links_from + per_dev))
        def _():
            links_copy(c - links_from).start()

        total = sum_ref[...]
        for p in range(PER_COPY):
            t = c * PER_COPY + p
            parts = []
            for i in range(TILE // LANES):
                hit = assign_ref[row_at(t, i), :] == cl
                parts.append(jnp.where(hit, x_ref[row_at(t, i), :], 0.0).astype(jnp.bfloat16))
            left = jnp.concatenate(parts, axis=1)
            block = slots_ref[lax.rem(c, SLOTS), p * TILE : (p + 1) * TILE, :]
            turned_ref[:, tile_at(t)] = block.T
            total += jnp.dot(left, block, preferred_element_type=jnp.float32)
        sum_ref[...] = total

        @pl.when(c + SLOTS < copies)
        def _():
            basis_copy(c + SLOTS).start()

    put_sums(per_dev, sum_ref, out_ref)
    for j in range(per_dev):
        links_copy(j).wait()


def link_kernel(
    norm, devices, per_dev, slot_of_ref, partners_ref, parts_ref, links_ref, out_ref, scaled_ref, picked_ref, mixed_ref
):
    n_links, rank = links_ref.shape[1:3]
    step = 2 * GROUP
    for owner in range(devices):
        coef = parts_ref[(owner + REACH) % devices, :, :LANES].astype(jnp.float32)
        for g in range(1, NEAR):
            coef += parts_ref[(owner + REACH - g) % devices, :, g * LANES : (g + 1) * LANES].astype(jnp.float32)
        scaled_ref[owner * per_dev : (owner + 1) * per_dev, :] = (coef * norm).astype(jnp.bfloat16).astype(jnp.float32)

    def partner(j, k):
        return scaled_ref[pl.ds(slot_of_ref[partners_ref[j, k]], 1), :]

    row = lax.broadcasted_iota(jnp.int32, (GROUP, rank), 0)
    mixed_ref[...] = jnp.zeros_like(mixed_ref)
    for j in range(per_dev):
        acc = jnp.zeros((rank, rank), jnp.float32)
        few = jnp.zeros((GROUP, rank), jnp.float32)
        for k in range(0, n_links, step):
            at = (j * n_links + k) // 2
            for u in range(GROUP):
                picked_ref[at + u : at + u + 1, :] = partner(j, k + GROUP + u)
            blocks = links_ref[j, k + GROUP : k + step].reshape(GROUP * rank, rank)
            picked = picked_ref[at : at + GROUP, :].astype(jnp.bfloat16)
            products = lax.dot_general(picked, blocks, (((1,), (1,)), ((), ())), preferred_element_type=jnp.float32)
            for u in range(GROUP):
                acc += links_ref[j, k + u].astype(jnp.float32) * partner(j, k + u)
            for u in range(GROUP):
                few += jnp.where(row == u, products[:, u * rank : (u + 1) * rank], 0.0)
        mixed_ref[j : j + 1, :] = jnp.sum(acc.T, axis=0, keepdims=True) + jnp.sum(few, axis=0, keepdims=True)
    out_ref[...] = mixed_ref[:per_dev, :].astype(jnp.bfloat16)


def own_product(hit, products):
    return jnp.sum(jnp.where(hit, products, 0.0), axis=0, keepdims=True)


def prepare_kernel(after_ref, scores_hbm, basis_hbm, slope_ref, head_ref, scores_ref, sems):
    scores_copy = pltpu.make_async_copy(scores_hbm, scores_ref, sems.at[0])
    head_copy = pltpu.make_async_copy(basis_hbm.at[pl.ds(0, COPY), :], head_ref, sems.at[1])
    scores_copy.start()
    head_copy.start()
    scores_copy.wait()
    sig = jax.nn.sigmoid(scores_ref[...])
    slope_ref[...] = sig * (1.0 - sig)
    head_copy.wait()


def both_kernel(
    per_dev, cl_ref, behind_ref, own_ref, ahead_ref, assign_ref, slope_ref, head_ref, turned_ref, basis_hbm,
    first_ref, out_ref, rows_ref, sum_ref, even_ref, odd_ref, even_left, odd_left, slots_ref, basis_sem,
):
    tiles = turned_ref.shape[1] // TILE
    copies = tiles // PER_COPY

    def basis_copy(c):
        return slot_copy(basis_hbm, slots_ref, basis_sem, c)

    for c in range(1, SLOTS + 1):
        basis_copy(c).start()
    near_rows(per_dev, (behind_ref, own_ref, ahead_ref), rows_ref)
    sum_ref[...] = jnp.zeros_like(sum_ref)
    cl = cl_ref[...]
    rows = rows_ref[...].astype(jnp.bfloat16)
    products_of = (even_ref, odd_ref)
    left_of = (even_left, odd_left)

    def multiply(t, side):
        products_of[side][...] = jnp.dot(rows, turned_ref[:, tile_at(t)], preferred_element_type=jnp.float32)

    def select(t, side):
        for i in range(TILE // LANES):
            at = slice(i * LANES, (i + 1) * LANES)
            hit = assign_ref[row_at(t, i), :] == cl
            first = own_product(hit, products_of[side][:, at])
            first_ref[row_at(t, i), :] = first
            weighted = slope_ref[row_at(t, i), :] * first
            left_of[side][:, at] = jnp.where(hit, weighted, 0.0).astype(jnp.bfloat16)

    def add_up(c, p):
        at = slice(p * TILE, (p + 1) * TILE)
        block = head_ref[at, :] if isinstance(c, int) and c == 0 else slots_ref[lax.rem(c, SLOTS), at, :]
        sum_ref[...] += jnp.dot(left_of[p % 2][...], block, preferred_element_type=jnp.float32)

    def body(c):
        for p in range(PER_COPY):
            t = c * PER_COPY + p
            add_up(c, p)
            multiply(t + 2, p % 2)
            select(t + 1, (p + 1) % 2)

    multiply(0, 0)
    select(0, 0)
    multiply(1, 1)
    body(0)

    @pl.loop(1, copies - 1)
    def _(c):
        basis_copy(c).wait()
        body(c)

        @pl.when(c + SLOTS < copies)
        def _():
            basis_copy(c + SLOTS).start()

    basis_copy(copies - 1).wait()
    for p in range(PER_COPY):
        t = (copies - 1) * PER_COPY + p
        add_up(copies - 1, p)
        if p + 2 < PER_COPY:
            multiply(t + 2, p % 2)
        if p + 1 < PER_COPY:
            select(t + 1, (p + 1) % 2)
    put_sums(per_dev, sum_ref, out_ref)


def last_kernel(
    per_dev, cl_ref, behind_ref, own_ref, ahead_ref, assign_ref, first_ref, turned_ref, out_ref, rows_ref
):
    near_rows(per_dev, (behind_ref, own_ref, ahead_ref), rows_ref)
    cl = cl_ref[...]
    rows = rows_ref[...].astype(jnp.bfloat16)

    @pl.loop(0, turned_ref.shape[1] // (BODY * TILE))
    def _(c):
        for piece in range(BODY * TILE // PIECE):
            at = pl.ds(pl.multiple_of(c * (BODY * TILE) + piece * PIECE, PIECE), PIECE)
            products = jnp.dot(rows, turned_ref[:, at], preferred_element_type=jnp.float32)
            for k in range(PIECE // LANES):
                row = row_at(c * BODY, piece * (PIECE // LANES) + k)
                hit = assign_ref[row, :] == cl
                second = own_product(hit, products[:, k * LANES : (k + 1) * LANES])
                out_ref[row, :] = second + ridge * first_ref[row, :]


def shards(basis_rows, vector, scores, assign, slot_of, partners, link_blocks):
    devices = lax.axis_size("dev")
    clusters = slot_of.shape[0]
    per_dev, n_links, rank, _ = link_blocks.shape
    samples = assign.shape[0]
    norm = 1.0 / math.sqrt(S_DEV // CL_DEV)
    high = samples // LANES
    f32, bf16 = jnp.float32, jnp.bfloat16

    vector = vector.reshape(high, LANES)
    scores = scores.reshape(high, LANES)
    assign = assign.reshape(high, LANES)
    slot_row = slot_of.reshape(1, clusters)

    far = lambda x: pltpu.with_memory_space_constraint(x, pltpu.HBM)
    close = lambda x: pltpu.with_memory_space_constraint(x, pltpu.VMEM)
    vmem = pl.BlockSpec(memory_space=pltpu.VMEM)
    smem = pl.BlockSpec(memory_space=pltpu.SMEM)
    hbm = pl.BlockSpec(memory_space=pltpu.HBM)
    coef_shape = jax.ShapeDtypeStruct((per_dev, NEAR * rank), bf16)
    params = pltpu.CompilerParams(vmem_limit_bytes=12 * 1024 * 1024)

    coef1, turned_v, assign_v, cl_v, links_v = pl.pallas_call(
        functools.partial(coef_kernel, devices, per_dev),
        in_specs=[hbm] * 5,
        out_specs=[vmem] * 5,
        out_shape=[
            coef_shape,
            pltpu.VMEM((rank, samples), bf16),
            pltpu.VMEM((high, LANES), jnp.int32),
            pltpu.VMEM((ROWS, LANES), jnp.int32),
            pltpu.VMEM(link_blocks.shape, bf16),
        ],
        scratch_shapes=[
            pltpu.VMEM((1, clusters), jnp.int32),
            pltpu.VMEM((ROWS, rank), f32),
            pltpu.VMEM((high, LANES), bf16),
            pltpu.VMEM((high, LANES), f32),
            pltpu.VMEM((SLOTS, COPY, rank), bf16),
            pltpu.SemaphoreType.DMA((3,)),
            pltpu.SemaphoreType.DMA((SLOTS,)),
            pltpu.SemaphoreType.DMA((per_dev,)),
        ],
        compiler_params=params,
        name="coef_pass",
    )(far(slot_row), far(assign), far(vector), far(basis_rows), far(link_blocks))

    def to_all(block):
        copies = jnp.broadcast_to(block[None], (devices,) + block.shape)
        return lax.all_to_all(copies, "dev", 0, 0, tiled=True)

    def permute(block, pairs):
        return lax.ppermute(block, "dev", pairs)

    def to_chips(mixed):
        sibling = permute(mixed, [(i ^ 1, i) for i in range(devices)])
        own = jnp.concatenate([mixed, sibling], axis=0)
        behind = permute(own, [((i - 2) % devices, i) for i in range(devices)])
        ahead = permute(own, [((i + 2) % devices, i) for i in range(devices)])
        return behind, own, ahead

    def mix(coef):
        return pl.pallas_call(
            functools.partial(link_kernel, norm, devices, per_dev),
            in_specs=[smem, smem, vmem, vmem],
            out_specs=vmem,
            out_shape=jax.ShapeDtypeStruct((per_dev, rank), bf16),
            scratch_shapes=[
                pltpu.VMEM((clusters, rank), f32),
                pltpu.VMEM((per_dev * n_links // 2, rank), f32),
                pltpu.VMEM((8, rank), f32),
            ],
            compiler_params=params,
            name="link_product",
        )(slot_of, partners, to_all(coef), close(links_v))

    chips1 = to_chips(mix(coef1))
    slope_v, head_v = pl.pallas_call(
        prepare_kernel,
        in_specs=[vmem, hbm, hbm],
        out_specs=[vmem, vmem],
        out_shape=[pltpu.VMEM((high, LANES), f32), pltpu.VMEM((COPY, rank), bf16)],
        scratch_shapes=[pltpu.VMEM((high, LANES), f32), pltpu.SemaphoreType.DMA((2,))],
        compiler_params=params,
        cost_estimate=pl.CostEstimate(flops=0, bytes_accessed=4 * COPY * rank, transcendentals=samples),
        name="prepare",
    )(chips1[1], far(scores), far(basis_rows))

    first, coef2 = pl.pallas_call(
        functools.partial(both_kernel, per_dev),
        in_specs=[vmem] * 8 + [hbm],
        out_specs=[vmem, vmem],
        out_shape=[pltpu.VMEM((high, LANES), f32), coef_shape],
        scratch_shapes=[
            pltpu.VMEM((ROWS, rank), f32),
            pltpu.VMEM((ROWS, rank), f32),
            pltpu.VMEM((ROWS, TILE), f32),
            pltpu.VMEM((ROWS, TILE), f32),
            pltpu.VMEM((ROWS, TILE), bf16),
            pltpu.VMEM((ROWS, TILE), bf16),
            pltpu.VMEM((SLOTS, COPY, rank), bf16),
            pltpu.SemaphoreType.DMA((SLOTS,)),
        ],
        compiler_params=params,
        name="first_and_coef_pass",
    )(close(cl_v), *chips1, close(assign_v), close(slope_v), close(head_v), close(turned_v), far(basis_rows))

    out = pl.pallas_call(
        functools.partial(last_kernel, per_dev),
        in_specs=[vmem] * 7,
        out_specs=vmem,
        out_shape=jax.ShapeDtypeStruct((high, LANES), f32),
        scratch_shapes=[
            pltpu.VMEM((ROWS, rank), f32),
        ],
        compiler_params=params,
        name="last_pass",
    )(close(cl_v), *to_chips(mix(coef2)), close(assign_v), close(first), close(turned_v))
    return out.reshape(samples)


def solution(mesh):
    in_specs = (
        P(("groups", "dev"), None),
        P(("groups", "dev")),
        P(("groups", "dev")),
        P(("groups", "dev")),
        P("groups"),
        P(("groups", "dev"), None),
        P(("groups", "dev"), None, None, None),
    )
    out_specs = P(("groups", "dev"))
    return jax.shard_map(shards, mesh=mesh, in_specs=in_specs, out_specs=out_specs, check_vma=False)
```

```python
import functools
import math

import jax
import jax.numpy as jnp
from jax import lax
from jax.experimental import pallas as pl
from jax.experimental.pallas import tpu as pltpu
from jax.sharding import PartitionSpec as P

REACH = 2
NEAR = 2 * REACH + 1
CL_DEV = 4
S_DEV = 65536
LANES = 128
ROWS = 24

COPY = 8192
TILE = 4096
PER_COPY = COPY // TILE
SLOTS = 4
BODY = 8
PIECE = 1024
GROUP = 8

ridge = 0.5


def near_clusters(devices, per_dev, slot_of_ref, cl_ref):
    clusters = devices * per_dev
    me = lax.axis_index("dev")
    near = lax.broadcasted_iota(jnp.int32, (ROWS, clusters), 0)
    slots = (me + devices - REACH) * per_dev + near
    slots = lax.rem(slots, clusters)
    number = lax.broadcasted_iota(jnp.int32, (ROWS, clusters), 1)
    hit = (slot_of_ref[...] == slots) & (near < NEAR * per_dev)
    found = jnp.sum(jnp.where(hit, number + 1, 0), axis=1, keepdims=True) - 1
    cl_ref[...] = jnp.broadcast_to(found, cl_ref.shape)


def near_rows(per_dev, chips, rows_ref):
    even_core = lax.rem(lax.axis_index("dev"), 2) == 0
    chips = [chip[...].astype(jnp.float32) for chip in chips]
    rows_ref[...] = jnp.zeros_like(rows_ref)
    for g in range(NEAR):
        if g % 2 == 0:
            rows = chips[g // 2][:per_dev, :]
        else:
            rows = jnp.where(even_core, chips[g // 2][per_dev:, :], chips[g // 2 + 1][per_dev:, :])
        rows_ref[g * per_dev : (g + 1) * per_dev, :] = rows


def put_sums(per_dev, sum_ref, out_ref):
    for g in range(NEAR):
        out_ref[:, g * LANES : (g + 1) * LANES] = sum_ref[g * per_dev : (g + 1) * per_dev, :].astype(jnp.bfloat16)


def slot_copy(basis_hbm, slots_ref, sem, c):
    slot = lax.rem(c, SLOTS)
    rows = pl.ds(pl.multiple_of(c * COPY, COPY), COPY)
    return pltpu.make_async_copy(basis_hbm.at[rows, :], slots_ref.at[slot], sem.at[slot])


def tile_at(t):
    return pl.ds(pl.multiple_of(t * TILE, TILE), TILE)


def row_at(t, i):
    return pl.ds(t * (TILE // LANES) + i, 1)


def coef_kernel(
    devices, per_dev, slot_of_hbm, assign_hbm, vector_hbm, basis_hbm, links_hbm,
    out_ref, turned_ref, assign_ref, cl_ref, links_ref,
    slot_of_ref, sum_ref, vector_ref, x_ref, slots_ref, small_sem, basis_sem, links_sem,
):
    copies = basis_hbm.shape[0] // COPY

    def basis_copy(c):
        return slot_copy(basis_hbm, slots_ref, basis_sem, c)

    links_from = copies - per_dev - 1

    def links_copy(j):
        return pltpu.make_async_copy(links_hbm.at[j], links_ref.at[j], links_sem.at[j])

    slot_of_copy = pltpu.make_async_copy(slot_of_hbm, slot_of_ref, small_sem.at[2])
    assign_copy = pltpu.make_async_copy(assign_hbm, assign_ref, small_sem.at[0])
    vector_copy = pltpu.make_async_copy(vector_hbm, vector_ref, small_sem.at[1])
    slot_of_copy.start()
    assign_copy.start()
    vector_copy.start()
    for c in range(SLOTS):
        basis_copy(c).start()
    slot_of_copy.wait()
    near_clusters(devices, per_dev, slot_of_ref, cl_ref)
    sum_ref[...] = jnp.zeros_like(sum_ref)
    assign_copy.wait()
    vector_copy.wait()
    x_ref[...] = vector_ref[...].astype(jnp.float32)
    cl = cl_ref[...]

    @pl.loop(0, copies)
    def _(c):
        basis_copy(c).wait()

        @pl.when((c >= links_from) & (c < links_from + per_dev))
        def _():
            links_copy(c - links_from).start()

        total = sum_ref[...]
        for p in range(PER_COPY):
            t = c * PER_COPY + p
            parts = []
            for i in range(TILE // LANES):
                hit = assign_ref[row_at(t, i), :] == cl
                parts.append(jnp.where(hit, x_ref[row_at(t, i), :], 0.0).astype(jnp.bfloat16))
            left = jnp.concatenate(parts, axis=1)
            block = slots_ref[lax.rem(c, SLOTS), p * TILE : (p + 1) * TILE, :]
            turned_ref[:, tile_at(t)] = block.T
            total += jnp.dot(left, block, preferred_element_type=jnp.float32)
        sum_ref[...] = total

        @pl.when(c + SLOTS < copies)
        def _():
            basis_copy(c + SLOTS).start()

    put_sums(per_dev, sum_ref, out_ref)
    for j in range(per_dev):
        links_copy(j).wait()


def link_kernel(
    norm, devices, per_dev, slot_of_ref, partners_ref, parts_ref, links_ref, out_ref, scaled_ref, picked_ref, mixed_ref
):
    n_links, rank = links_ref.shape[1:3]
    step = 2 * GROUP
    for owner in range(devices):
        coef = parts_ref[(owner + REACH) % devices, :, :LANES].astype(jnp.float32)
        for g in range(1, NEAR):
            coef += parts_ref[(owner + REACH - g) % devices, :, g * LANES : (g + 1) * LANES].astype(jnp.float32)
        scaled_ref[owner * per_dev : (owner + 1) * per_dev, :] = (coef * norm).astype(jnp.bfloat16).astype(jnp.float32)

    def partner(j, k):
        return scaled_ref[pl.ds(slot_of_ref[partners_ref[j, k]], 1), :]

    row = lax.broadcasted_iota(jnp.int32, (GROUP, rank), 0)
    mixed_ref[...] = jnp.zeros_like(mixed_ref)
    for j in range(per_dev):
        acc = jnp.zeros((rank, rank), jnp.float32)
        few = jnp.zeros((GROUP, rank), jnp.float32)
        for k in range(0, n_links, step):
            at = (j * n_links + k) // 2
            for u in range(GROUP):
                picked_ref[at + u : at + u + 1, :] = partner(j, k + GROUP + u)
            blocks = links_ref[j, k + GROUP : k + step].reshape(GROUP * rank, rank)
            picked = picked_ref[at : at + GROUP, :].astype(jnp.bfloat16)
            products = lax.dot_general(picked, blocks, (((1,), (1,)), ((), ())), preferred_element_type=jnp.float32)
            for u in range(GROUP):
                acc += links_ref[j, k + u].astype(jnp.float32) * partner(j, k + u)
            for u in range(GROUP):
                few += jnp.where(row == u, products[:, u * rank : (u + 1) * rank], 0.0)
        mixed_ref[j : j + 1, :] = jnp.sum(acc.T, axis=0, keepdims=True) + jnp.sum(few, axis=0, keepdims=True)
    out_ref[...] = mixed_ref[:per_dev, :].astype(jnp.bfloat16)


def own_product(hit, products):
    return jnp.sum(jnp.where(hit, products, 0.0), axis=0, keepdims=True)


def prepare_kernel(after_ref, scores_hbm, basis_hbm, slope_ref, head_ref, scores_ref, sems):
    scores_copy = pltpu.make_async_copy(scores_hbm, scores_ref, sems.at[0])
    head_copy = pltpu.make_async_copy(basis_hbm.at[pl.ds(0, COPY), :], head_ref, sems.at[1])
    scores_copy.start()
    head_copy.start()
    scores_copy.wait()
    sig = jax.nn.sigmoid(scores_ref[...])
    slope_ref[...] = sig * (1.0 - sig)
    head_copy.wait()


def both_kernel(
    per_dev, cl_ref, behind_ref, own_ref, ahead_ref, assign_ref, slope_ref, head_ref, turned_ref, basis_hbm,
    first_ref, out_ref, rows_ref, sum_ref, even_ref, odd_ref, even_left, odd_left, slots_ref, basis_sem,
):
    tiles = turned_ref.shape[1] // TILE
    copies = tiles // PER_COPY

    def basis_copy(c):
        return slot_copy(basis_hbm, slots_ref, basis_sem, c)

    for c in range(1, SLOTS + 1):
        basis_copy(c).start()
    near_rows(per_dev, (behind_ref, own_ref, ahead_ref), rows_ref)
    sum_ref[...] = jnp.zeros_like(sum_ref)
    cl = cl_ref[...]
    rows = rows_ref[...].astype(jnp.bfloat16)
    products_of = (even_ref, odd_ref)
    left_of = (even_left, odd_left)

    def multiply(t, side):
        products_of[side][...] = jnp.dot(rows, turned_ref[:, tile_at(t)], preferred_element_type=jnp.float32)

    def select(t, side):
        for i in range(TILE // LANES):
            at = slice(i * LANES, (i + 1) * LANES)
            hit = assign_ref[row_at(t, i), :] == cl
            first = own_product(hit, products_of[side][:, at])
            first_ref[row_at(t, i), :] = first
            weighted = slope_ref[row_at(t, i), :] * first
            left_of[side][:, at] = jnp.where(hit, weighted, 0.0).astype(jnp.bfloat16)

    def add_up(c, p):
        at = slice(p * TILE, (p + 1) * TILE)
        block = head_ref[at, :] if isinstance(c, int) and c == 0 else slots_ref[lax.rem(c, SLOTS), at, :]
        sum_ref[...] += jnp.dot(left_of[p % 2][...], block, preferred_element_type=jnp.float32)

    def body(c):
        for p in range(PER_COPY):
            t = c * PER_COPY + p
            add_up(c, p)
            multiply(t + 2, p % 2)
            select(t + 1, (p + 1) % 2)

    multiply(0, 0)
    select(0, 0)
    multiply(1, 1)
    body(0)

    @pl.loop(1, copies - 1)
    def _(c):
        basis_copy(c).wait()
        body(c)

        @pl.when(c + SLOTS < copies)
        def _():
            basis_copy(c + SLOTS).start()

    basis_copy(copies - 1).wait()
    for p in range(PER_COPY):
        t = (copies - 1) * PER_COPY + p
        add_up(copies - 1, p)
        if p + 2 < PER_COPY:
            multiply(t + 2, p % 2)
        if p + 1 < PER_COPY:
            select(t + 1, (p + 1) % 2)
    put_sums(per_dev, sum_ref, out_ref)


def last_kernel(
    per_dev, cl_ref, behind_ref, own_ref, ahead_ref, assign_ref, first_ref, turned_ref, out_ref, rows_ref
):
    near_rows(per_dev, (behind_ref, own_ref, ahead_ref), rows_ref)
    cl = cl_ref[...]
    rows = rows_ref[...].astype(jnp.bfloat16)

    @pl.loop(0, turned_ref.shape[1] // (BODY * TILE))
    def _(c):
        for piece in range(BODY * TILE // PIECE):
            at = pl.ds(pl.multiple_of(c * (BODY * TILE) + piece * PIECE, PIECE), PIECE)
            products = jnp.dot(rows, turned_ref[:, at], preferred_element_type=jnp.float32)
            for k in range(PIECE // LANES):
                row = row_at(c * BODY, piece * (PIECE // LANES) + k)
                hit = assign_ref[row, :] == cl
                second = own_product(hit, products[:, k * LANES : (k + 1) * LANES])
                out_ref[row, :] = second + ridge * first_ref[row, :]


def shards(basis_rows, vector, scores, assign, slot_of, partners, link_blocks):
    devices = lax.axis_size("dev")
    clusters = slot_of.shape[0]
    per_dev, n_links, rank, _ = link_blocks.shape
    samples = assign.shape[0]
    norm = 1.0 / math.sqrt(S_DEV // CL_DEV)
    high = samples // LANES
    f32, bf16 = jnp.float32, jnp.bfloat16

    vector = vector.reshape(high, LANES)
    scores = scores.reshape(high, LANES)
    assign = assign.reshape(high, LANES)
    slot_row = slot_of.reshape(1, clusters)

    far = lambda x: pltpu.with_memory_space_constraint(x, pltpu.HBM)
    close = lambda x: pltpu.with_memory_space_constraint(x, pltpu.VMEM)
    vmem = pl.BlockSpec(memory_space=pltpu.VMEM)
    smem = pl.BlockSpec(memory_space=pltpu.SMEM)
    hbm = pl.BlockSpec(memory_space=pltpu.HBM)
    coef_shape = jax.ShapeDtypeStruct((per_dev, NEAR * rank), bf16)
    params = pltpu.CompilerParams(vmem_limit_bytes=12 * 1024 * 1024)

    coef1, turned_v, assign_v, cl_v, links_v = pl.pallas_call(
        functools.partial(coef_kernel, devices, per_dev),
        in_specs=[hbm] * 5,
        out_specs=[vmem] * 5,
        out_shape=[
            coef_shape,
            pltpu.VMEM((rank, samples), bf16),
            pltpu.VMEM((high, LANES), jnp.int32),
            pltpu.VMEM((ROWS, LANES), jnp.int32),
            pltpu.VMEM(link_blocks.shape, bf16),
        ],
        scratch_shapes=[
            pltpu.VMEM((1, clusters), jnp.int32),
            pltpu.VMEM((ROWS, rank), f32),
            pltpu.VMEM((high, LANES), bf16),
            pltpu.VMEM((high, LANES), f32),
            pltpu.VMEM((SLOTS, COPY, rank), bf16),
            pltpu.SemaphoreType.DMA((3,)),
            pltpu.SemaphoreType.DMA((SLOTS,)),
            pltpu.SemaphoreType.DMA((per_dev,)),
        ],
        compiler_params=params,
        name="coef_pass",
    )(far(slot_row), far(assign), far(vector), far(basis_rows), far(link_blocks))

    def to_all(block):
        copies = jnp.broadcast_to(block[None], (devices,) + block.shape)
        return lax.all_to_all(copies, "dev", 0, 0, tiled=True)

    def permute(block, pairs):
        return lax.ppermute(block, "dev", pairs)

    def to_chips(mixed):
        sibling = permute(mixed, [(i ^ 1, i) for i in range(devices)])
        own = jnp.concatenate([mixed, sibling], axis=0)
        behind = permute(own, [((i - 2) % devices, i) for i in range(devices)])
        ahead = permute(own, [((i + 2) % devices, i) for i in range(devices)])
        return behind, own, ahead

    def mix(coef):
        return pl.pallas_call(
            functools.partial(link_kernel, norm, devices, per_dev),
            in_specs=[smem, smem, vmem, vmem],
            out_specs=vmem,
            out_shape=jax.ShapeDtypeStruct((per_dev, rank), bf16),
            scratch_shapes=[
                pltpu.VMEM((clusters, rank), f32),
                pltpu.VMEM((per_dev * n_links // 2, rank), f32),
                pltpu.VMEM((8, rank), f32),
            ],
            compiler_params=params,
            name="link_product",
        )(slot_of, partners, to_all(coef), close(links_v))

    chips1 = to_chips(mix(coef1))
    slope_v, head_v = pl.pallas_call(
        prepare_kernel,
        in_specs=[vmem, hbm, hbm],
        out_specs=[vmem, vmem],
        out_shape=[pltpu.VMEM((high, LANES), f32), pltpu.VMEM((COPY, rank), bf16)],
        scratch_shapes=[pltpu.VMEM((high, LANES), f32), pltpu.SemaphoreType.DMA((2,))],
        compiler_params=params,
        cost_estimate=pl.CostEstimate(flops=0, bytes_accessed=4 * COPY * rank, transcendentals=samples),
        name="prepare",
    )(chips1[1], far(scores), far(basis_rows))

    first, coef2 = pl.pallas_call(
        functools.partial(both_kernel, per_dev),
        in_specs=[vmem] * 8 + [hbm],
        out_specs=[vmem, vmem],
        out_shape=[pltpu.VMEM((high, LANES), f32), coef_shape],
        scratch_shapes=[
            pltpu.VMEM((ROWS, rank), f32),
            pltpu.VMEM((ROWS, rank), f32),
            pltpu.VMEM((ROWS, TILE), f32),
            pltpu.VMEM((ROWS, TILE), f32),
            pltpu.VMEM((ROWS, TILE), bf16),
            pltpu.VMEM((ROWS, TILE), bf16),
            pltpu.VMEM((SLOTS, COPY, rank), bf16),
            pltpu.SemaphoreType.DMA((SLOTS,)),
        ],
        compiler_params=params,
        name="first_and_coef_pass",
    )(close(cl_v), *chips1, close(assign_v), close(slope_v), close(head_v), close(turned_v), far(basis_rows))

    out = pl.pallas_call(
        functools.partial(last_kernel, per_dev),
        in_specs=[vmem] * 7,
        out_specs=vmem,
        out_shape=jax.ShapeDtypeStruct((high, LANES), f32),
        scratch_shapes=[
            pltpu.VMEM((ROWS, rank), f32),
        ],
        compiler_params=params,
        name="last_pass",
    )(close(cl_v), *to_chips(mix(coef2)), close(assign_v), close(first), close(turned_v))
    return out.reshape(samples)


def solution(mesh):
    in_specs = (
        P(("groups", "dev"), None),
        P(("groups", "dev")),
        P(("groups", "dev")),
        P(("groups", "dev")),
        P("groups"),
        P(("groups", "dev"), None),
        P(("groups", "dev"), None, None, None),
    )
    out_specs = P(("groups", "dev"))
    return jax.shard_map(shards, mesh=mesh, in_specs=in_specs, out_specs=out_specs, check_vma=False)
```
